128 devices in a mesh: dp: 8 (over x_hi, z), tensor: 16 (over x_lo, y, core).
Axes of the slice: x: 4 (x_hi: 2, x_lo: 2; x = x_hi * 2 + x_lo), y: 4, z: 4, core: 2. Of those that a mesh axis runs over, the one named last changes fastest.
Arguments:
- history: bfloat16 [17, 16384, 2048], P(None, ('dp', 'tensor')), may hold values from -6 to 6
- cotangent: bfloat16 [16384, 2048], P(('dp', 'tensor')), may hold values from -6 to 6
- lengths: int32 [8, 4], replicated, may hold values from 0 to 2048, as said below
- mix_gain: float32 [2048], replicated, may hold values from 0.5 to 1.5
- mix_first: float32 [2048, 68], replicated, may hold values from -0.125 to 0.125
- mix_second: float32 [68, 68], replicated, may hold values from -0.3 to 0.3
- mix_bias: float32 [68], replicated, may hold values from -1.8 to 1.8
- gain_query: float32 [2048], replicated, may hold values from 0.5 to 1.5
- gain_key: float32 [2048], replicated, may hold values from 0.5 to 1.5
- gain_value: float32 [2048], replicated, may hold values from 0.5 to 1.5
- gain_mlp: float32 [2048], replicated, may hold values from 0.5 to 1.5
- w_query: bfloat16 [2048, 2048], P(None, 'tensor'), may hold values from -0.125 to 0.125
- w_key: bfloat16 [2048, 2048], P(None, 'tensor'), may hold values from -0.125 to 0.125
- w_value: bfloat16 [2048, 2048], P(None, 'tensor'), may hold values from -0.125 to 0.125
- w_output: bfloat16 [2048, 2048], P('tensor'), may hold values from -1 to 1
- w_expand: bfloat16 [2048, 8192], P(None, 'tensor'), may hold values from -0.125 to 0.125
- w_reduce: bfloat16 [8192, 2048], P('tensor'), may hold values from -0.0625 to 0.0625
Outputs:
- output: bfloat16 [16384, 2048], P(('dp', 'tensor'))
- grad_history: bfloat16 [17, 16384, 2048], P(None, ('dp', 'tensor'))
- grad_mix_gain: float32 [2048], replicated
- grad_mix_first: float32 [2048, 68], replicated
- grad_mix_second: float32 [68, 68], replicated
- grad_mix_bias: float32 [68], replicated
- grad_gain_query: float32 [2048], replicated
- grad_gain_key: float32 [2048], replicated
- grad_gain_value: float32 [2048], replicated
- grad_gain_mlp: float32 [2048], replicated
- grad_w_query: float32 [2048, 2048], P('dp', 'tensor')
- grad_w_key: float32 [2048, 2048], P('dp', 'tensor')
- grad_w_value: float32 [2048, 2048], P('dp', 'tensor')
- grad_w_output: float32 [2048, 2048], P('tensor', 'dp')
- grad_w_expand: float32 [2048, 8192], P('dp', 'tensor')
- grad_w_reduce: float32 [8192, 2048], P('tensor', 'dp')
The draws below stay inside these ranges and needn't reach their ends.
Inputs may be any that keep to these rules, and one draw needn't show every extreme that they name: Row g holds, in order, the lengths of the sequences packed into the 2048 tokens of data index g (0 marks an empty slot); each row sums to 2048, its longest entry is 1024 or more, and in some row one sequence fills all 2048 tokens.
All inputs are finite; a program needn't handle non-finite values.
Results may differ from the reference program's by a relative error of at most 0.019.
Values may be sent and summed in bfloat16 or wider, within the bound.
A program may use at most 320 MiB of HBM per device.

```python
import jax
import jax.numpy as jnp
from jax import lax

D = 2048
HEADS = 16
HEAD_DIM = 128
FF = 8192
HISTORY = 17
STREAMS = 4
MIX = 68
SEQS = 4
TOK_GRP = 2048
TOKENS = 16384
N_DP = 8


def draw_lengths(key, part):
    key_long, key_cut, key_whole, key_order = jax.random.split(key, 4)
    group_count = TOKENS // TOK_GRP
    half_tokens = TOK_GRP // 2
    longest = jax.random.randint(key_long, (group_count,), half_tokens, TOK_GRP + 1)
    whole_row = jax.random.randint(key_whole, (), 0, group_count)
    longest = jnp.where(jnp.arange(group_count) == whole_row, TOK_GRP, longest)
    remain = TOK_GRP - longest
    cut_points = jax.random.randint(key_cut, (group_count, SEQS - 2), 0, 1 << 20) % (remain[:, None] + 1)
    cut_points = jnp.sort(cut_points, axis=1)
    bounds = jnp.concatenate([jnp.zeros((group_count, 1), jnp.int32), cut_points.astype(jnp.int32), remain[:, None].astype(jnp.int32)], axis=1)
    others = bounds[:, 1:] - bounds[:, :-1]
    row_values = jnp.concatenate([longest[:, None].astype(jnp.int32), others], axis=1)
    rank_keys = jax.random.randint(key_order, (group_count, SEQS), 0, 1 << 20) * SEQS + jnp.arange(SEQS)
    column_order = jnp.argsort(rank_keys, axis=1, stable=True)
    return jnp.take_along_axis(row_values, column_order, axis=1).astype(jnp.int32)


def level_of(stream_key, shape, cuts, least, top_value):
    factor_of, own = 1.0, jax.random.fold_in(stream_key, 6)
    for position, blocks in cuts:
        steps = jnp.exp(jax.random.uniform(jax.random.fold_in(own, position), (blocks,), jnp.float32, least / len(cuts), top_value / len(cuts)))
        factor_of = factor_of * jnp.repeat(steps, shape[position] // blocks).reshape([-1 if axis == position else 1 for axis in range(len(shape))])
    return factor_of


def gaussian(rng, extent, scale, most, cuts=(), kind=jnp.bfloat16):
    loudness = level_of(rng, extent, cuts, -0.22, 0.18) if cuts else 1.0
    values = jax.random.normal(rng, extent, jnp.float32) * scale * loudness
    return jnp.minimum(jnp.maximum(values, -most), most).astype(kind)


def setup_inputs(seed: int = 0) -> dict:
    seeds = jax.random.split(jax.random.key(seed), 18)
    history = gaussian(seeds[0], (HISTORY, TOKENS, D), 1.0, 6.0, ((1, 128),))
    cotangent = gaussian(seeds[1], (TOKENS, D), 1.0, 6.0, ((0, 128),))
    lengths = draw_lengths(jax.random.fold_in(seeds[17], 71), 0)
    mix_gain = jnp.clip(1.0 + 0.1 * jax.random.normal(seeds[3], (D,), jnp.float32), 0.5, 1.5)
    mix_first = gaussian(seeds[4], (D, MIX), D ** -0.5, 0.125, (), jnp.float32)
    mix_second = gaussian(seeds[5], (MIX, MIX), 0.05, 0.3, (), jnp.float32)
    mix_bias = gaussian(seeds[6], (MIX,), 0.3, 1.8, (), jnp.float32)
    gain_query = jnp.clip(1.0 + 0.1 * jax.random.normal(seeds[7], (D,), jnp.float32), 0.5, 1.5)
    gain_key = jnp.clip(1.0 + 0.1 * jax.random.normal(seeds[8], (D,), jnp.float32), 0.5, 1.5)
    gain_value = jnp.clip(1.0 + 0.1 * jax.random.normal(seeds[9], (D,), jnp.float32), 0.5, 1.5)
    gain_mlp = jnp.clip(1.0 + 0.1 * jax.random.normal(seeds[10], (D,), jnp.float32), 0.5, 1.5)
    w_query = gaussian(seeds[11], (D, D), D ** -0.5, 0.125, ((1, 16),))
    w_key = gaussian(seeds[12], (D, D), D ** -0.5, 0.125, ((1, 16),))
    w_value = gaussian(seeds[13], (D, D), D ** -0.5, 0.125, ((1, 16),))
    w_output = gaussian(seeds[14], (D, D), (D // 64) ** -0.5, 1.0, ((0, 16),))
    w_expand = gaussian(seeds[15], (D, FF), D ** -0.5, 0.125, ((1, 16),))
    w_reduce = gaussian(seeds[16], (FF, D), FF ** -0.5, 0.0625, ((0, 16),))
    return {"history": history, "cotangent": cotangent, "lengths": lengths, "mix_gain": mix_gain, "mix_first": mix_first, "mix_second": mix_second, "mix_bias": mix_bias, "gain_query": gain_query, "gain_key": gain_key, "gain_value": gain_value, "gain_mlp": gain_mlp, "w_query": w_query, "w_key": w_key, "w_value": w_value, "w_output": w_output, "w_expand": w_expand, "w_reduce": w_reduce}


NORM_EPS = 1e-06
MASKED = -1e+30
PRECISE = lax.Precision.HIGHEST

@jax.custom_vjp
def low(v):
    return lax.optimization_barrier(v.astype(jnp.bfloat16)).astype(jnp.float32)

@jax.custom_vjp
def low_back(v):
    return v

def low_keep(v):
    return (low(v), None)

def low_pass(kept, grad):
    return (grad,)

def back_keep(v):
    return (v, None)

def back_low(kept, grad):
    return (low(grad),)
low.defvjp(low_keep, low_pass)
low_back.defvjp(back_keep, back_low)

def rms_scale(values, gain_vector):
    inverse = lax.rsqrt(lax.optimization_barrier(jnp.mean(values * values, axis=-1, keepdims=True)) + NORM_EPS)
    return values * inverse * gain_vector

def matmul(left_side, right_side):
    return jnp.dot(left_side, right_side, precision=PRECISE)

def front_part(history_float, mix_gain, mix_first, mix_second, mix_bias, gain_query, gain_key, gain_value):
    latest = rms_scale(history_float[HISTORY - 1], mix_gain)
    hidden = jax.nn.gelu(matmul(latest, mix_first), approximate=False)
    mixing = (matmul(hidden, mix_second) + mix_bias).reshape(history_float.shape[1], STREAMS, HISTORY)
    streams = jnp.einsum('tkj,jtd->ktd', mixing, history_float, precision=PRECISE)
    return (rms_scale(streams[0], gain_query), rms_scale(streams[1], gain_key), rms_scale(streams[2], gain_value), streams[3])

def attend(query_heads, key_heads, value_heads, segment):
    tok_count = query_heads.shape[0]
    block_rows = min(512, tok_count)
    blocks = tok_count // block_rows
    positions = jnp.arange(tok_count, dtype=jnp.int32)
    scale_factor = HEAD_DIM ** (-0.5)

    def one_block(pieces):
        query_block, position_block, segment_block = pieces
        scores = low_back(jnp.einsum('qhd,khd->hqk', query_block, key_heads, precision=PRECISE) * scale_factor)
        allowed = (position_block[:, None] >= positions[None, :]) & (segment_block[:, None] == segment[None, :])
        masked = jnp.where(allowed[None], scores, MASKED)
        top_score = lax.optimization_barrier(jnp.max(masked, axis=-1, keepdims=True))
        exponent = jnp.exp(masked - top_score)
        weights_low = low(exponent / lax.optimization_barrier(jnp.sum(exponent, axis=-1, keepdims=True)))
        return jnp.einsum('hqk,khd->qhd', weights_low, value_heads, precision=PRECISE)
    context = lax.map(jax.checkpoint(one_block), (query_heads.reshape(blocks, block_rows, HEADS, HEAD_DIM), positions.reshape(blocks, block_rows), segment.reshape(blocks, block_rows)))
    return low(low_back(context.reshape(tok_count, HEADS * HEAD_DIM)))

def layer(history_float, params, segment):
    mix_gain, mix_first, mix_second, mix_bias, gain_query, gain_key, gain_value, gain_mlp, w_query, w_key, w_value, w_output, w_expand, w_reduce = params
    query_norm, key_norm, value_norm, residual = front_part(history_float, mix_gain, mix_first, mix_second, mix_bias, gain_query, gain_key, gain_value)
    tok_count = residual.shape[0]
    queries = low(low_back(matmul(low(query_norm), w_query))).reshape(tok_count, HEADS, HEAD_DIM)
    key_heads = low(low_back(matmul(low(key_norm), w_key))).reshape(tok_count, HEADS, HEAD_DIM)
    value_heads = low(low_back(matmul(low(value_norm), w_value))).reshape(tok_count, HEADS, HEAD_DIM)
    context = attend(queries, key_heads, value_heads, segment)
    attended = low_back(matmul(context, w_output))
    middle = residual + attended
    mlp_input = low(rms_scale(middle, gain_mlp))
    expanded = low_back(matmul(mlp_input, w_expand))
    activated = low(jax.nn.gelu(expanded, approximate=False))
    return middle + matmul(activated, w_reduce)

def reference(history, cotangent, lengths, mix_gain, mix_first, mix_second, mix_bias, gain_query, gain_key, gain_value, gain_mlp, w_query, w_key, w_value, w_output, w_expand, w_reduce):
    weights = tuple((weight_arg.astype(jnp.float32) for weight_arg in (mix_gain, mix_first, mix_second, mix_bias, gain_query, gain_key, gain_value, gain_mlp, w_query, w_key, w_value, w_output, w_expand, w_reduce)))
    history_groups = jnp.moveaxis(history.reshape(HISTORY, N_DP, TOK_GRP, D), 1, 0)
    cot_groups = cotangent.reshape(N_DP, TOK_GRP, D)
    positions = jnp.arange(TOK_GRP, dtype=jnp.int32)

    def one_group(totals, pieces):
        history_group, cot_group, length_row = pieces
        doc_ends = jnp.cumsum(length_row).astype(jnp.int32)
        segment = lax.optimization_barrier(jnp.sum((positions[:, None] >= doc_ends[None, :]).astype(jnp.int32), axis=1)).astype(jnp.int32)

        def forward(history_float, params):
            return layer(history_float, params, segment)
        result, backward = jax.vjp(forward, history_group.astype(jnp.float32), weights)
        grad_hist, grad_params = backward(cot_group.astype(jnp.float32))
        totals = jax.tree.map(lambda left_side, right_side: left_side + right_side, totals, grad_params)
        return (totals, (result.astype(jnp.bfloat16), grad_hist.astype(jnp.bfloat16)))
    start_totals = jax.tree.map(jnp.zeros_like, weights)
    totals, (outputs, grads_history) = lax.scan(one_group, start_totals, (history_groups, cot_groups, lengths))
    output = outputs.reshape(TOKENS, D)
    grad_history = jnp.moveaxis(grads_history, 0, 1).reshape(HISTORY, TOKENS, D)
    return (output, grad_history, totals[0], totals[1], totals[2], totals[3], totals[4], totals[5], totals[6], totals[7], totals[8], totals[9], totals[10], totals[11], totals[12], totals[13])
```

```python
import functools

import jax
import jax.numpy as jnp
from jax import lax
from jax.experimental import pallas as pl
from jax.experimental.pallas import tpu as pltpu
from jax.sharding import PartitionSpec as P

HEAD_DIM = 128
HISTORY = 17
STREAMS = 4
MIX = HISTORY * STREAMS
D = 2048
ROWS = 128
FF_SHARD = 512
NORM_EPS = 1e-06
MASKED = -1e30
PRECISE = lax.Precision.HIGHEST
MESH = pl.DeviceIdType.MESH
BF = jnp.bfloat16
F32 = jnp.float32
VMEM = pltpu.VMEM
ANY = pl.ANY
MIB = 2**20

Y1, Y2, Y3 = 2, 4, 6
SIB, XN, DIAG = 1, 8, 9
A_MASKS = (0, SIB, XN, DIAG)
LO, HI = pl.ds(0, 64), pl.ds(64, 64)


def flip(value, mask):
    for bit in (1, 2, 4, 8):
        if mask & bit:
            value = value + bit - 2 * bit * lax.rem(lax.div(value, bit), 2)
    return value


def dev(t_mask, dp_mask=0):
    return (flip(lax.axis_index("dp"), dp_mask), flip(lax.axis_index("tensor"), t_mask))


def enter(partners):
    barrier = pltpu.get_barrier_semaphore()
    for partner in partners:
        pl.semaphore_signal(barrier, inc=1, device_id=dev(*partner), device_id_type=MESH)
    pl.semaphore_wait(barrier, len(partners))


def rcopy(src, dst, send, recv, target):
    return pltpu.make_async_remote_copy(
        src_ref=src, dst_ref=dst, send_sem=send, recv_sem=recv, device_id=dev(*target), device_id_type=MESH
    )


def nt(a, b):
    return lax.dot_general(a, b, (((1,), (1,)), ((), ())), preferred_element_type=F32)


def tn(a, b):
    return lax.dot_general(a, b, (((0,), (0,)), ((), ())), preferred_element_type=F32)


def nn(a, b):
    return jnp.dot(a, b, preferred_element_type=F32)


class Gather:
    def __init__(self, own, rows, send, recv):
        def c(i, src, dst, target):
            return rcopy(src, dst, send.at[i], recv.at[i], (target,))

        self.copies = [
            c(0, own.at[LO], rows.at[1, LO], Y1),
            c(1, own.at[HI], rows.at[3, HI], Y3),
            c(2, own.at[HI], rows.at[1, HI], Y1),
            c(3, own.at[LO], rows.at[3, LO], Y3),
            c(4, rows.at[1, LO], rows.at[2, LO], Y3),
            c(5, rows.at[3, HI], rows.at[2, HI], Y1),
        ]

    def start(self):
        for i in range(4):
            self.copies[i].start()

    def forward(self):
        self.copies[0].wait_recv()
        self.copies[4].start()
        self.copies[1].wait_recv()
        self.copies[5].start()

    def arrived(self, slot):
        for i in {1: (2,), 3: (3,), 2: (4, 5)}[slot]:
            self.copies[i].wait_recv()

    def finish(self):
        for c in self.copies:
            c.wait_send()


class Scatter:
    def __init__(self, out, passed, got, send, recv):
        def c(i, src, dst, target):
            return rcopy(src, dst, send.at[i], recv.at[i], (target,))

        self.out, self.passed, self.got = out, passed, got
        self.copies = [
            c(0, out.at[0, LO], passed.at[LO], Y1),
            c(1, out.at[0, HI], passed.at[HI], Y3),
            c(2, out.at[1, LO], got.at[0, LO], Y1),
            c(3, out.at[2, HI], got.at[1, HI], Y3),
            c(4, out.at[2, LO], got.at[1, LO], Y3),
            c(5, out.at[1, HI], got.at[0, HI], Y1),
        ]

    def opposite(self, part):
        self.out[0] = part.astype(BF)
        self.copies[0].start()
        self.copies[1].start()

    def first(self, part):
        self.out[1, LO] = part[0:64].astype(BF)
        self.copies[2].start()

    def second(self, part):
        self.out[2, HI] = part[64:128].astype(BF)
        self.copies[3].start()

    def relay(self, first_ref, second_ref):
        self.copies[0].wait_recv()
        self.out[2, LO] = (second_ref[LO] + self.passed[LO].astype(F32)).astype(BF)
        self.copies[4].start()
        self.copies[1].wait_recv()
        self.out[1, HI] = (first_ref[HI] + self.passed[HI].astype(F32)).astype(BF)
        self.copies[5].start()

    def total(self):
        for i in (2, 3, 4, 5):
            self.copies[i].wait_recv()
        return self.got[0].astype(F32) + self.got[1].astype(F32)

    def finish(self):
        for c in self.copies:
            c.wait_send()


def gelu_parts(x):
    cdf = 0.5 * (1.0 + lax.erf(x * (0.5**0.5)))
    return x * cdf, cdf + x * jnp.exp(-0.5 * x * x) * 0.3989422804014327


def front_kernel(
    hist, latest, mix_gain, mix_first, mix_second, mix_bias, gains, x_out, n_out, inv_out, resid_out, mix_out, pre_out, mix
):
    @pl.when(pl.program_id(0) == 0)
    def _():
        last = latest[0].astype(F32)
        inverse = lax.rsqrt(jnp.mean(last * last, axis=-1, keepdims=True) + NORM_EPS)
        pre = jnp.dot(last * inverse * mix_gain[...], mix_first[...], precision=PRECISE, preferred_element_type=F32)
        pre_out[...] = pre
        hidden = gelu_parts(pre)[0]
        mixing = jnp.dot(hidden, mix_second[...], precision=PRECISE, preferred_element_type=F32) + mix_bias[...]
        mix[...] = mixing
        mix_out[...] = mixing

    rows = hist.shape[1]
    here = mix[pl.ds(pl.multiple_of(pl.program_id(0) * rows, rows), rows), :]
    spread = [jnp.broadcast_to(here[:, i : i + 1], (rows, 128)) for i in range(MIX)]
    squares = [jnp.zeros((rows, 128), F32) for _ in range(3)]
    sums = []
    width = 256
    for c in range(D // width):
        tiles = [[None] * (width // 128) for _ in range(STREAMS)]
        for j in range(HISTORY):
            h = hist[j, :, c * width : (c + 1) * width].astype(F32)
            for lane in range(width // 128):
                piece = h[:, lane * 128 : (lane + 1) * 128]
                for k in range(STREAMS):
                    term = spread[k * HISTORY + j] * piece
                    tiles[k][lane] = term if j == 0 else tiles[k][lane] + term
        for lane in range(width // 128):
            at = slice(c * width + lane * 128, c * width + (lane + 1) * 128)
            resid_out[:, at] = tiles[3][lane]
            for k in range(3):
                squares[k] = squares[k] + tiles[k][lane] * tiles[k][lane]
        sums.append(tiles)
    for k in range(3):
        inverse = lax.rsqrt(jnp.sum(squares[k], axis=-1, keepdims=True) * (1.0 / D) + NORM_EPS)
        inv_out[k] = jnp.broadcast_to(inverse, (rows, 128))
        for c in range(D // width):
            for lane in range(width // 128):
                at = slice(c * width + lane * 128, c * width + (lane + 1) * 128)
                normal = sums[c][k][lane] * inverse
                n_out[k, :, at] = normal.astype(BF)
                x_out[k, :, at] = (normal * gains[k : k + 1, at]).astype(BF)


def front(history, mix_gain, mix_first, mix_second, mix_bias, gains):
    rows = 16
    return pl.pallas_call(
        front_kernel,
        grid=(ROWS // rows,),
        in_specs=[
            pl.BlockSpec((HISTORY, rows, D), lambda i: (0, i, 0)),
            pl.BlockSpec((1, ROWS, D), lambda i: (HISTORY - 1, 0, 0)),
            pl.BlockSpec((1, D), lambda i: (0, 0)),
            pl.BlockSpec((D, MIX), lambda i: (0, 0)),
            pl.BlockSpec((MIX, MIX), lambda i: (0, 0)),
            pl.BlockSpec((1, MIX), lambda i: (0, 0)),
            pl.BlockSpec((3, D), lambda i: (0, 0)),
        ],
        out_specs=[
            pl.BlockSpec((3, rows, D), lambda i: (0, i, 0)),
            pl.BlockSpec((3, rows, D), lambda i: (0, i, 0)),
            pl.BlockSpec((3, rows, 128), lambda i: (0, i, 0)),
            pl.BlockSpec((rows, D), lambda i: (i, 0)),
            pl.BlockSpec((ROWS, MIX), lambda i: (0, 0)),
            pl.BlockSpec((ROWS, MIX), lambda i: (0, 0)),
        ],
        out_shape=[
            jax.ShapeDtypeStruct((3, ROWS, D), BF),
            jax.ShapeDtypeStruct((3, ROWS, D), BF),
            jax.ShapeDtypeStruct((3, ROWS, 128), F32),
            jax.ShapeDtypeStruct((ROWS, D), F32),
            jax.ShapeDtypeStruct((ROWS, MIX), F32),
            jax.ShapeDtypeStruct((ROWS, MIX), F32),
        ],
        scratch_shapes=[VMEM((ROWS, MIX), F32)],
        compiler_params=pltpu.CompilerParams(vmem_limit_bytes=48 * MIB),
        name="front",
    )(history, history, mix_gain[None], mix_first, mix_second, mix_bias[None], gains)


def qkv_kernel(
    x, w_query, w_key, w_value, w_output, w_expand,
    heads, rows_out, w_out, wo_all, we_two,
    rows, weights, proj, g_send, g_recv, w_send, w_recv, f_send, f_recv, h_send, h_recv, local,
):
    enter([(Y1,), (Y3,), (SIB,), (XN,), (XN, 4), (DIAG,)])
    t = lax.axis_index("tensor")
    sources = [w_query, w_key, w_value, w_output, w_expand]
    slots = [lambda r, i=i: weights.at[i, r] for i in range(3)]
    slots += [lambda r: wo_all.at[r], lambda r: we_two.at[r - 1]]
    to_sib, to_x, onward = [], [], []
    for i, src in enumerate(sources):
        half = src.shape[0] // 2
        lo, hi = pl.ds(0, half), pl.ds(half, half)
        to_x.append(
            (
                rcopy(src.at[lo], slots[i](2).at[lo], w_send.at[i, 0], w_recv.at[i, 0], (XN,)),
                rcopy(src.at[hi], slots[i](2).at[hi], w_send.at[i, 1], w_recv.at[i, 1], (XN, 4)),
            )
        )
        to_sib.append(rcopy(src, slots[i](1), w_send.at[i, 2], w_recv.at[i, 2], (SIB,)))
        if i < 4:
            onward.append(rcopy(slots[i](2), slots[i](3), f_send.at[i], f_recv.at[i], (SIB,)))
    keep = [pltpu.make_async_copy(sources[i], slots[i](0), local.at[i]) for i in range(4)]
    gathers = [Gather(x.at[a], rows.at[a], g_send.at[a], g_recv.at[a]) for a in range(3)]
    for a in range(3):
        to_x[a][0].start()
        to_x[a][1].start()
        gathers[a].start()
        to_sib[a].start()
        keep[a].start()
    for i in (3, 4):
        to_x[i][0].start()
        to_x[i][1].start()
        to_sib[i].start()
    keep[3].start()
    for a in range(3):
        for c in to_x[a]:
            c.wait_recv()
        onward[a].start()
        gathers[a].forward()
    sends = []

    def project(a, s):
        block = x[a] if s == 0 else rows[a, s]
        for p in range(2):
            pair = jnp.concatenate([weights[a, 2 * p], weights[a, 2 * p + 1]], axis=1)
            y = nn(block, pair).astype(BF)
            proj[a, s, 2 * p] = y[:, :128]
            proj[a, s, 2 * p + 1] = y[:, 128:]
        place = flip(t, 2 * s)
        for r in range(4):
            src, dst = proj.at[a, s, r], heads.at[a, place]
            if r == 0:
                c = pltpu.make_async_copy(src, dst, h_send.at[a, s, 0])
            else:
                c = rcopy(src, dst, h_send.at[a, s, r], h_recv.at[a, s, r], (A_MASKS[r],))
            c.start()
            sends.append((r, c))

    for a in range(3):
        keep[a].wait()
        to_sib[a].wait_recv()
        onward[a].wait_recv()
        project(a, 0)
    store = []
    for a in range(3):
        c = pltpu.make_async_copy(weights.at[a], w_out.at[a], local.at[4 + a])
        c.start()
        store.append(c)
        c = pltpu.make_async_copy(x.at[a], rows_out.at[a, 0], local.at[7 + a])
        c.start()
        store.append(c)
    for a in range(3):
        for s in (1, 3):
            gathers[a].arrived(s)
            project(a, s)
    for c in to_x[3]:
        c.wait_recv()
    onward[3].start()
    for a in range(3):
        gathers[a].arrived(2)
        project(a, 2)
        c = pltpu.make_async_copy(rows.at[a, pl.ds(1, 3)], rows_out.at[a, pl.ds(1, 3)], local.at[10 + a])
        c.start()
        store.append(c)
    for g in gathers:
        g.finish()
    for r, c in sends:
        if r == 0:
            c.wait()
        else:
            c.wait_send()
    for r, c in sends:
        if r:
            c.wait_recv()
    for i in range(5):
        for c in to_x[i]:
            c.wait_send()
            if i > 3:
                c.wait_recv()
        to_sib[i].wait_send()
        if i > 2:
            to_sib[i].wait_recv()
    for i in range(4):
        onward[i].wait_send()
    onward[3].wait_recv()
    keep[3].wait()
    for c in store:
        c.wait()


def qkv(x, w_query, w_key, w_value, w_output, w_expand):
    dma = pltpu.SemaphoreType.DMA
    return pl.pallas_call(
        qkv_kernel,
        in_specs=[pl.BlockSpec(memory_space=VMEM)] + [pl.BlockSpec(memory_space=ANY)] * 5,
        out_specs=[pl.BlockSpec(memory_space=ANY)] * 5,
        out_shape=[
            jax.ShapeDtypeStruct((3, 16, ROWS, HEAD_DIM), BF),
            jax.ShapeDtypeStruct((3, 4, ROWS, D), BF),
            jax.ShapeDtypeStruct((3, 4, D, HEAD_DIM), BF),
            jax.ShapeDtypeStruct((4, HEAD_DIM, D), BF),
            jax.ShapeDtypeStruct((2, D, FF_SHARD), BF),
        ],
        scratch_shapes=[
            VMEM((3, 4, ROWS, D), BF),
            VMEM((3, 4, D, HEAD_DIM), BF),
            VMEM((3, 4, 4, ROWS, HEAD_DIM), BF),
            dma((3, 6)), dma((3, 6)), dma((5, 3)), dma((5, 3)), dma((4,)), dma((4,)), dma((3, 4, 4)), dma((3, 4, 4)), dma((13,)),
        ],
        compiler_params=pltpu.CompilerParams(collective_id=1, has_side_effects=True, vmem_limit_bytes=48 * MIB),
        cost_estimate=pl.CostEstimate(flops=6 * 512 * 2048 * 512, bytes_accessed=30 * MIB, transcendentals=0),
        name="qkv",
    )(x, w_query, w_key, w_value, w_output, w_expand)


def attend_kernel(q, k, v, first, ctx):
    tokens, step = q.shape[0], 256
    scale = HEAD_DIM ** (-0.5)
    for i in range(tokens // step):
        length = (i + 1) * step
        at = slice(i * step, length)
        scores = nt(q[at], k[:length]) * scale
        key_place = lax.broadcasted_iota(jnp.int32, (step, length), 1)
        query_place = lax.broadcasted_iota(jnp.int32, (step, 1), 0) + i * step
        allowed = (key_place >= first[at]) & (key_place <= query_place)
        scores = jnp.where(allowed, scores, MASKED)
        top = jnp.max(scores, axis=-1, keepdims=True)
        e = jnp.exp(scores - top)
        low = (e * (1.0 / jnp.sum(e, axis=-1, keepdims=True))).astype(BF)
        ctx[at] = nn(low, v[:length]).astype(BF)


def attend(q, k, v, first_column):
    full = pl.BlockSpec(memory_space=VMEM)
    return pl.pallas_call(
        attend_kernel,
        in_specs=[full] * 4,
        out_specs=full,
        out_shape=jax.ShapeDtypeStruct(q.shape, BF),
        compiler_params=pltpu.CompilerParams(vmem_limit_bytes=48 * MIB),
        cost_estimate=pl.CostEstimate(flops=4 * 2048 * 1024 * 128, bytes_accessed=4 * MIB, transcendentals=2048 * 1024),
        name="attend",
    )(q, k, v, first_column)


def attend_back_kernel(q, k, v, gc, first, dq, dk, dv, dk_sum, dv_sum):
    tokens, step = q.shape[0], 256
    scale = HEAD_DIM ** (-0.5)
    k_turned = k[...].astype(F32).T.astype(BF)
    for i in range(tokens // step):
        length = (i + 1) * step
        at = slice(i * step, length)
        scores = nt(k[:length], q[at]) * scale
        key_place = lax.broadcasted_iota(jnp.int32, (length, step), 0)
        query_place = lax.broadcasted_iota(jnp.int32, (1, step), 1) + i * step
        allowed = (key_place >= first[:, at]) & (key_place <= query_place)
        scores = jnp.where(allowed, scores, MASKED)
        top = jnp.max(scores, axis=0, keepdims=True)
        e = jnp.exp(scores - top)
        probs = e * (1.0 / jnp.sum(e, axis=0, keepdims=True))
        grad_probs = nt(v[:length], gc[at])
        delta = jnp.sum(grad_probs * probs, axis=0, keepdims=True)
        grad_scores = (probs * (grad_probs - delta)).astype(BF)
        low = probs.astype(BF)
        dq[at] = (nn(k_turned[:, :length], grad_scores) * scale).T.astype(BF)
        key_part = nn(grad_scores, q[at])
        value_part = nn(low, gc[at])
        if i:
            dk_sum[: i * step] += key_part[: i * step]
            dv_sum[: i * step] += value_part[: i * step]
        dk_sum[at] = key_part[i * step :]
        dv_sum[at] = value_part[i * step :]
    dk[...] = (dk_sum[...] * scale).astype(BF)
    dv[...] = dv_sum[...].astype(BF)


def attend_back(q, k, v, grad_context, first_row):
    full = pl.BlockSpec(memory_space=VMEM)
    return pl.pallas_call(
        attend_back_kernel,
        in_specs=[full] * 5,
        out_specs=[full] * 3,
        out_shape=[jax.ShapeDtypeStruct(q.shape, BF)] * 3,
        scratch_shapes=[VMEM(q.shape, F32)] * 2,
        compiler_params=pltpu.CompilerParams(vmem_limit_bytes=48 * MIB),
        cost_estimate=pl.CostEstimate(flops=10 * 2048 * 1024 * 128, bytes_accessed=8 * MIB, transcendentals=2048 * 1024),
        name="attend_back",
    )(q, k, v, grad_context, first_row)


def moved(x, mask):
    return x if mask == 0 else lax.ppermute(x, "tensor", [(i, i ^ mask) for i in range(16)])


def y_gather_plain(x):
    return jnp.stack([moved(x, 2 * s) for s in range(4)])


def y_sum_plain(parts):
    return sum(moved(parts[s].astype(BF), 2 * s).astype(F32) if s else parts[0] for s in range(4))


def to_rows_plain(heads):
    t = lax.axis_index("tensor")
    out = []
    for r in range(4):
        piece = jnp.stack([heads[(t ^ A_MASKS[r]) ^ (2 * s)] for s in range(4)])
        out.append(moved(piece, A_MASKS[r]))
    return jnp.stack(out, 1)


def to_heads_plain(rows):
    t = lax.axis_index("tensor")
    out = jnp.zeros((16, 128, 128), rows.dtype)
    for r in range(4):
        got = moved(rows[:, r], A_MASKS[r])
        for s in range(4):
            out = out.at[(t ^ A_MASKS[r]) ^ (2 * s)].set(got[s])
    return out


def mlp_plain(ctx, wo_all, resid, gain_mlp, cot, w_expand, we_two, w_reduce):
    ctx_rows = to_rows_plain(ctx)
    we = jnp.stack([w_expand, we_two[0], we_two[1], moved(we_two[1], SIB)])
    wr = jnp.stack([moved(w_reduce, m) for m in A_MASKS])
    cot_rows = y_gather_plain(cot)
    attended = y_sum_plain(jnp.einsum("srtd,rdo->sto", ctx_rows, wo_all, preferred_element_type=F32))
    middle = resid + attended
    inverse = lax.rsqrt(jnp.mean(middle * middle, -1, keepdims=True) + NORM_EPS)
    normal = middle * inverse
    mlp_rows = y_gather_plain((normal * gain_mlp).astype(BF))
    expanded = jnp.einsum("std,rdf->srtf", mlp_rows, we, preferred_element_type=F32)
    act, slope = gelu_parts(expanded)
    act = act.astype(BF)
    reduced = jnp.einsum("srtf,rfd->std", act, wr, preferred_element_type=F32)
    grad_active = jnp.einsum("std,rfd->srtf", cot_rows, wr, preferred_element_type=F32)
    gexp = (grad_active * slope).astype(BF)
    grad_wr = jnp.einsum("srtf,std->rfd", act, cot_rows, preferred_element_type=F32).astype(BF)
    grad_we = jnp.einsum("std,srtf->rdf", mlp_rows, gexp, preferred_element_type=F32).astype(BF)
    gmlp = y_sum_plain(jnp.einsum("srtf,rdf->std", gexp, we, preferred_element_type=F32))
    grad_gain = jnp.sum(gmlp * normal, 0, keepdims=True)
    scaled = gmlp * gain_mlp
    grad_middle = cot.astype(F32) + inverse * (scaled - normal * jnp.mean(scaled * normal, -1, keepdims=True))
    return ctx_rows, middle, reduced, grad_we, grad_wr, grad_gain, grad_middle


def out_back_plain(grad_middle, middle, reduced, ctx_rows, wo_all):
    gmid_rows = y_gather_plain(grad_middle.astype(BF))
    output = (middle + y_sum_plain(reduced)).astype(BF)
    gctx = jnp.einsum("std,rhd->srth", gmid_rows, wo_all, preferred_element_type=F32).astype(BF)
    grad_wo = jnp.einsum("srth,std->rhd", ctx_rows, gmid_rows, preferred_element_type=F32).astype(BF)
    return output, to_heads_plain(gctx), grad_wo


def streams_back_plain(grads, rows, w_all):
    dw, gs = [], []
    for a in range(3):
        g = to_rows_plain(grads[a])
        dw.append(jnp.einsum("std,srth->rdh", rows[a], g, preferred_element_type=F32).astype(BF))
        gs.append(y_sum_plain(jnp.einsum("srth,rdh->std", g, w_all[a], preferred_element_type=F32)))
    return jnp.stack(gs), jnp.stack(dw)


def weight_sum_plain(dw, split):
    own = y = sum(moved(dw[r], A_MASKS[r]).astype(F32) for r in range(4))
    return lax.psum_scatter(own, "dp", scatter_dimension=split, tiled=True)


def front_back_plain(history, gs, grad_middle, n, inv, mix, pre, mix_gain, mix_first, mix_second, gains):
    grads_gain, ds = [], []
    for k in range(3):
        normal = n[k].astype(F32)
        grads_gain.append(jnp.sum(gs[k] * normal, 0))
        scaled = gs[k] * gains[k]
        ds.append(inv[k][:, :1] * (scaled - normal * jnp.mean(scaled * normal, -1, keepdims=True)))
    ds = jnp.stack(ds + [grad_middle])
    h = history.astype(F32)
    gmix = jnp.einsum("ktd,jtd->tkj", ds, h, precision=PRECISE).reshape(ROWS, MIX)
    hidden, slope = gelu_parts(pre)
    last = h[HISTORY - 1]
    inverse = lax.rsqrt(jnp.mean(last * last, -1, keepdims=True) + NORM_EPS)
    normal = last * inverse
    latest = normal * mix_gain
    g_bias = gmix.sum(0)
    g_second = jnp.dot(hidden.T, gmix, precision=PRECISE)
    dpre = jnp.dot(gmix, mix_second.T, precision=PRECISE) * slope
    g_first = jnp.dot(latest.T, dpre, precision=PRECISE)
    dl = jnp.dot(dpre, mix_first.T, precision=PRECISE)
    g_gain = jnp.sum(dl * normal, 0)
    scaled = dl * mix_gain
    extra = inverse * (scaled - normal * jnp.mean(scaled * normal, -1, keepdims=True))
    gh = jnp.einsum("tkj,ktd->jtd", mix.reshape(ROWS, STREAMS, HISTORY), ds, precision=PRECISE)
    gh = gh.at[HISTORY - 1].add(extra).astype(BF)
    return gh, g_gain, g_first, g_second, g_bias, grads_gain[0], grads_gain[1], grads_gain[2]


def on_device(
    history, cotangent, lengths, mix_gain, mix_first, mix_second, mix_bias,
    gain_query, gain_key, gain_value, gain_mlp, w_query, w_key, w_value, w_output, w_expand, w_reduce,
):
    gains = jnp.stack([gain_query, gain_key, gain_value])
    row = lax.dynamic_index_in_dim(lengths, lax.axis_index("dp"), 0, keepdims=False)
    places = jnp.arange(2048, dtype=jnp.int32)
    first = jnp.zeros_like(places)
    end = jnp.int32(0)
    for i in range(lengths.shape[1]):
        end = end + row[i]
        first = jnp.where(places >= end, end, first)
    x, n, inv, resid, mix, pre = front(history, mix_gain, mix_first, mix_second, mix_bias, gains)
    heads, rows, w_all, wo_all, we_two = qkv(x, w_query, w_key, w_value, w_output, w_expand)
    q, k, v = [heads[a].reshape(2048, HEAD_DIM) for a in range(3)]
    ctx = attend(q, k, v, first[:, None]).reshape(16, ROWS, HEAD_DIM)
    ctx_rows, middle, reduced, grad_we, grad_wr, g_gain_mlp, grad_middle = mlp_plain(
        ctx, wo_all, resid, gain_mlp, cotangent, w_expand, we_two, w_reduce)
    output, gctx, grad_wo = out_back_plain(grad_middle, middle, reduced, ctx_rows, wo_all)
    dq, dk, dv = attend_back(q, k, v, gctx.reshape(2048, HEAD_DIM), first[None])
    gs, dw = streams_back_plain([z.reshape(16, ROWS, HEAD_DIM) for z in (dq, dk, dv)], rows, w_all)
    small = front_back_plain(history, gs, grad_middle, n, inv, mix, pre, mix_gain, mix_first, mix_second, gains)
    summed = lax.psum(small[1:] + (g_gain_mlp[0],), ("dp", "tensor"))
    return (output, small[0], *summed,
        weight_sum_plain(dw[0], 0), weight_sum_plain(dw[1], 0), weight_sum_plain(dw[2], 0),
        weight_sum_plain(grad_wo, 1), weight_sum_plain(grad_we, 0), weight_sum_plain(grad_wr, 1))


def solution(mesh):
    rows, cols, both = P("tensor", None), P(None, "tensor"), ("dp", "tensor")
    return jax.shard_map(
        on_device,
        mesh=mesh,
        in_specs=(P(None, both, None), P(both, None)) + (P(),) * 9 + (cols, cols, cols, rows, cols, rows),
        out_specs=(P(both, None), P(None, both, None)) + (P(),) * 8
        + (P("dp", "tensor"),) * 3 + (P("tensor", "dp"), P("dp", "tensor"), P("tensor", "dp")),
        check_vma=False,
    )
```

```python
import functools

import jax
import jax.numpy as jnp
from jax import lax
from jax.experimental import pallas as pl
from jax.experimental.pallas import tpu as pltpu
from jax.sharding import PartitionSpec as P

HEAD_DIM = 128
HISTORY = 17
STREAMS = 4
MIX = HISTORY * STREAMS
D = 2048
ROWS = 128
FF_SHARD = 512
NORM_EPS = 1e-06
MASKED = -1e30
PRECISE = lax.Precision.HIGHEST
MESH = pl.DeviceIdType.MESH
BF = jnp.bfloat16
F32 = jnp.float32
VMEM = pltpu.VMEM
ANY = pl.ANY
MIB = 2**20

Y1, Y2, Y3 = 2, 4, 6
SIB, XN, DIAG = 1, 8, 9
A_MASKS = (0, SIB, XN, DIAG)
LO, HI = pl.ds(0, 64), pl.ds(64, 64)


def flip(value, mask):
    for bit in (1, 2, 4, 8):
        if mask & bit:
            value = value + bit - 2 * bit * lax.rem(lax.div(value, bit), 2)
    return value


def dev(t_mask, dp_mask=0):
    return (flip(lax.axis_index("dp"), dp_mask), flip(lax.axis_index("tensor"), t_mask))


def enter(partners):
    barrier = pltpu.get_barrier_semaphore()
    for partner in partners:
        pl.semaphore_signal(barrier, inc=1, device_id=dev(*partner), device_id_type=MESH)
    pl.semaphore_wait(barrier, len(partners))


def rcopy(src, dst, send, recv, target):
    return pltpu.make_async_remote_copy(
        src_ref=src, dst_ref=dst, send_sem=send, recv_sem=recv, device_id=dev(*target), device_id_type=MESH
    )


def nt(a, b):
    return lax.dot_general(a, b, (((1,), (1,)), ((), ())), preferred_element_type=F32)


def tn(a, b):
    return lax.dot_general(a, b, (((0,), (0,)), ((), ())), preferred_element_type=F32)


def nn(a, b):
    return jnp.dot(a, b, preferred_element_type=F32)


class Gather:
    def __init__(self, own, rows, send, recv):
        def c(i, src, dst, target):
            return rcopy(src, dst, send.at[i], recv.at[i], (target,))

        self.copies = [
            c(0, own.at[LO], rows.at[1, LO], Y1),
            c(1, own.at[HI], rows.at[3, HI], Y3),
            c(2, own.at[HI], rows.at[1, HI], Y1),
            c(3, own.at[LO], rows.at[3, LO], Y3),
            c(4, rows.at[1, LO], rows.at[2, LO], Y3),
            c(5, rows.at[3, HI], rows.at[2, HI], Y1),
        ]

    def start(self):
        for i in range(4):
            self.copies[i].start()

    def forward(self):
        self.copies[0].wait_recv()
        self.copies[4].start()
        self.copies[1].wait_recv()
        self.copies[5].start()

    def arrived(self, slot):
        for i in {1: (2,), 3: (3,), 2: (4, 5)}[slot]:
            self.copies[i].wait_recv()

    def finish(self):
        for c in self.copies:
            c.wait_send()


class Scatter:
    def __init__(self, out, passed, got, send, recv):
        def c(i, src, dst, target):
            return rcopy(src, dst, send.at[i], recv.at[i], (target,))

        self.out, self.passed, self.got = out, passed, got
        self.copies = [
            c(0, out.at[0, LO], passed.at[LO], Y1),
            c(1, out.at[0, HI], passed.at[HI], Y3),
            c(2, out.at[1, LO], got.at[0, LO], Y1),
            c(3, out.at[2, HI], got.at[1, HI], Y3),
            c(4, out.at[2, LO], got.at[1, LO], Y3),
            c(5, out.at[1, HI], got.at[0, HI], Y1),
        ]

    def opposite(self, part):
        self.out[0] = part.astype(BF)
        self.copies[0].start()
        self.copies[1].start()

    def first(self, part):
        self.out[1, LO] = part[0:64].astype(BF)
        self.copies[2].start()

    def second(self, part):
        self.out[2, HI] = part[64:128].astype(BF)
        self.copies[3].start()

    def relay(self, first_ref, second_ref):
        self.copies[0].wait_recv()
        self.out[2, LO] = (second_ref[LO] + self.passed[LO].astype(F32)).astype(BF)
        self.copies[4].start()
        self.copies[1].wait_recv()
        self.out[1, HI] = (first_ref[HI] + self.passed[HI].astype(F32)).astype(BF)
        self.copies[5].start()

    def total(self):
        for i in (2, 3, 4, 5):
            self.copies[i].wait_recv()
        return self.got[0].astype(F32) + self.got[1].astype(F32)

    def finish(self):
        for c in self.copies:
            c.wait_send()


def gelu_parts(x):
    cdf = 0.5 * (1.0 + lax.erf(x * (0.5**0.5)))
    return x * cdf, cdf + x * jnp.exp(-0.5 * x * x) * 0.3989422804014327


def front_kernel(
    hist, latest, mix_gain, mix_first, mix_second, mix_bias, gains, x_out, n_out, inv_out, resid_out, mix_out, pre_out, mix
):
    @pl.when(pl.program_id(0) == 0)
    def _():
        last = latest[0].astype(F32)
        inverse = lax.rsqrt(jnp.mean(last * last, axis=-1, keepdims=True) + NORM_EPS)
        pre = jnp.dot(last * inverse * mix_gain[...], mix_first[...], precision=PRECISE, preferred_element_type=F32)
        pre_out[...] = pre
        hidden = gelu_parts(pre)[0]
        mixing = jnp.dot(hidden, mix_second[...], precision=PRECISE, preferred_element_type=F32) + mix_bias[...]
        mix[...] = mixing
        mix_out[...] = mixing

    rows = hist.shape[1]
    here = mix[pl.ds(pl.multiple_of(pl.program_id(0) * rows, rows), rows), :]
    spread = [jnp.broadcast_to(here[:, i : i + 1], (rows, 128)) for i in range(MIX)]
    squares = [jnp.zeros((rows, 128), F32) for _ in range(3)]
    sums = []
    width = 256
    for c in range(D // width):
        tiles = [[None] * (width // 128) for _ in range(STREAMS)]
        for j in range(HISTORY):
            h = hist[j, :, c * width : (c + 1) * width].astype(F32)
            for lane in range(width // 128):
                piece = h[:, lane * 128 : (lane + 1) * 128]
                for k in range(STREAMS):
                    term = spread[k * HISTORY + j] * piece
                    tiles[k][lane] = term if j == 0 else tiles[k][lane] + term
        for lane in range(width // 128):
            at = slice(c * width + lane * 128, c * width + (lane + 1) * 128)
            resid_out[:, at] = tiles[3][lane]
            for k in range(3):
                squares[k] = squares[k] + tiles[k][lane] * tiles[k][lane]
        sums.append(tiles)
    for k in range(3):
        inverse = lax.rsqrt(jnp.sum(squares[k], axis=-1, keepdims=True) * (1.0 / D) + NORM_EPS)
        inv_out[k] = jnp.broadcast_to(inverse, (rows, 128))
        for c in range(D // width):
            for lane in range(width // 128):
                at = slice(c * width + lane * 128, c * width + (lane + 1) * 128)
                normal = sums[c][k][lane] * inverse
                n_out[k, :, at] = normal.astype(BF)
                x_out[k, :, at] = (normal * gains[k : k + 1, at]).astype(BF)


def front(history, mix_gain, mix_first, mix_second, mix_bias, gains):
    rows = 16
    return pl.pallas_call(
        front_kernel,
        grid=(ROWS // rows,),
        in_specs=[
            pl.BlockSpec((HISTORY, rows, D), lambda i: (0, i, 0)),
            pl.BlockSpec((1, ROWS, D), lambda i: (HISTORY - 1, 0, 0)),
            pl.BlockSpec((1, D), lambda i: (0, 0)),
            pl.BlockSpec((D, MIX), lambda i: (0, 0)),
            pl.BlockSpec((MIX, MIX), lambda i: (0, 0)),
            pl.BlockSpec((1, MIX), lambda i: (0, 0)),
            pl.BlockSpec((3, D), lambda i: (0, 0)),
        ],
        out_specs=[
            pl.BlockSpec((3, rows, D), lambda i: (0, i, 0)),
            pl.BlockSpec((3, rows, D), lambda i: (0, i, 0)),
            pl.BlockSpec((3, rows, 128), lambda i: (0, i, 0)),
            pl.BlockSpec((rows, D), lambda i: (i, 0)),
            pl.BlockSpec((ROWS, MIX), lambda i: (0, 0)),
            pl.BlockSpec((ROWS, MIX), lambda i: (0, 0)),
        ],
        out_shape=[
            jax.ShapeDtypeStruct((3, ROWS, D), BF),
            jax.ShapeDtypeStruct((3, ROWS, D), BF),
            jax.ShapeDtypeStruct((3, ROWS, 128), F32),
            jax.ShapeDtypeStruct((ROWS, D), F32),
            jax.ShapeDtypeStruct((ROWS, MIX), F32),
            jax.ShapeDtypeStruct((ROWS, MIX), F32),
        ],
        scratch_shapes=[VMEM((ROWS, MIX), F32)],
        compiler_params=pltpu.CompilerParams(vmem_limit_bytes=48 * MIB),
        name="front",
    )(history, history, mix_gain[None], mix_first, mix_second, mix_bias[None], gains)


def qkv_kernel(
    x, w_query, w_key, w_value, w_output, w_expand,
    heads, rows_out, w_out, wo_all, we_two,
    rows, weights, proj, g_send, g_recv, w_send, w_recv, f_send, f_recv, h_send, h_recv, local,
):
    enter([(Y1,), (Y3,), (SIB,), (XN,), (XN, 4), (DIAG,)])
    t = lax.axis_index("tensor")
    sources = [w_query, w_key, w_value, w_output, w_expand]
    slots = [lambda r, i=i: weights.at[i, r] for i in range(3)]
    slots += [lambda r: wo_all.at[r], lambda r: we_two.at[r - 1]]
    to_sib, to_x, onward = [], [], []
    for i, src in enumerate(sources):
        half = src.shape[0] // 2
        lo, hi = pl.ds(0, half), pl.ds(half, half)
        to_x.append(
            (
                rcopy(src.at[lo], slots[i](2).at[lo], w_send.at[i, 0], w_recv.at[i, 0], (XN,)),
                rcopy(src.at[hi], slots[i](2).at[hi], w_send.at[i, 1], w_recv.at[i, 1], (XN, 4)),
            )
        )
        to_sib.append(rcopy(src, slots[i](1), w_send.at[i, 2], w_recv.at[i, 2], (SIB,)))
        if i < 4:
            onward.append(rcopy(slots[i](2), slots[i](3), f_send.at[i], f_recv.at[i], (SIB,)))
    keep = [pltpu.make_async_copy(sources[i], slots[i](0), local.at[i]) for i in range(4)]
    gathers = [Gather(x.at[a], rows.at[a], g_send.at[a], g_recv.at[a]) for a in range(3)]
    for a in range(3):
        to_x[a][0].start()
        to_x[a][1].start()
        gathers[a].start()
        to_sib[a].start()
        keep[a].start()
    for i in (3, 4):
        to_x[i][0].start()
        to_x[i][1].start()
        to_sib[i].start()
    keep[3].start()
    for a in range(3):
        for c in to_x[a]:
            c.wait_recv()
        onward[a].start()
        gathers[a].forward()
    sends = []

    def project(a, s):
        block = x[a] if s == 0 else rows[a, s]
        for p in range(2):
            pair = jnp.concatenate([weights[a, 2 * p], weights[a, 2 * p + 1]], axis=1)
            y = nn(block, pair).astype(BF)
            proj[a, s, 2 * p] = y[:, :128]
            proj[a, s, 2 * p + 1] = y[:, 128:]
        place = flip(t, 2 * s)
        for r in range(4):
            src, dst = proj.at[a, s, r], heads.at[a, place]
            if r == 0:
                c = pltpu.make_async_copy(src, dst, h_send.at[a, s, 0])
            else:
                c = rcopy(src, dst, h_send.at[a, s, r], h_recv.at[a, s, r], (A_MASKS[r],))
            c.start()
            sends.append((r, c))

    for a in range(3):
        keep[a].wait()
        to_sib[a].wait_recv()
        onward[a].wait_recv()
        project(a, 0)
    store = []
    for a in range(3):
        c = pltpu.make_async_copy(weights.at[a], w_out.at[a], local.at[4 + a])
        c.start()
        store.append(c)
        c = pltpu.make_async_copy(x.at[a], rows_out.at[a, 0], local.at[7 + a])
        c.start()
        store.append(c)
    for a in range(3):
        for s in (1, 3):
            gathers[a].arrived(s)
            project(a, s)
    for c in to_x[3]:
        c.wait_recv()
    onward[3].start()
    for a in range(3):
        gathers[a].arrived(2)
        project(a, 2)
        c = pltpu.make_async_copy(rows.at[a, pl.ds(1, 3)], rows_out.at[a, pl.ds(1, 3)], local.at[10 + a])
        c.start()
        store.append(c)
    for g in gathers:
        g.finish()
    for r, c in sends:
        if r == 0:
            c.wait()
        else:
            c.wait_send()
    for r, c in sends:
        if r:
            c.wait_recv()
    for i in range(5):
        for c in to_x[i]:
            c.wait_send()
            if i > 3:
                c.wait_recv()
        to_sib[i].wait_send()
        if i > 2:
            to_sib[i].wait_recv()
    for i in range(4):
        onward[i].wait_send()
    onward[3].wait_recv()
    keep[3].wait()
    for c in store:
        c.wait()


def qkv(x, w_query, w_key, w_value, w_output, w_expand):
    dma = pltpu.SemaphoreType.DMA
    return pl.pallas_call(
        qkv_kernel,
        in_specs=[pl.BlockSpec(memory_space=VMEM)] + [pl.BlockSpec(memory_space=ANY)] * 5,
        out_specs=[pl.BlockSpec(memory_space=ANY)] * 5,
        out_shape=[
            jax.ShapeDtypeStruct((3, 16, ROWS, HEAD_DIM), BF),
            jax.ShapeDtypeStruct((3, 4, ROWS, D), BF),
            jax.ShapeDtypeStruct((3, 4, D, HEAD_DIM), BF),
            jax.ShapeDtypeStruct((4, HEAD_DIM, D), BF),
            jax.ShapeDtypeStruct((2, D, FF_SHARD), BF),
        ],
        scratch_shapes=[
            VMEM((3, 4, ROWS, D), BF),
            VMEM((3, 4, D, HEAD_DIM), BF),
            VMEM((3, 4, 4, ROWS, HEAD_DIM), BF),
            dma((3, 6)), dma((3, 6)), dma((5, 3)), dma((5, 3)), dma((4,)), dma((4,)), dma((3, 4, 4)), dma((3, 4, 4)), dma((13,)),
        ],
        compiler_params=pltpu.CompilerParams(collective_id=1, has_side_effects=True, vmem_limit_bytes=48 * MIB),
        cost_estimate=pl.CostEstimate(flops=6 * 512 * 2048 * 512, bytes_accessed=30 * MIB, transcendentals=0),
        name="qkv",
    )(x, w_query, w_key, w_value, w_output, w_expand)


def attend_kernel(q, k, v, first, ctx):
    tokens, step = q.shape[0], 256
    scale = HEAD_DIM ** (-0.5)
    for i in range(tokens // step):
        length = (i + 1) * step
        at = slice(i * step, length)
        scores = nt(q[at], k[:length]) * scale
        key_place = lax.broadcasted_iota(jnp.int32, (step, length), 1)
        query_place = lax.broadcasted_iota(jnp.int32, (step, 1), 0) + i * step
        allowed = (key_place >= first[at]) & (key_place <= query_place)
        scores = jnp.where(allowed, scores, MASKED)
        top = jnp.max(scores, axis=-1, keepdims=True)
        e = jnp.exp(scores - top)
        low = (e * (1.0 / jnp.sum(e, axis=-1, keepdims=True))).astype(BF)
        ctx[at] = nn(low, v[:length]).astype(BF)


def attend_back_kernel(q, k, v, gc, first, dq, dk, dv, dk_sum, dv_sum, hooks):
    tokens, step = q.shape[0], 256
    scale = HEAD_DIM ** (-0.5)
    k_turned = k[...].astype(F32).T.astype(BF)
    for i in range(tokens // step):
        if i in hooks:
            hooks[i]()
        length = (i + 1) * step
        at = slice(i * step, length)
        scores = nt(k[:length], q[at]) * scale
        key_place = lax.broadcasted_iota(jnp.int32, (length, step), 0)
        query_place = lax.broadcasted_iota(jnp.int32, (1, step), 1) + i * step
        allowed = (key_place >= first[:, at]) & (key_place <= query_place)
        scores = jnp.where(allowed, scores, MASKED)
        top = jnp.max(scores, axis=0, keepdims=True)
        e = jnp.exp(scores - top)
        probs = e * (1.0 / jnp.sum(e, axis=0, keepdims=True))
        grad_probs = nt(v[:length], gc[at])
        delta = jnp.sum(grad_probs * probs, axis=0, keepdims=True)
        grad_scores = (probs * (grad_probs - delta)).astype(BF)
        low = probs.astype(BF)
        dq[at] = (nn(k_turned[:, :length], grad_scores) * scale).T.astype(BF)
        key_part = nn(grad_scores, q[at])
        value_part = nn(low, gc[at])
        if i:
            dk_sum[: i * step] += key_part[: i * step]
            dv_sum[: i * step] += value_part[: i * step]
        dk_sum[at] = key_part[i * step :]
        dv_sum[at] = value_part[i * step :]
    dk[...] = (dk_sum[...] * scale).astype(BF)
    dv[...] = dv_sum[...].astype(BF)


def mlp_kernel(
    q, k, v, first_place, wo_all, resid, gain, cot, w_expand, we_two, w_reduce,
    ctx_rows, middle_out, reduced_out, keep_out, sib_out, grad_gain, grad_middle, grad_low,
    ctx, we, wr, mlp_rows, cot_rows, act, gexp, turned, parts, stage, sc_out, sc_pass, sc_got,
    g_send, g_recv, s_send, s_recv, w_send, w_recv, c_send, c_recv, d_send, d_recv, local,
):
    enter([(Y1,), (Y3,), (SIB,), (XN,), (XN, 4), (DIAG,)])
    t = lax.axis_index("tensor")
    cot_gather = Gather(cot, cot_rows, g_send.at[0], g_recv.at[0])
    cot_gather.start()
    half = FF_SHARD // 2
    lo, hi = pl.ds(0, half), pl.ds(half, half)
    loads = [
        pltpu.make_async_copy(w_expand, we.at[0], local.at[0]),
        pltpu.make_async_copy(we_two, we.at[pl.ds(1, 2)], local.at[1]),
        pltpu.make_async_copy(w_reduce, wr.at[0], local.at[2]),
    ]
    for c in loads:
        c.start()
    sib = [
        rcopy(we_two.at[1], we.at[3], w_send.at[0], w_recv.at[0], (SIB,)),
        rcopy(w_reduce, wr.at[1], w_send.at[1], w_recv.at[1], (SIB,)),
        rcopy(wr.at[2], wr.at[3], w_send.at[2], w_recv.at[2], (SIB,)),
    ]
    across = [
        rcopy(w_reduce.at[lo], wr.at[2, lo], w_send.at[3], w_recv.at[3], (XN,)),
        rcopy(w_reduce.at[hi], wr.at[2, hi], w_send.at[4], w_recv.at[4], (XN, 4)),
    ]
    sib[0].start()
    sib[1].start()
    cot_gather.forward()
    attend_kernel(q, k, v, first_place, ctx)
    back = {}
    for s in (2, 1, 3, 0):
        for r in range(4):
            place = pl.multiple_of(flip(t, A_MASKS[r] + 2 * s) * ROWS, ROWS)
            src, dst = ctx.at[pl.ds(place, ROWS)], ctx_rows.at[s, r]
            if r:
                back[s, r] = rcopy(src, dst, c_send.at[s, r], c_recv.at[s, r], (A_MASKS[r],))
            else:
                back[s, r] = pltpu.make_async_copy(src, dst, c_send.at[s, r])
            back[s, r].start()
    for c in across:
        c.start()

    def rows_of(s):
        for r in range(4):
            back[s, r].wait_recv() if r else back[s, r].wait()
        return jnp.concatenate([ctx_rows[s, r] for r in range(4)], axis=1)

    weight = wo_all[...].reshape(4 * HEAD_DIM, D)

    def scatter(index, part_of):
        sc = Scatter(sc_out.at[index], sc_pass.at[index], sc_got.at[index], s_send.at[index], s_recv.at[index])
        part_of(2, parts.at[0])
        sc.opposite(parts[0])
        part_of(1, parts.at[1])
        sc.first(parts[1])
        part_of(3, parts.at[2])
        sc.second(parts[2])
        sc.relay(parts.at[1], parts.at[2])
        part_of(0, parts.at[0])
        return sc

    def attended(s, into):
        into[...] = nn(rows_of(s), weight)

    sc = scatter(0, attended)
    for c in across:
        c.wait_recv()
    sib[2].start()
    middle = resid[...] + parts[0] + sc.total()
    middle_out[...] = middle
    inverse = lax.rsqrt(jnp.mean(middle * middle, axis=-1, keepdims=True) + NORM_EPS)
    mlp_rows[0] = (middle * inverse * gain[...]).astype(BF)
    mlp_gather = Gather(mlp_rows.at[0], mlp_rows, g_send.at[1], g_recv.at[1])
    mlp_gather.start()
    for c in loads:
        c.wait()
    for c in sib:
        c.wait_recv()
    cot_rows[0] = cot[...]

    def block(s):
        @pl.loop(0, 4)
        def _(r):
            expanded = nn(mlp_rows[s], we[r])
            grad_active = nt(cot_rows[s], wr[r])
            value, slope = gelu_parts(expanded)
            act[s, r] = value.astype(BF)
            gexp[s, r] = (grad_active * slope).astype(BF)

    block(0)
    mlp_gather.forward()
    for s in (1, 3, 2):
        cot_gather.arrived(s)
        mlp_gather.arrived(s)
        block(s)

    def grad_mlp(s, into):
        into[...] = jnp.zeros((ROWS, D), F32)

        @pl.loop(0, 4)
        def _(r):
            into[...] += nt(gexp[s, r], we[r])

    sc2 = scatter(1, grad_mlp)
    turned[...] = mlp_rows[...].reshape(512, D).T
    cot_all = cot_rows[...].reshape(512, D)
    sends = {}
    for n, r in enumerate((1, 3, 0, 2)):
        buffer = stage.at[n % 2]
        if n > 1:
            sends[n - 2].wait_send()
        grad_e = nn(turned[...], gexp[:, r].reshape(512, FF_SHARD)).astype(BF)
        for d in range(8):
            for c in range(2):
                buffer[d, c * 256 : (c + 1) * 256] = grad_e[d * 256 : (d + 1) * 256, c * 256 : (c + 1) * 256]
        grad_r = tn(act[:, r].reshape(512, FF_SHARD), cot_all).astype(BF)
        for d in range(8):
            buffer[d, 512:] = grad_r[:, d * 256 : (d + 1) * 256]
        if n < 2:
            c = rcopy(buffer, sib_out.at[n], d_send.at[n], d_recv.at[n], (SIB,))
        else:
            c = pltpu.make_async_copy(buffer, keep_out.at[n - 2], d_send.at[n])
        c.start()
        sends[n] = c
    for s in range(4):
        reduced = nn(act[s, 0], wr[0])
        for r in range(1, 4):
            reduced += nn(act[s, r], wr[r])
        reduced_out[s] = reduced.astype(BF)
    got = parts[0] + sc2.total()
    middle = middle_out[...]
    inverse = lax.rsqrt(jnp.mean(middle * middle, axis=-1, keepdims=True) + NORM_EPS)
    normal = middle * inverse
    grad_gain[...] = jnp.sum(got * normal, axis=0, keepdims=True)
    scaled = got * gain[...]
    grad = cot[...].astype(F32) + inverse * (scaled - normal * jnp.mean(scaled * normal, axis=-1, keepdims=True))
    grad_middle[...] = grad
    grad_low[...] = grad.astype(BF)
    sc.finish()
    sc2.finish()
    cot_gather.finish()
    mlp_gather.finish()
    for c in sib + across:
        c.wait_send()
    for (s, r), c in back.items():
        if r:
            c.wait_send()
    for n in range(2):
        sends[n].wait_recv()
    for n in (2, 3):
        sends[n].wait()


def mlp(q, k, v, first_column, wo_all, resid, gain_mlp, cot, w_expand, we_two, w_reduce):
    dma = pltpu.SemaphoreType.DMA
    vm, hbm = pl.BlockSpec(memory_space=VMEM), pl.BlockSpec(memory_space=ANY)
    return pl.pallas_call(
        mlp_kernel,
        in_specs=[vm] * 8 + [hbm] * 3,
        out_specs=[vm, vm, vm, hbm, hbm, vm, vm, vm],
        out_shape=[
            jax.ShapeDtypeStruct((4, 4, ROWS, HEAD_DIM), BF),
            jax.ShapeDtypeStruct((ROWS, D), F32),
            jax.ShapeDtypeStruct((4, ROWS, D), BF),
            jax.ShapeDtypeStruct((2, 8, 1024, 256), BF),
            jax.ShapeDtypeStruct((2, 8, 1024, 256), BF),
            jax.ShapeDtypeStruct((1, D), F32),
            jax.ShapeDtypeStruct((ROWS, D), F32),
            jax.ShapeDtypeStruct((ROWS, D), BF),
        ],
        scratch_shapes=[
            VMEM((2048, HEAD_DIM), BF),
            VMEM((4, D, FF_SHARD), BF),
            VMEM((4, FF_SHARD, D), BF),
            VMEM((4, ROWS, D), BF),
            VMEM((4, ROWS, D), BF),
            VMEM((4, 4, ROWS, FF_SHARD), BF),
            VMEM((4, 4, ROWS, FF_SHARD), BF),
            VMEM((D, 512), BF),
            VMEM((3, ROWS, D), F32),
            VMEM((2, 8, 1024, 256), BF),
            VMEM((2, 3, ROWS, D), BF),
            VMEM((2, ROWS, D), BF),
            VMEM((2, 2, ROWS, D), BF),
            dma((2, 6)), dma((2, 6)), dma((2, 6)), dma((2, 6)), dma((5,)), dma((5,)), dma((4, 4)), dma((4, 4)),
            dma((4,)), dma((4,)), dma((3,)),
        ],
        compiler_params=pltpu.CompilerParams(collective_id=2, has_side_effects=True, vmem_limit_bytes=60 * MIB),
        cost_estimate=pl.CostEstimate(flops=30 * 10**9, bytes_accessed=50 * MIB, transcendentals=0),
        name="mlp",
    )(q, k, v, first_column, wo_all, resid, gain_mlp[None], cot, w_expand, we_two, w_reduce)


class Ring:
    def __init__(self, part, out, passed, got, send, recv, near, far, size):
        half = size // 2
        lo, hi = pl.ds(0, half), pl.ds(half, half)

        def c(i, src, dst, target):
            return rcopy(src, dst, send.at[i], recv.at[i], target)

        self.part, self.out, self.passed, self.got, self.lo, self.hi = part, out, passed, got, lo, hi
        self.copies = [
            c(0, out.at[0, lo], passed.at[lo], near),
            c(1, out.at[0, hi], passed.at[hi], far),
            c(2, out.at[1, lo], got.at[0, lo], near),
            c(3, out.at[2, hi], got.at[1, hi], far),
            c(4, out.at[2, lo], got.at[1, lo], far),
            c(5, out.at[1, hi], got.at[0, hi], near),
        ]

    def begin(self):
        for i, (slot, s, half) in enumerate(((0, 2, self.lo), (0, 2, self.hi), (1, 1, self.lo), (2, 3, self.hi))):
            self.out[slot, half] = self.part(s, half).astype(BF)
            self.copies[i].start()

    def send(self, slot, s, half, value, i):
        self.out[slot, half] = value.astype(BF)
        self.copies[i].start()

    def relay(self):
        for i, slot, s, half in ((0, 2, 3, self.lo), (1, 1, 1, self.hi)):
            self.copies[i].wait_recv()
            self.out[slot, half] = (self.part(s, half) + self.passed[half].astype(F32)).astype(BF)
            self.copies[4 + i].start()

    def arrive(self):
        for i in (2, 3, 4, 5):
            self.copies[i].wait_recv()

    def total(self, index):
        return self.part(0, index) + self.got[0, index].astype(F32) + self.got[1, index].astype(F32)

    def finish(self):
        for c in self.copies:
            c.wait_send()


X_RING = ((XN,), (XN, 4))
Z_RING = ((0, 1), (0, 3))


class GridSum:
    @staticmethod
    def scratch(rows):
        half, dma = rows // 2, pltpu.SemaphoreType.DMA
        return [
            VMEM((2, 8, rows, 256), BF),
            VMEM((2, 8, rows, 256), BF),
            VMEM((2, 3, 4, half, 256), BF),
            VMEM((2, 4, half, 256), BF),
            VMEM((2, 2, 4, half, 256), BF),
            VMEM((2, 4, half, 256), F32),
            VMEM((2, 3, half, 256), BF),
            VMEM((2, half, 256), BF),
            VMEM((2, 2, half, 256), BF),
            dma((4, 6)),
            dma((4, 6)),
            dma((4,)),
        ]

    def __init__(self, pieces, scratch):
        (self.a, self.b, out1, pass1, got1, self.mid, out2, pass2, got2, send, recv, load) = scratch
        rows = self.a.shape[2]
        self.half = half = rows // 2
        self.loads, start = [], 0
        for i, (kept, given) in enumerate(pieces):
            at = pl.ds(start, kept.shape[2])
            start += kept.shape[2]
            self.loads += [
                pltpu.make_async_copy(kept, self.a.at[:, :, at], load.at[2 * i]),
                pltpu.make_async_copy(given, self.b.at[:, :, at], load.at[2 * i + 1]),
            ]
        dp = lax.axis_index("dp")
        place = {(sx, sz): flip(dp, (4 if sx in (2, 3) else 0) + sz) for sx in range(4) for sz in range(4)}

        def block(sx, sz, path):
            shard = 0 if sx in (0, 2) else 1
            at = slice(path * half, (path + 1) * half)
            d = place[sx, sz]
            return self.a[shard, d, at].astype(F32) + self.b[shard, d, at].astype(F32)

        def span(ds):
            return range(ds.start, ds.start + ds.size)

        def over_x(s, half_):
            return jnp.stack([block(s, z, 0) for z in span(half_)])

        def over_z(s, half_):
            return jnp.stack([block(x, s, 1) for x in span(half_)])

        rings = (X_RING, Z_RING)
        self.first, self.second = [], []
        for path, part in enumerate((over_x, over_z)):
            near, far = rings[path]
            self.first.append(
                Ring(part, out1.at[path], pass1.at[path], got1.at[path], send.at[path], recv.at[path], near, far, 4)
            )
            near, far = rings[1 - path]
            mid = self.mid.at[path]

            def later(s, half_, mid=mid):
                return mid[s, half_]

            self.second.append(
                Ring(
                    later, out2.at[path], pass2.at[path], got2.at[path], send.at[2 + path], recv.at[2 + path], near, far, half
                )
            )

    def load(self):
        for c in self.loads:
            c.start()

    def begin(self):
        for c in self.loads:
            c.wait()
        for ring in self.first:
            ring.begin()

    def relay(self):
        for ring in self.first:
            ring.relay()

    def turn(self):
        for path in range(2):
            ring = self.first[path]
            ring.arrive()
            for s in (2, 1, 3, 0):
                self.mid[path, s] = ring.total(pl.ds(s, 1))[0]
            self.second[path].begin()

    def relay2(self):
        for ring in self.second:
            ring.relay()

    def result(self):
        parts = []
        for ring in self.second:
            ring.arrive()
            parts.append(ring.total(pl.ds(0, self.half)))
        return jnp.concatenate(parts, axis=0)

    def finish(self):
        for ring in self.first + self.second:
            ring.finish()


def back_kernel(
    q, k, v, first_place, grad_low, wo_all, ctx_rows, reduced, middle, keep_in, sib_in,
    output, grads, summed, keep_out, sib_out,
    rows, proj, gc, dk_sum, dv_sum, stage, sc_out, sc_pass, sc_got,
    g_send, g_recv, s_send, s_recv, c_send, c_recv, d_send, d_recv, *grid_scratch,
):
    enter([(Y1,), (Y3,), (SIB,), (DIAG,), *X_RING, *Z_RING])
    t = lax.axis_index("tensor")
    gather = Gather(grad_low, rows, g_send, g_recv)
    gather.start()
    part = pl.ds(0, 512)
    grid = GridSum([(keep_in.at[:, :, part], sib_in.at[:, :, part])], grid_scratch)
    grid.load()
    ring = Ring(
        lambda s, half: reduced[s, half].astype(F32), sc_out, sc_pass, sc_got, s_send, s_recv, (Y1,), (Y3,), ROWS
    )
    rows[0] = grad_low[...]
    weight = wo_all[...].reshape(4 * HEAD_DIM, D)
    moves = []

    def project(s):
        y = nt(rows[s], weight).astype(BF)
        place = pl.multiple_of(flip(t, 2 * s) * ROWS, ROWS)
        for r in range(4):
            proj[s, r] = y[:, r * HEAD_DIM : (r + 1) * HEAD_DIM]
            src, dst = proj.at[s, r], gc.at[pl.ds(place, ROWS)]
            if r:
                c = rcopy(src, dst, c_send.at[s, r], c_recv.at[s, r], (A_MASKS[r],))
            else:
                c = pltpu.make_async_copy(src, dst, c_send.at[s, r])
            c.start()
            moves.append((r, c))

    project(0)
    gather.forward()
    ring.begin()
    grid.begin()
    for s in (1, 3, 2):
        gather.arrived(s)
        project(s)
    ring.relay()
    grid.relay()
    all_rows = rows[...].reshape(4 * ROWS, D)
    sends = []
    for n, r in enumerate((1, 3, 0, 2)):
        lhs = jnp.concatenate([ctx_rows[s, r] for s in range(4)], axis=0)
        grad_o = tn(lhs, all_rows).astype(BF)
        for d in range(8):
            stage[n, d] = grad_o[:, d * 256 : (d + 1) * 256]
        if n < 2:
            c = rcopy(stage.at[n], sib_out.at[n], d_send.at[n], d_recv.at[n], (SIB,))
        else:
            c = pltpu.make_async_copy(stage.at[n], keep_out.at[n - 2], d_send.at[n])
        c.start()
        sends.append(c)
    for r, c in moves:
        c.wait_recv() if r else c.wait()
    hooks = {4: grid.turn, 7: grid.relay2}
    attend_back_kernel(q, k, v, gc, first_place, grads.at[0], grads.at[1], grads.at[2], dk_sum, dv_sum, hooks)
    summed[...] = grid.result()
    grid.finish()
    ring.arrive()
    output[...] = (middle[...] + ring.total(pl.ds(0, ROWS))).astype(BF)
    gather.finish()
    ring.finish()
    for r, c in moves:
        if r:
            c.wait_send()
    for n, c in enumerate(sends):
        c.wait()


def back(q, k, v, first_row, grad_low, wo_all, ctx_rows, reduced, middle, keep, sib):
    dma = pltpu.SemaphoreType.DMA
    vm, hbm = pl.BlockSpec(memory_space=VMEM), pl.BlockSpec(memory_space=ANY)
    return pl.pallas_call(
        back_kernel,
        in_specs=[vm] * 9 + [hbm] * 2,
        out_specs=[vm, vm, vm, hbm, hbm],
        out_shape=[
            jax.ShapeDtypeStruct((ROWS, D), BF),
            jax.ShapeDtypeStruct((3, 2048, HEAD_DIM), BF),
            jax.ShapeDtypeStruct((512, 256), F32),
            jax.ShapeDtypeStruct((2, 8, ROWS, 256), BF),
            jax.ShapeDtypeStruct((2, 8, ROWS, 256), BF),
        ],
        scratch_shapes=[
            VMEM((4, ROWS, D), BF),
            VMEM((4, 4, ROWS, HEAD_DIM), BF),
            VMEM((2048, HEAD_DIM), BF),
            VMEM((2048, HEAD_DIM), F32),
            VMEM((2048, HEAD_DIM), F32),
            VMEM((4, 8, ROWS, 256), BF),
            VMEM((3, ROWS, D), BF),
            VMEM((ROWS, D), BF),
            VMEM((2, ROWS, D), BF),
            dma((6,)), dma((6,)), dma((6,)), dma((6,)), dma((4, 4)), dma((4, 4)), dma((4,)), dma((4,)),
            *GridSum.scratch(512),
        ],
        compiler_params=pltpu.CompilerParams(collective_id=3, has_side_effects=True, vmem_limit_bytes=60 * MIB),
        cost_estimate=pl.CostEstimate(flops=8 * 10**9, bytes_accessed=20 * MIB, transcendentals=0),
        name="back",
    )(q, k, v, first_row, grad_low, wo_all, ctx_rows, reduced, middle, keep, sib)


def streams_kernel(
    grads, rows_in, w_in, keep_in, sib_in,
    out, summed, keep_out, sib_out,
    rows, weights, g, turned, parts, stage, sc_out, sc_pass, sc_got,
    s_send, s_recv, c_send, c_recv, d_send, d_recv, local, *grid_scratch,
):
    enter([(Y1,), (Y3,), (SIB,), (DIAG,), *X_RING, *Z_RING])
    t = lax.axis_index("tensor")
    part = pl.ds(512, 512)
    grid = GridSum([(keep_in.at[:, :, part], sib_in.at[:, :, part])], grid_scratch)
    moves = {}
    for a in range(3):
        for s in (2, 1, 3, 0):
            for r in range(4):
                place = pl.multiple_of(flip(t, A_MASKS[r] + 2 * s) * ROWS, ROWS)
                src, dst = grads.at[a, pl.ds(place, ROWS)], g.at[a, s, r]
                if r:
                    c = rcopy(src, dst, c_send.at[a, s, r], c_recv.at[a, s, r], (A_MASKS[r],))
                else:
                    c = pltpu.make_async_copy(src, dst, c_send.at[a, s, r])
                c.start()
                moves[a, s, r] = c
    loads = []
    for a in range(3):
        c = pltpu.make_async_copy(w_in.at[a], weights.at[a], local.at[a])
        c.start()
        loads.append(c)
    for a in range(3):
        loads.append(pltpu.make_async_copy(rows_in.at[a], rows, local.at[3 + a]))
    loads[3].start()
    grid.load()
    rings = []
    for a in range(3):
        loads[a].wait()
        weight = jnp.concatenate([weights[a, r] for r in range(4)], axis=1)
        ring = Ring(
            lambda s, half, a=a: parts[a, pl.ds({0: 0, 1: 64, 3: 192}[s] + half.start, half.size)],
            sc_out.at[a], sc_pass.at[a], sc_got.at[a], s_send.at[a], s_recv.at[a], (Y1,), (Y3,), ROWS,
        )
        rings.append(ring)
        for s in (2, 1, 3, 0):
            for r in range(4):
                c = moves[a, s, r]
                c.wait_recv() if r else c.wait()
            lhs = jnp.concatenate([g[a, s, r] for r in range(4)], axis=1)
            value = nt(lhs, weight)
            if s == 0:
                parts[a, 0:128] = value
            elif s == 1:
                ring.send(1, s, ring.lo, value[:64], 2)
                parts[a, 128:192] = value[64:]
            elif s == 3:
                ring.send(2, s, ring.hi, value[64:], 3)
                parts[a, 192:256] = value[:64]
            else:
                ring.send(0, s, ring.lo, value[:64], 0)
                ring.send(0, s, ring.hi, value[64:], 1)
        if a == 0:
            grid.begin()
    for ring in rings:
        ring.relay()
    grid.relay()
    for a in range(3):
        loads[3 + a].wait()
        turned[...] = rows[...].reshape(512, D).T
        if a < 2:
            loads[4 + a].start()
        grad_w = nn(
            turned[...], jnp.concatenate([g[a, :, r].reshape(512, HEAD_DIM) for r in range(4)], axis=1)
        ).astype(BF)
        for n, r in enumerate((1, 3, 0, 2)):
            for d in range(8):
                block = grad_w[d * 256 : (d + 1) * 256, r * HEAD_DIM : (r + 1) * HEAD_DIM]
                if a < 2:
                    stage[n, d, 0:256, a * 128 : (a + 1) * 128] = block
                else:
                    stage[n, d, 256:384, 0:128] = block[:128]
                    stage[n, d, 256:384, 128:256] = block[128:]
        if a == 1:
            grid.turn()
    sends = []
    for n in range(4):
        if n < 2:
            c = rcopy(stage.at[n], sib_out.at[n], d_send.at[n], d_recv.at[n], (SIB,))
        else:
            c = pltpu.make_async_copy(stage.at[n], keep_out.at[n - 2], d_send.at[n])
        c.start()
        sends.append(c)
    grid.relay2()
    summed[...] = grid.result()
    grid.finish()
    for a, ring in enumerate(rings):
        ring.arrive()
        out[a] = ring.total(pl.ds(0, ROWS))
    for ring in rings:
        ring.finish()
    for (a, s, r), c in moves.items():
        if r:
            c.wait_send()
    for c in sends:
        c.wait()


def streams_back(grads, rows, w_all, keep, sib):
    dma = pltpu.SemaphoreType.DMA
    vm, hbm = pl.BlockSpec(memory_space=VMEM), pl.BlockSpec(memory_space=ANY)
    return pl.pallas_call(
        streams_kernel,
        in_specs=[vm, hbm, hbm, hbm, hbm],
        out_specs=[vm, vm, hbm, hbm],
        out_shape=[
            jax.ShapeDtypeStruct((3, ROWS, D), F32),
            jax.ShapeDtypeStruct((512, 256), F32),
            jax.ShapeDtypeStruct((2, 8, 384, 256), BF),
            jax.ShapeDtypeStruct((2, 8, 384, 256), BF),
        ],
        scratch_shapes=[
            VMEM((4, ROWS, D), BF),
            VMEM((3, 4, D, HEAD_DIM), BF),
            VMEM((3, 4, 4, ROWS, HEAD_DIM), BF),
            VMEM((D, 512), BF),
            VMEM((3, 256, D), F32),
            VMEM((4, 8, 384, 256), BF),
            VMEM((3, 3, ROWS, D), BF),
            VMEM((3, ROWS, D), BF),
            VMEM((3, 2, ROWS, D), BF),
            dma((3, 6)), dma((3, 6)), dma((3, 4, 4)), dma((3, 4, 4)), dma((4,)), dma((4,)), dma((6,)),
            *GridSum.scratch(512),
        ],
        compiler_params=pltpu.CompilerParams(collective_id=4, has_side_effects=True, vmem_limit_bytes=60 * MIB),
        cost_estimate=pl.CostEstimate(flops=8 * 10**9, bytes_accessed=20 * MIB, transcendentals=0),
        name="streams_back",
    )(grads, rows, w_all, keep, sib)


SMALL_ROWS, SMALL_COLS = 80, D + 128
RING_OF = {
    "y": ((Y1, 0), (Y2, 0), (Y3, 0)),
    "x": ((XN, 0), (0, 4), (XN, 4)),
    "z": ((0, 1), (0, 2), (0, 3)),
}


def finish_kernel(
    hist_in, gs, grad_middle, n, inv, mix, pre, mix_gain, mix_first, mix_second, gains, gain_mlp,
    keep_q, sib_q, keep_o, sib_o,
    grad_hist, summed, small_out,
    hist, ds, sums, gmix, extra, pack, acc, acc1, acc2, acc3, core_out, core_got, y_out, y_got, x_out, x_got, z_out, z_got,
    res, hist_sem, out_sem, r_send, r_recv, a_send, a_recv, *grid_scratch,
):
    load = pltpu.make_async_copy(hist_in, hist, hist_sem)
    load.start()
    enter([(SIB,), *RING_OF["y"], *RING_OF["x"], *RING_OF["z"]])
    grid = GridSum([(keep_q, sib_q), (keep_o, sib_o)], grid_scratch)
    grid.load()
    t, dp = lax.axis_index("tensor"), lax.axis_index("dp")
    core, y, z = lax.rem(t, 2), lax.rem(lax.div(t, 2), 4), lax.rem(dp, 4)
    x = 2 * lax.div(dp, 4) + lax.div(t, 8)
    sums[...] = jnp.zeros(sums.shape, F32)
    step = 16
    lane = lax.broadcasted_iota(jnp.int32, (step, 128), 1)
    grid.begin()
    load.wait()

    def gradients(tile):
        at = pl.ds(pl.multiple_of(tile * step, step), step)
        for k in range(3):
            g, normal = gs[k, at], n[k, at].astype(F32)
            gn = g * normal
            sums[k] += gn[:8] + gn[8:]
            scaled = g * gains[k : k + 1]
            mean = jnp.sum(scaled * normal, axis=-1, keepdims=True) * (1.0 / D)
            ds[k, at] = (scaled - normal * mean) * inv[k, at, 0:1]

        def entry(j, found):
            h = hist[j, at].astype(F32)
            for k in range(STREAMS):
                product = (ds[k, at] if k < 3 else grad_middle[at]) * h
                total = product[:, :128]
                for i in range(1, D // 128):
                    total = total + product[:, i * 128 : (i + 1) * 128]
                found = jnp.where(lane == k * HISTORY + j, jnp.sum(total, axis=-1, keepdims=True), found)
            return found

        gmix[at] = lax.fori_loop(0, HISTORY, entry, jnp.zeros((step, 128), F32))

    @pl.loop(0, 4)
    def _(tile):
        gradients(tile)

    grid.relay()

    @pl.loop(4, ROWS // step)
    def _(tile):
        gradients(tile)

    def exact(a, b, dims):
        return lax.dot_general(a, b, (dims, ((), ())), precision=PRECISE, preferred_element_type=F32)

    grad_mixing = gmix[:, :MIX]
    hidden, slope = gelu_parts(pre[...])
    last = hist[HISTORY - 1].astype(F32)
    inverse = lax.rsqrt(jnp.mean(last * last, axis=-1, keepdims=True) + NORM_EPS)
    normal = last * inverse
    grad_pre = exact(grad_mixing, mix_second[...], ((1,), (1,))) * slope
    pack[...] = jnp.zeros(pack.shape, F32)
    pack[0:MIX, 0:D] = exact(grad_pre, normal * mix_gain[...], ((0,), (0,)))
    pack[0:MIX, D : D + MIX] = exact(hidden, grad_mixing, ((0,), (0,)))
    grad_latest = exact(grad_pre, mix_first[...], ((1,), (1,)))
    pack[68:69, 0:D] = jnp.sum(grad_latest * normal, axis=0, keepdims=True)
    for k in range(3):
        pack[69 + k : 70 + k, 0:D] = jnp.sum(sums[k], axis=0, keepdims=True)
    pack[72:73, 0:D] = gain_mlp[...]
    pack[68:69, D : D + MIX] = jnp.sum(grad_mixing, axis=0, keepdims=True)
    scaled = grad_latest * mix_gain[...]
    extra[...] = inverse * (scaled - normal * jnp.mean(scaled * normal, axis=-1, keepdims=True))
    acc[...] = jnp.zeros(acc.shape, F32)
    columns = SMALL_COLS // 128
    for i in range(SMALL_ROWS // 16):
        for j in range(columns):
            b = i * columns + j
            acc[b // 64, b // 16 % 4, b // 4 % 4, b % 4] = pack[i * 16 : (i + 1) * 16, j * 128 : (j + 1) * 128]

    saves = []

    def history_tile(tile):
        at = pl.ds(tile * step, step)
        here = mix[at]
        spread = [jnp.broadcast_to(here[:, i : i + 1], (step, 128)) for i in range(MIX)]

        @pl.loop(0, D // 128)
        def _(c):
            cols = pl.ds(pl.multiple_of(c * 128, 128), 128)
            grad = [ds[k, at, cols] if k < 3 else grad_middle[at, cols] for k in range(STREAMS)]
            for j in range(HISTORY):
                value = spread[j] * grad[0]
                for k in range(1, STREAMS):
                    value = value + spread[k * HISTORY + j] * grad[k]
                if j == HISTORY - 1:
                    value = value + extra[at, cols]
                hist[j, at, cols] = value.astype(BF)

        c = pltpu.make_async_copy(hist.at[:, at], grad_hist.at[:, at], out_sem.at[tile])
        c.start()
        saves.append(c)

    core_out[...] = acc[1 - core].astype(BF)
    over_core = rcopy(core_out, core_got, r_send.at[0, 0], r_recv.at[0, 0], (SIB,))
    over_core.start()
    history_tile(0)
    over_core.wait()
    acc1[...] = acc[core] + core_got[...].astype(F32)

    def reduce_over(level, source, out, got, me, axis, between):
        copies = []
        for i, target in enumerate(RING_OF[axis]):
            out[i] = source[flip(me, i + 1)].astype(BF)
            c = rcopy(out.at[i], got.at[i], r_send.at[level, i], r_recv.at[level, i], target)
            c.start()
            copies.append(c)
        between()
        for c in copies:
            c.wait()
        return source[me] + got[0].astype(F32) + got[1].astype(F32) + got[2].astype(F32)

    acc2[...] = reduce_over(1, acc1, y_out, y_got, y, "y", lambda: history_tile(1))
    grid.turn()
    acc3[...] = reduce_over(2, acc2, x_out, x_got, x, "x", lambda: history_tile(2))
    total = reduce_over(3, acc3, z_out, z_got, z, "z", lambda: history_tile(3))
    res[core, y, x, z] = total.astype(BF)

    def spread_over(level, ref, axis, between):
        copies = []
        for i, target in enumerate(RING_OF[axis] if axis else ((SIB, 0),)):
            c = rcopy(ref, ref, a_send.at[level, i], a_recv.at[level, i], target)
            c.start()
            copies.append(c)
        between()
        for c in copies:
            c.wait()

    spread_over(0, res.at[core, y, x, z], "z", lambda: history_tile(4))
    grid.relay2()
    spread_over(1, res.at[core, y, x], "x", lambda: history_tile(5))
    spread_over(2, res.at[core, y], "y", lambda: history_tile(6))
    spread_over(3, res.at[core], "", lambda: history_tile(7))
    for i in range(SMALL_ROWS // 16):
        for j in range(columns):
            b = i * columns + j
            small_out[i * 16 : (i + 1) * 16, j * 128 : (j + 1) * 128] = res[b // 64, b // 16 % 4, b // 4 % 4, b % 4].astype(F32)
    summed[...] = grid.result()
    grid.finish()
    for c in saves:
        c.wait()


def finish(history, gs, grad_middle, n, inv, mix, pre, mix_gain, mix_first, mix_second, gains, gain_mlp, *packs):
    dma = pltpu.SemaphoreType.DMA
    vm, hbm = pl.BlockSpec(memory_space=VMEM), pl.BlockSpec(memory_space=ANY)
    tile = (16, 128)
    return pl.pallas_call(
        finish_kernel,
        in_specs=[hbm] + [vm] * 11 + [hbm] * 4,
        out_specs=[hbm, vm, vm],
        out_shape=[
            jax.ShapeDtypeStruct((HISTORY, ROWS, D), BF),
            jax.ShapeDtypeStruct((512, 256), F32),
            jax.ShapeDtypeStruct((SMALL_ROWS, SMALL_COLS), F32),
        ],
        scratch_shapes=[
            VMEM((HISTORY, ROWS, D), BF),
            VMEM((3, ROWS, D), F32),
            VMEM((3, 8, D), F32),
            VMEM((ROWS, 128), F32),
            VMEM((ROWS, D), F32),
            VMEM((SMALL_ROWS, SMALL_COLS), F32),
            VMEM((2, 4, 4, 4, *tile), F32),
            VMEM((4, 4, 4, *tile), F32),
            VMEM((4, 4, *tile), F32),
            VMEM((4, *tile), F32),
            VMEM((4, 4, 4, *tile), BF),
            VMEM((4, 4, 4, *tile), BF),
            VMEM((3, 4, 4, *tile), BF),
            VMEM((3, 4, 4, *tile), BF),
            VMEM((3, 4, *tile), BF),
            VMEM((3, 4, *tile), BF),
            VMEM((3, *tile), BF),
            VMEM((3, *tile), BF),
            VMEM((2, 4, 4, 4, *tile), BF),
            dma(()), dma((8,)), dma((4, 3)), dma((4, 3)), dma((4, 3)), dma((4, 3)),
            *GridSum.scratch(512),
        ],
        compiler_params=pltpu.CompilerParams(collective_id=5, has_side_effects=True, vmem_limit_bytes=60 * MIB),
        cost_estimate=pl.CostEstimate(flops=10**9, bytes_accessed=30 * MIB, transcendentals=0),
        name="finish",
    )(history, gs, grad_middle, n, inv, mix, pre, mix_gain[None], mix_first, mix_second, gains, gain_mlp, *packs)


def on_device(
    history, cotangent, lengths, mix_gain, mix_first, mix_second, mix_bias,
    gain_query, gain_key, gain_value, gain_mlp, w_query, w_key, w_value, w_output, w_expand, w_reduce,
):
    gains = jnp.stack([gain_query, gain_key, gain_value])
    row = lax.dynamic_index_in_dim(lengths, lax.axis_index("dp"), 0, keepdims=False)
    places = jnp.arange(2048, dtype=jnp.int32)
    first = jnp.zeros_like(places)
    end = jnp.int32(0)
    for i in range(lengths.shape[1]):
        end = end + row[i]
        first = jnp.where(places >= end, end, first)
    x, n, inv, resid, mix, pre = front(history, mix_gain, mix_first, mix_second, mix_bias, gains)
    heads, rows, w_all, wo_all, we_two = qkv(x, w_query, w_key, w_value, w_output, w_expand)
    q, k, v = [heads[a].reshape(2048, HEAD_DIM) for a in range(3)]
    ctx_rows, middle, reduced, keep_mlp, sib_mlp, g_gain_mlp, grad_middle, grad_low = mlp(
        q, k, v, first[:, None], wo_all, resid, gain_mlp, cotangent, w_expand, we_two, w_reduce)
    output, grads, sum_e, keep_o, sib_o = back(
        q, k, v, first[None], grad_low, wo_all, ctx_rows, reduced, middle, keep_mlp, sib_mlp)
    gs, sum_r, keep_q, sib_q = streams_back(grads, rows, w_all, keep_mlp, sib_mlp)
    grad_history, sum_a, small = finish(
        history, gs, grad_middle, n, inv, mix, pre, mix_gain, mix_first, mix_second, gains, g_gain_mlp,
        keep_q, sib_q, keep_o, sib_o)
    return (
        output, grad_history,
        small[68, :D], small[:MIX, :D].T, small[:MIX, D : D + MIX], small[68, D : D + MIX],
        small[69, :D], small[70, :D], small[71, :D], small[72, :D],
        sum_a[:256, :128], sum_a[:256, 128:], jnp.concatenate([sum_a[256:384, :128], sum_a[256:384, 128:]], 0),
        sum_a[384:], jnp.concatenate([sum_e[:256], sum_e[256:]], 1), sum_r,
    )


def solution(mesh):
    rows, cols, both = P("tensor", None), P(None, "tensor"), ("dp", "tensor")
    return jax.shard_map(
        on_device,
        mesh=mesh,
        in_specs=(P(None, both, None), P(both, None)) + (P(),) * 9 + (cols, cols, cols, rows, cols, rows),
        out_specs=(P(both, None), P(None, both, None)) + (P(),) * 8
        + (P("dp", "tensor"),) * 3 + (P("tensor", "dp"), P("dp", "tensor"), P("tensor", "dp")),
        check_vma=False,
    )
```

```python
import functools

import jax
import jax.numpy as jnp
from jax import lax
from jax.experimental import pallas as pl
from jax.experimental.pallas import tpu as pltpu
from jax.sharding import PartitionSpec as P

HEAD_DIM = 128
HISTORY = 17
STREAMS = 4
MIX = HISTORY * STREAMS
D = 2048
ROWS = 128
FF_SHARD = 512
NORM_EPS = 1e-06
MASKED = -1e30
PRECISE = lax.Precision.HIGHEST
MESH = pl.DeviceIdType.MESH
BF = jnp.bfloat16
F32 = jnp.float32
VMEM = pltpu.VMEM
ANY = pl.ANY
MIB = 2**20

Y1, Y2, Y3 = 2, 4, 6
SIB, XN, DIAG = 1, 8, 9
A_MASKS = (0, SIB, XN, DIAG)
LO, HI = pl.ds(0, 64), pl.ds(64, 64)


def flip(value, mask):
    for bit in (1, 2, 4, 8):
        if mask & bit:
            value = value + bit - 2 * bit * lax.rem(lax.div(value, bit), 2)
    return value


def dev(t_mask, dp_mask=0):
    return (flip(lax.axis_index("dp"), dp_mask), flip(lax.axis_index("tensor"), t_mask))


def enter(partners):
    barrier = pltpu.get_barrier_semaphore()
    for partner in partners:
        pl.semaphore_signal(barrier, inc=1, device_id=dev(*partner), device_id_type=MESH)
    pl.semaphore_wait(barrier, len(partners))


def rcopy(src, dst, send, recv, target):
    return pltpu.make_async_remote_copy(
        src_ref=src, dst_ref=dst, send_sem=send, recv_sem=recv, device_id=dev(*target), device_id_type=MESH
    )


def nt(a, b):
    return lax.dot_general(a, b, (((1,), (1,)), ((), ())), preferred_element_type=F32)


def tn(a, b):
    return lax.dot_general(a, b, (((0,), (0,)), ((), ())), preferred_element_type=F32)


def nn(a, b):
    return jnp.dot(a, b, preferred_element_type=F32)


class Gather:
    def __init__(self, own, rows, send, recv, slots=(0, 1, 2, 3)):
        def c(i, src, dst, target):
            return rcopy(src, dst, send.at[i], recv.at[i], (target,))

        _, one, two, three = slots
        self.copies = [
            c(0, own.at[LO], rows.at[one, LO], Y1),
            c(1, own.at[HI], rows.at[three, HI], Y3),
            c(2, own.at[HI], rows.at[one, HI], Y1),
            c(3, own.at[LO], rows.at[three, LO], Y3),
            c(4, rows.at[one, LO], rows.at[two, LO], Y3),
            c(5, rows.at[three, HI], rows.at[two, HI], Y1),
        ]

    def start(self):
        for i in range(4):
            self.copies[i].start()

    def forward(self):
        self.copies[0].wait_recv()
        self.copies[4].start()
        self.copies[1].wait_recv()
        self.copies[5].start()

    def arrived(self, slot):
        for i in {1: (2,), 3: (3,), 2: (4, 5)}[slot]:
            self.copies[i].wait_recv()

    def finish(self):
        for c in self.copies:
            c.wait_send()


def gelu_parts(x):
    cdf = 0.5 * (1.0 + lax.erf(x * (0.5**0.5)))
    return x * cdf, cdf + x * jnp.exp(-0.5 * x * x) * 0.3989422804014327


STEP = 16
WIDE = 256


def mix_tokens(last, mix_gain, mix_first, mix_second, mix_bias, pre_out, mix_out):
    inverse = lax.rsqrt(jnp.mean(last * last, axis=-1, keepdims=True) + NORM_EPS)
    pre = lax.dot_general(
        last * inverse * mix_gain[...], mix_first[...], (((1,), (1,)), ((), ())),
        precision=PRECISE, preferred_element_type=F32,
    )
    pre_out[...] = pre
    hidden = gelu_parts(pre)[0]
    mix_out[...] = jnp.dot(hidden, mix_second[...], precision=PRECISE, preferred_element_type=F32) + mix_bias[...]


def halves(value):
    high = value.astype(BF)
    return high, (value - high.astype(F32)).astype(BF)


def make_streams(at, hist, mix, gains, held, x_out, n_out, inv_out, resid_out):
    here = mix[at]
    lane = lax.broadcasted_iota(jnp.int32, (STEP, 128), 1)
    own = lax.rem(lane, STEP) == lax.broadcasted_iota(jnp.int32, (STEP, 128), 0)
    entry = lax.div(lane, STEP)
    high, low = [], []
    for k in range(STREAMS):
        pieces = []
        for part in range(2):
            piece = jnp.zeros((STEP, 128), F32)
            for j in range(8):
                i = k * HISTORY + part * 8 + j
                piece = jnp.where(entry == j, here[:, i : i + 1], piece)
            pieces.append(jnp.where(own, piece, 0.0))
        h, m = halves(jnp.concatenate(pieces, axis=1))
        high.append(h)
        low.append(m)
    left = jnp.concatenate(high + low, axis=0)
    squares = [jnp.zeros((STEP, 1), F32) for _ in range(3)]
    for c in range(D // 512):
        cols = slice(c * 512, (c + 1) * 512)
        product = nn(left, hist[0 : HISTORY - 1, at, cols].reshape(256, 512))
        newest = hist[HISTORY - 1, at, cols].astype(F32)
        for k in range(STREAMS):
            i = k * HISTORY + HISTORY - 1
            value = product[k * STEP : (k + 1) * STEP] + product[(4 + k) * STEP : (5 + k) * STEP]
            value = value + here[:, i : i + 1] * newest
            if k == 3:
                resid_out[at, cols] = value
            else:
                held[k, :, cols] = value
                squares[k] = squares[k] + jnp.sum(value * value, axis=-1, keepdims=True)
    for k in range(3):
        inverse = lax.rsqrt(squares[k] * (1.0 / D) + NORM_EPS)
        inv_out[k, at] = jnp.broadcast_to(inverse, (STEP, 128))
        normal = held[k] * inverse
        n_out[k, at] = normal.astype(BF)
        x_out[k, at] = (normal * gains[k][...]).astype(BF)


def qkv_kernel(
    hist_in, cot, mix_gain, mix_first, mix_second, mix_bias, gain_q, gain_k, gain_v,
    w_query, w_key, w_value, w_output, w_expand,
    heads, rows_out, w_out, wo_all, we_two, cot_all, n_out, inv_out, resid_out, mix, pre,
    hist, held, x, rows, weights, proj, hist_sem, cot_send, cot_recv, g_send, g_recv, w_send, w_recv, f_send, f_recv, h_send, h_recv, local,
):
    tiles = ROWS // STEP
    latest = pltpu.make_async_copy(hist_in.at[HISTORY - 1], hist.at[HISTORY - 1], hist_sem.at[tiles])
    latest.start()
    older = pl.ds(0, HISTORY - 1)

    def tile_load(tile):
        at = pl.ds(pl.multiple_of(tile * STEP, STEP), STEP)
        return pltpu.make_async_copy(hist_in.at[older, at], hist.at[older, at], hist_sem.at[tile])

    for tile in range(tiles):
        tile_load(tile).start()
    enter([(Y1,), (Y3,), (SIB,), (XN,), (XN, 4), (DIAG,)])
    t = lax.axis_index("tensor")
    left = pl.ds(0, D // 2)
    cot_gather = Gather(cot.at[:, left], cot_all, cot_send, cot_recv, (0, 1, 3, 2))
    cot_gather.start()
    cot_keep = pltpu.make_async_copy(cot.at[:, left], cot_all.at[0], hist_sem.at[tiles + 1])
    cot_keep.start()
    sources = [w_query, w_key, w_value, w_output, w_expand]
    slots = [lambda r, i=i: weights.at[i, r] for i in range(3)]
    slots += [lambda r: wo_all.at[r], lambda r: we_two.at[r - 1]]
    to_sib, to_x, onward = [], [], []
    for i, src in enumerate(sources):
        half = src.shape[0] // 2
        lo, hi = pl.ds(0, half), pl.ds(half, half)
        to_x.append(
            (
                rcopy(src.at[lo], slots[i](2).at[lo], w_send.at[i, 0], w_recv.at[i, 0], (XN,)),
                rcopy(src.at[hi], slots[i](2).at[hi], w_send.at[i, 1], w_recv.at[i, 1], (XN, 4)),
            )
        )
        to_sib.append(rcopy(src, slots[i](1), w_send.at[i, 2], w_recv.at[i, 2], (SIB,)))
        if i < 4:
            onward.append(rcopy(slots[i](2), slots[i](3), f_send.at[i], f_recv.at[i], (SIB,)))
    keep = [pltpu.make_async_copy(sources[i], slots[i](0), local.at[i]) for i in range(4)]
    gathers = [Gather(x.at[a], rows.at[a], g_send.at[a], g_recv.at[a]) for a in range(3)]
    for a in range(3):
        to_x[a][0].start()
        to_x[a][1].start()
        to_sib[a].start()
        keep[a].start()
    latest.wait()
    mix_tokens(hist[HISTORY - 1].astype(F32), mix_gain, mix_first, mix_second, mix_bias, pre, mix)

    @pl.loop(0, tiles)
    def _(tile):
        tile_load(tile).wait()
        at = pl.ds(pl.multiple_of(tile * STEP, STEP), STEP)
        make_streams(at, hist, mix, (gain_q, gain_k, gain_v), held, x, n_out, inv_out, resid_out)

    cot_gather.forward()
    for a in range(3):
        gathers[a].start()
    for i in (3, 4):
        to_x[i][0].start()
        to_x[i][1].start()
        to_sib[i].start()
    keep[3].start()
    for a in range(3):
        for c in to_x[a]:
            c.wait_recv()
        onward[a].start()
        gathers[a].forward()
    sends = []

    def project(a, s):
        block = x[a] if s == 0 else rows[a, s]
        for p in range(2):
            pair = jnp.concatenate([weights[a, 2 * p], weights[a, 2 * p + 1]], axis=1)
            y = nn(block, pair).astype(BF)
            proj[a, s, 2 * p] = y[:, :128]
            proj[a, s, 2 * p + 1] = y[:, 128:]
        place = flip(t, 2 * s)
        for r in range(4):
            src, dst = proj.at[a, s, r], heads.at[a, place]
            if r == 0:
                c = pltpu.make_async_copy(src, dst, h_send.at[a, s, 0])
            else:
                c = rcopy(src, dst, h_send.at[a, s, r], h_recv.at[a, s, r], (A_MASKS[r],))
            c.start()
            sends.append((r, c))

    for a in range(3):
        keep[a].wait()
        to_sib[a].wait_recv()
        onward[a].wait_recv()
        project(a, 0)
    store = []
    for a in range(3):
        c = pltpu.make_async_copy(weights.at[a], w_out.at[a], local.at[4 + a])
        c.start()
        store.append(c)
        c = pltpu.make_async_copy(x.at[a], rows_out.at[a, 0], local.at[7 + a])
        c.start()
        store.append(c)
    for a in range(3):
        for s in (1, 3):
            gathers[a].arrived(s)
            project(a, s)
    for c in to_x[3]:
        c.wait_recv()
    onward[3].start()
    for a in range(3):
        gathers[a].arrived(2)
        project(a, 2)
        c = pltpu.make_async_copy(rows.at[a, pl.ds(1, 3)], rows_out.at[a, pl.ds(1, 3)], local.at[10 + a])
        c.start()
        store.append(c)
    for s in (1, 3, 2):
        cot_gather.arrived(s)
    cot_keep.wait()
    for g in gathers + [cot_gather]:
        g.finish()
    for r, c in sends:
        if r == 0:
            c.wait()
        else:
            c.wait_send()
    for r, c in sends:
        if r:
            c.wait_recv()
    for i in range(5):
        for c in to_x[i]:
            c.wait_send()
            if i > 3:
                c.wait_recv()
        to_sib[i].wait_send()
        if i > 2:
            to_sib[i].wait_recv()
    for i in range(4):
        onward[i].wait_send()
    onward[3].wait_recv()
    keep[3].wait()
    for c in store:
        c.wait()


def qkv(history, cot, mix_gain, mix_first, mix_second, mix_bias, gains, *weights):
    dma = pltpu.SemaphoreType.DMA
    vm, hbm = pl.BlockSpec(memory_space=VMEM), pl.BlockSpec(memory_space=ANY)
    return pl.pallas_call(
        qkv_kernel,
        in_specs=[hbm] * 2 + [vm] * 7 + [hbm] * 5,
        out_specs=[hbm] * 6 + [vm] * 5,
        out_shape=[
            jax.ShapeDtypeStruct((3, 16, ROWS, HEAD_DIM), BF),
            jax.ShapeDtypeStruct((3, 4, ROWS, D), BF),
            jax.ShapeDtypeStruct((3, 4, D, HEAD_DIM), BF),
            jax.ShapeDtypeStruct((4, HEAD_DIM, D), BF),
            jax.ShapeDtypeStruct((2, D, FF_SHARD), BF),
            jax.ShapeDtypeStruct((4, ROWS, D // 2), BF),
            jax.ShapeDtypeStruct((3, ROWS, D), BF),
            jax.ShapeDtypeStruct((3, ROWS, 128), F32),
            jax.ShapeDtypeStruct((ROWS, D), F32),
            jax.ShapeDtypeStruct((ROWS, MIX), F32),
            jax.ShapeDtypeStruct((ROWS, MIX), F32),
        ],
        scratch_shapes=[
            VMEM((HISTORY, ROWS, D), BF),
            VMEM((3, STEP, D), F32),
            VMEM((3, ROWS, D), BF),
            VMEM((3, 4, ROWS, D), BF),
            VMEM((3, 4, D, HEAD_DIM), BF),
            VMEM((3, 4, 4, ROWS, HEAD_DIM), BF),
            dma((ROWS // STEP + 2,)), dma((6,)), dma((6,)),
            dma((3, 6)), dma((3, 6)), dma((5, 3)), dma((5, 3)), dma((4,)), dma((4,)), dma((3, 4, 4)), dma((3, 4, 4)), dma((13,)),
        ],
        compiler_params=pltpu.CompilerParams(collective_id=1, has_side_effects=True, vmem_limit_bytes=61 * MIB),
        cost_estimate=pl.CostEstimate(flops=6 * 512 * 2048 * 512, bytes_accessed=30 * MIB, transcendentals=0),
        name="qkv",
    )(
        history, cot, mix_gain[None], mix_first.T, mix_second, mix_bias[None], *[g[None] for g in gains], *weights
    )


def first_places(lengths, places):
    group = lax.axis_index("dp")
    first, end = jnp.zeros_like(places), jnp.int32(0)
    for i in range(lengths.shape[1]):
        end = end + lengths[group, i]
        first = jnp.where(places >= end, end, first)
    return first


def attend_kernel(q, k, v, lengths, ctx):
    tokens, step = q.shape[0], 256
    scale = HEAD_DIM ** (-0.5)
    for i in range(tokens // step):
        length = (i + 1) * step
        at = slice(i * step, length)
        scores = nt(q[at], k[:length]) * scale
        key_place = lax.broadcasted_iota(jnp.int32, (step, length), 1)
        query_place = lax.broadcasted_iota(jnp.int32, (step, 1), 0) + i * step
        allowed = (key_place >= first_places(lengths, query_place)) & (key_place <= query_place)
        scores = jnp.where(allowed, scores, MASKED)
        top = jnp.max(scores, axis=-1, keepdims=True)
        e = jnp.exp(scores - top)
        low = (e * (1.0 / jnp.sum(e, axis=-1, keepdims=True))).astype(BF)
        ctx[at] = nn(low, v[:length]).astype(BF)


def attend_back_kernel(q, k, v, gc, lengths, dq, dk, dv, dk_sum, dv_sum, hooks):
    tokens, step = q.shape[0], 256
    scale = HEAD_DIM ** (-0.5)
    k_turned = k[...].astype(F32).T.astype(BF)
    for i in range(tokens // step):
        if i in hooks:
            hooks[i]()
        length = (i + 1) * step
        at = slice(i * step, length)
        scores = nt(k[:length], q[at]) * scale
        key_place = lax.broadcasted_iota(jnp.int32, (length, step), 0)
        query_place = lax.broadcasted_iota(jnp.int32, (1, step), 1) + i * step
        allowed = (key_place >= first_places(lengths, query_place)) & (key_place <= query_place)
        scores = jnp.where(allowed, scores, MASKED)
        top = jnp.max(scores, axis=0, keepdims=True)
        e = jnp.exp(scores - top)
        probs = e * (1.0 / jnp.sum(e, axis=0, keepdims=True))
        grad_probs = nt(v[:length], gc[at])
        delta = jnp.sum(grad_probs * probs, axis=0, keepdims=True)
        grad_scores = (probs * (grad_probs - delta)).astype(BF)
        low = probs.astype(BF)
        dq[at] = (nn(k_turned[:, :length], grad_scores) * scale).T.astype(BF)
        key_part = nn(grad_scores, q[at])
        value_part = nn(low, gc[at])
        if i:
            dk_sum[: i * step] += key_part[: i * step]
            dv_sum[: i * step] += value_part[: i * step]
        dk_sum[at] = key_part[i * step :]
        dv_sum[at] = value_part[i * step :]
    dk[...] = (dk_sum[...] * scale).astype(BF)
    dv[...] = dv_sum[...].astype(BF)


def mlp_kernel(
    heads, lengths, wo_all, resid, gain, cot, cot_all, w_expand, we_two, w_reduce,
    ctx_rows, middle_out, reduced_out, keep_out, grad_gain, grad_middle, grad_low,
    ctx, we, wr, mlp_rows, cot_rows, act, gexp, parts, stage, sc_out, sc_pass, sc_got,
    mlp_sib, cot_sib, act_sib, gexp_sib, act_turned,
    g_send, g_recv, s_send, s_recv, w_send, w_recv, c_send, c_recv, d_send, d_recv, local, keep_sem, cot_send, cot_recv,
):
    enter([(Y1,), (Y3,), (SIB,), (XN,), (XN, 4), (DIAG,)])
    t = lax.axis_index("tensor")
    q, k, v = heads.at[0], heads.at[1], heads.at[2]
    slots = (0, 1, 3, 2)
    right = pl.ds(D // 2, D // 2)
    cot_gather = Gather(cot.at[:, right], cot_rows.at[:, :, right], cot_send, cot_recv, slots)
    cot_gather.start()
    half = FF_SHARD // 2
    lo, hi = pl.ds(0, half), pl.ds(half, half)
    loads = [
        pltpu.make_async_copy(w_expand, we.at[0], local.at[0]),
        pltpu.make_async_copy(we_two, we.at[pl.ds(1, 2)], local.at[1]),
        pltpu.make_async_copy(w_reduce, wr.at[0], local.at[2]),
        pltpu.make_async_copy(cot_all, cot_rows.at[:, :, pl.ds(0, D // 2)], local.at[3]),
        pltpu.make_async_copy(cot.at[:, right], cot_rows.at[0, :, right], local.at[4]),
    ]
    for c in loads:
        c.start()
    sib = [
        rcopy(we_two.at[1], we.at[3], w_send.at[0], w_recv.at[0], (SIB,)),
        rcopy(w_reduce, wr.at[1], w_send.at[1], w_recv.at[1], (SIB,)),
        rcopy(wr.at[2], wr.at[3], w_send.at[2], w_recv.at[2], (SIB,)),
    ]
    across = [
        rcopy(w_reduce.at[lo], wr.at[2, lo], w_send.at[3], w_recv.at[3], (XN,)),
        rcopy(w_reduce.at[hi], wr.at[2, hi], w_send.at[4], w_recv.at[4], (XN, 4)),
    ]
    sib[0].start()
    sib[1].start()
    attend_kernel(q, k, v, lengths, ctx)
    cot_gather.forward()
    back = {}
    for s in (2, 1, 3, 0):
        for r in range(4):
            place = pl.multiple_of(flip(t, A_MASKS[r] + 2 * s) * ROWS, ROWS)
            src, dst = ctx.at[pl.ds(place, ROWS)], ctx_rows.at[s, r]
            if r:
                back[s, r] = rcopy(src, dst, c_send.at[s, r], c_recv.at[s, r], (A_MASKS[r],))
            else:
                back[s, r] = pltpu.make_async_copy(src, dst, c_send.at[s, r])
            back[s, r].start()
    for c in across:
        c.start()

    def rows_of(s):
        for r in range(4):
            back[s, r].wait_recv() if r else back[s, r].wait()
        return jnp.concatenate([ctx_rows[s, r] for r in range(4)], axis=1)

    weight = wo_all[...].reshape(4 * HEAD_DIM, D)

    def ring(index):
        return Ring(
            lambda s, half: parts[{1: 0, 3: 1, 0: 2, 2: 3}[s], half],
            sc_out, sc_pass, sc_got, s_send.at[index], s_recv.at[index], (Y1,), (Y3,), ROWS,
        )

    ring1 = ring(0)
    parts[3] = nn(rows_of(2), weight)
    ring1.opposite()
    three = jnp.concatenate([rows_of(1), rows_of(3), rows_of(0)], axis=0)
    parts[0:3] = nn(three, weight).reshape(3, ROWS, D)
    ring1.neighbours()
    ring1.relay()
    for c in across:
        c.wait_recv()
    sib[2].start()
    for c in loads:
        c.wait()
    ring1.arrive()
    middle = resid[...] + ring1.total(pl.ds(0, ROWS))
    middle_out[...] = middle
    inverse = lax.rsqrt(jnp.mean(middle * middle, axis=-1, keepdims=True) + NORM_EPS)
    mlp_rows[0] = (middle * inverse * gain[...]).astype(BF)
    mlp_gather = Gather(mlp_rows.at[0], mlp_rows, g_send, g_recv, slots)
    mlp_gather.start()
    for s in (1, 3, 2):
        cot_gather.arrived(s)
    shares = [
        rcopy(cot_rows, cot_sib, d_send.at[0], d_recv.at[0], (SIB,)),
        rcopy(mlp_rows, mlp_sib, d_send.at[1], d_recv.at[1], (SIB,)),
    ]
    shares[0].start()
    for c in sib:
        c.wait_recv()

    def block(start, count):
        at, m = pl.ds(start, count), count * ROWS

        @pl.loop(0, 4)
        def _(r):
            expanded = nn(mlp_rows[at].reshape(m, D), we[r])
            grad_active = nt(cot_rows[at].reshape(m, D), wr[r])
            value, slope = gelu_parts(expanded)
            act[r, at] = value.astype(BF).reshape(count, ROWS, FF_SHARD)
            gexp[r, at] = (grad_active * slope).astype(BF).reshape(count, ROWS, FF_SHARD)

    block(0, 1)
    mlp_gather.forward()
    for s in (1, 3):
        mlp_gather.arrived(s)
    block(1, 2)
    mlp_gather.arrived(2)
    shares[1].start()
    block(3, 1)
    for n, r in enumerate((1, 3)):
        shares.append(rcopy(act.at[r], act_sib.at[n], d_send.at[2 + n], d_recv.at[2 + n], (SIB,)))
        shares.append(rcopy(gexp.at[r], gexp_sib.at[n], d_send.at[4 + n], d_recv.at[4 + n], (SIB,)))
    for c in shares[2:]:
        c.start()

    def grad_mlp(start, count):
        at, m = pl.ds(start, count), count * ROWS
        parts[at] = jnp.zeros((count, ROWS, D), F32)

        @pl.loop(0, 4)
        def _(r):
            parts[at] += nt(gexp[r, at].reshape(m, FF_SHARD), we[r]).reshape(count, ROWS, D)

    ring1.finish()
    ring2 = ring(1)
    grad_mlp(3, 1)
    ring2.opposite()
    parts[0:3] = jnp.zeros((3, ROWS, D), F32)

    @pl.loop(0, 4)
    def _(r):
        lhs = jnp.concatenate([gexp[r, 1], gexp[r, 2], gexp[r, 0]], axis=0)
        parts[0:3] += nt(lhs, we[r]).reshape(3, ROWS, D)

    ring2.neighbours()
    ring2.relay()
    for s in range(4):
        reduced = nn(act[0, s], wr[0])
        for r in range(1, 4):
            reduced += nn(act[r, s], wr[r])
        reduced_out[(0, 1, 3, 2)[s]] = reduced.astype(BF)
    for c in shares:
        c.wait_recv()
    @pl.loop(0, 8)
    def _(d):
        cols = pl.ds(pl.multiple_of(d * 256, 256), 256)
        own, other = mlp_rows[:, :, cols].reshape(512, 256).T, mlp_sib[:, :, cols].reshape(512, 256).T
        for n, r in enumerate((0, 2)):
            grad_e = nn(own, gexp[r].reshape(512, FF_SHARD)) + nn(other, gexp_sib[n].reshape(512, FF_SHARD))
            for c in range(2):
                stage[n, d, c * 256 : (c + 1) * 256] = grad_e[:, c * 256 : (c + 1) * 256].astype(BF)

    for n, r in enumerate((0, 2)):
        act_turned[n] = jnp.concatenate([act[r].reshape(512, FF_SHARD), act_sib[n].reshape(512, FF_SHARD)], axis=0).T

    @pl.loop(0, 8)
    def _(d):
        cols = pl.ds(pl.multiple_of(d * 256, 256), 256)
        rhs = jnp.concatenate([cot_rows[:, :, cols].reshape(512, 256), cot_sib[:, :, cols].reshape(512, 256)], axis=0)
        for n in range(2):
            stage[n, d, 512:1024] = nn(act_turned[n], rhs).astype(BF)

    keeps = [pltpu.make_async_copy(stage, keep_out, keep_sem)]
    keeps[0].start()
    ring2.arrive()
    got = ring2.total(pl.ds(0, ROWS))
    middle = middle_out[...]
    inverse = lax.rsqrt(jnp.mean(middle * middle, axis=-1, keepdims=True) + NORM_EPS)
    normal = middle * inverse
    grad_gain[...] = jnp.sum(got * normal, axis=0, keepdims=True)
    scaled = got * gain[...]
    grad = cot_rows[0].astype(F32) + inverse * (scaled - normal * jnp.mean(scaled * normal, axis=-1, keepdims=True))
    grad_middle[...] = grad
    grad_low[...] = grad.astype(BF)
    ring2.finish()
    cot_gather.finish()
    mlp_gather.finish()
    for c in sib + across + shares:
        c.wait_send()
    for (s, r), c in back.items():
        if r:
            c.wait_send()
    for c in keeps:
        c.wait()


def mlp(heads, lengths, wo_all, resid, gain_mlp, cot, cot_all, w_expand, we_two, w_reduce):
    dma = pltpu.SemaphoreType.DMA
    vm, hbm, sm = [pl.BlockSpec(memory_space=m) for m in (VMEM, ANY, pltpu.SMEM)]
    return pl.pallas_call(
        mlp_kernel,
        in_specs=[vm, sm] + [vm] * 3 + [hbm] * 5,
        out_specs=[vm, vm, vm, hbm, vm, vm, vm],
        out_shape=[
            jax.ShapeDtypeStruct((4, 4, ROWS, HEAD_DIM), BF),
            jax.ShapeDtypeStruct((ROWS, D), F32),
            jax.ShapeDtypeStruct((4, ROWS, D), BF),
            jax.ShapeDtypeStruct((2, 8, 1024, 256), BF),
            jax.ShapeDtypeStruct((1, D), F32),
            jax.ShapeDtypeStruct((ROWS, D), F32),
            jax.ShapeDtypeStruct((ROWS, D), BF),
        ],
        scratch_shapes=[
            VMEM((2048, HEAD_DIM), BF),
            VMEM((4, D, FF_SHARD), BF),
            VMEM((4, FF_SHARD, D), BF),
            VMEM((4, ROWS, D), BF),
            VMEM((4, ROWS, D), BF),
            VMEM((4, 4, ROWS, FF_SHARD), BF),
            VMEM((4, 4, ROWS, FF_SHARD), BF),
            VMEM((4, ROWS, D), F32),
            VMEM((2, 8, 1024, 256), BF),
            VMEM((3, ROWS, D), BF),
            VMEM((ROWS, D), BF),
            VMEM((2, ROWS, D), BF),
            VMEM((4, ROWS, D), BF),
            VMEM((4, ROWS, D), BF),
            VMEM((2, 4, ROWS, FF_SHARD), BF),
            VMEM((2, 4, ROWS, FF_SHARD), BF),
            VMEM((2, FF_SHARD, 1024), BF),
            dma((6,)), dma((6,)), dma((2, 6)), dma((2, 6)), dma((5,)), dma((5,)), dma((4, 4)), dma((4, 4)),
            dma((6,)), dma((6,)), dma((5,)), dma(()), dma((6,)), dma((6,)),
        ],
        compiler_params=pltpu.CompilerParams(collective_id=2, has_side_effects=True, vmem_limit_bytes=61 * MIB),
        cost_estimate=pl.CostEstimate(flops=30 * 10**9, bytes_accessed=50 * MIB, transcendentals=0),
        name="mlp",
    )(heads, lengths, wo_all, resid, gain_mlp[None], cot, cot_all, w_expand, we_two, w_reduce)


class Ring:
    def __init__(self, part, out, passed, got, send, recv, near, far, size):
        half = size // 2
        lo, hi = pl.ds(0, half), pl.ds(half, half)

        def c(i, src, dst, target):
            return rcopy(src, dst, send.at[i], recv.at[i], target)

        self.part, self.out, self.passed, self.got, self.lo, self.hi = part, out, passed, got, lo, hi
        self.copies = [
            c(0, out.at[0, lo], passed.at[lo], near),
            c(1, out.at[0, hi], passed.at[hi], far),
            c(2, out.at[1, lo], got.at[0, lo], near),
            c(3, out.at[2, hi], got.at[1, hi], far),
            c(4, out.at[2, lo], got.at[1, lo], far),
            c(5, out.at[1, hi], got.at[0, hi], near),
        ]

    def opposite(self):
        self.send(0, self.lo, self.part(2, self.lo), 0)
        self.send(0, self.hi, self.part(2, self.hi), 1)

    def neighbours(self):
        self.send(1, self.lo, self.part(1, self.lo), 2)
        self.send(2, self.hi, self.part(3, self.hi), 3)

    def begin(self):
        self.opposite()
        self.neighbours()

    def send(self, slot, half, value, i):
        self.out[slot, half] = value.astype(BF)
        self.copies[i].start()

    def relay(self):
        for i, slot, s, half in ((0, 2, 3, self.lo), (1, 1, 1, self.hi)):
            self.copies[i].wait_recv()
            self.out[slot, half] = (self.part(s, half) + self.passed[half].astype(F32)).astype(BF)
            self.copies[4 + i].start()

    def arrive(self):
        for i in (2, 3, 4, 5):
            self.copies[i].wait_recv()

    def total(self, index):
        return self.part(0, index) + self.got[0, index].astype(F32) + self.got[1, index].astype(F32)

    def finish(self):
        for c in self.copies:
            c.wait_send()


X_RING = ((XN,), (XN, 4))
Z_RING = ((0, 1), (0, 3))


class GridSum:
    @staticmethod
    def scratch(rows, pair=True):
        half, dma = rows // 2, pltpu.SemaphoreType.DMA
        return [
            VMEM((2, 8, rows, 256), BF),
            VMEM((2, 8, rows, 256) if pair else (16, 128), BF),
            VMEM((2, 3, 4, half, 256), BF),
            VMEM((2, 4, half, 256), BF),
            VMEM((2, 2, 4, half, 256), BF),
            VMEM((2, 4, half, 256), F32),
            VMEM((2, 3, half, 256), BF),
            VMEM((2, half, 256), BF),
            VMEM((2, 2, half, 256), BF),
            dma((4, 6)),
            dma((4, 6)),
            dma((4,)),
        ]

    def __init__(self, pieces, scratch):
        (self.a, self.b, out1, pass1, got1, self.mid, out2, pass2, got2, send, recv, load) = scratch
        rows = self.a.shape[2]
        self.half = half = rows // 2
        self.loads, start = [], 0
        for i, (kept, given) in enumerate(pieces):
            at = pl.ds(start, kept.shape[2])
            start += kept.shape[2]
            self.loads.append(pltpu.make_async_copy(kept, self.a.at[:, :, at], load.at[2 * i]))
            if given is not None:
                self.loads.append(pltpu.make_async_copy(given, self.b.at[:, :, at], load.at[2 * i + 1]))
        dp = lax.axis_index("dp")
        place = {(sx, sz): flip(dp, (4 if sx in (2, 3) else 0) + sz) for sx in range(4) for sz in range(4)}

        def block(sx, sz, path):
            shard = 0 if sx in (0, 2) else 1
            at = slice(path * half, (path + 1) * half)
            d = place[sx, sz]
            own = self.a[shard, d, at].astype(F32)
            return own if given is None else own + self.b[shard, d, at].astype(F32)

        def span(ds):
            return range(ds.start, ds.start + ds.size)

        def over_x(s, half_):
            return jnp.stack([block(s, z, 0) for z in span(half_)])

        def over_z(s, half_):
            return jnp.stack([block(x, s, 1) for x in span(half_)])

        rings = (X_RING, Z_RING)
        self.first, self.second = [], []
        for path, part in enumerate((over_x, over_z)):
            near, far = rings[path]
            self.first.append(
                Ring(part, out1.at[path], pass1.at[path], got1.at[path], send.at[path], recv.at[path], near, far, 4)
            )
            near, far = rings[1 - path]
            mid = self.mid.at[path]

            def later(s, half_, mid=mid):
                return mid[s, half_]

            self.second.append(
                Ring(
                    later, out2.at[path], pass2.at[path], got2.at[path], send.at[2 + path], recv.at[2 + path], near, far, half
                )
            )

    def load(self):
        for c in self.loads:
            c.start()

    def begin(self):
        for c in self.loads:
            c.wait()
        for ring in self.first:
            ring.begin()

    def relay(self):
        for ring in self.first:
            ring.relay()

    def turn(self):
        for path in range(2):
            ring = self.first[path]
            ring.arrive()
            for s in (2, 1, 3, 0):
                self.mid[path, s] = ring.total(pl.ds(s, 1))[0]
            self.second[path].begin()

    def relay2(self):
        for ring in self.second:
            ring.relay()

    def result(self):
        parts = []
        for ring in self.second:
            ring.arrive()
            parts.append(ring.total(pl.ds(0, self.half)))
        return jnp.concatenate(parts, axis=0)

    def finish(self):
        for ring in self.first + self.second:
            ring.finish()


def back_kernel(
    heads, lengths, grad_low, wo_all, ctx_rows, reduced, middle, keep_in,
    output, grads, summed, keep_out, sib_out,
    rows, proj, gc, dk_sum, dv_sum, stage, sc_out, sc_pass, sc_got,
    g_send, g_recv, s_send, s_recv, c_send, c_recv, d_send, d_recv, *grid_scratch,
):
    enter([(Y1,), (Y3,), (SIB,), (DIAG,), *X_RING, *Z_RING])
    t = lax.axis_index("tensor")
    gather = Gather(grad_low, rows, g_send, g_recv)
    gather.start()
    part = pl.ds(0, 512)
    grid = GridSum([(keep_in.at[:, :, part], None)], grid_scratch)
    grid.load()
    q, k, v = heads.at[0], heads.at[1], heads.at[2]
    ring = Ring(
        lambda s, half: reduced[s, half].astype(F32), sc_out, sc_pass, sc_got, s_send, s_recv, (Y1,), (Y3,), ROWS
    )
    rows[0] = grad_low[...]
    weight = wo_all[...].reshape(4 * HEAD_DIM, D)
    moves = []

    def project(s):
        y = nt(rows[s], weight).astype(BF)
        place = pl.multiple_of(flip(t, 2 * s) * ROWS, ROWS)
        for r in range(4):
            proj[s, r] = y[:, r * HEAD_DIM : (r + 1) * HEAD_DIM]
            src, dst = proj.at[s, r], gc.at[pl.ds(place, ROWS)]
            if r:
                c = rcopy(src, dst, c_send.at[s, r], c_recv.at[s, r], (A_MASKS[r],))
            else:
                c = pltpu.make_async_copy(src, dst, c_send.at[s, r])
            c.start()
            moves.append((r, c))

    project(0)
    gather.forward()
    ring.begin()
    grid.begin()
    for s in (1, 3, 2):
        gather.arrived(s)
        project(s)
    ring.relay()
    grid.relay()
    all_rows = rows[...].reshape(4 * ROWS, D)
    sends = []
    for n, r in enumerate((1, 3, 0, 2)):
        lhs = jnp.concatenate([ctx_rows[s, r] for s in range(4)], axis=0)
        grad_o = tn(lhs, all_rows).astype(BF)
        for d in range(8):
            stage[n, d] = grad_o[:, d * 256 : (d + 1) * 256]
        if n < 2:
            c = rcopy(stage.at[n], sib_out.at[n], d_send.at[n], d_recv.at[n], (SIB,))
        else:
            c = pltpu.make_async_copy(stage.at[n], keep_out.at[n - 2], d_send.at[n])
        c.start()
        sends.append(c)
    for r, c in moves:
        c.wait_recv() if r else c.wait()
    hooks = {4: grid.turn, 7: grid.relay2}
    attend_back_kernel(q, k, v, gc, lengths, grads.at[0], grads.at[1], grads.at[2], dk_sum, dv_sum, hooks)
    summed[...] = grid.result()
    grid.finish()
    ring.arrive()
    output[...] = (middle[...] + ring.total(pl.ds(0, ROWS))).astype(BF)
    gather.finish()
    ring.finish()
    for r, c in moves:
        if r:
            c.wait_send()
    for n, c in enumerate(sends):
        c.wait()


def back(heads, lengths, grad_low, wo_all, ctx_rows, reduced, middle, keep):
    dma = pltpu.SemaphoreType.DMA
    vm, hbm, sm = [pl.BlockSpec(memory_space=m) for m in (VMEM, ANY, pltpu.SMEM)]
    return pl.pallas_call(
        back_kernel,
        in_specs=[vm, sm] + [vm] * 5 + [hbm],
        out_specs=[vm, vm, vm, hbm, hbm],
        out_shape=[
            jax.ShapeDtypeStruct((ROWS, D), BF),
            jax.ShapeDtypeStruct((3, 2048, HEAD_DIM), BF),
            jax.ShapeDtypeStruct((512, 256), F32),
            jax.ShapeDtypeStruct((2, 8, ROWS, 256), BF),
            jax.ShapeDtypeStruct((2, 8, ROWS, 256), BF),
        ],
        scratch_shapes=[
            VMEM((4, ROWS, D), BF),
            VMEM((4, 4, ROWS, HEAD_DIM), BF),
            VMEM((2048, HEAD_DIM), BF),
            VMEM((2048, HEAD_DIM), F32),
            VMEM((2048, HEAD_DIM), F32),
            VMEM((4, 8, ROWS, 256), BF),
            VMEM((3, ROWS, D), BF),
            VMEM((ROWS, D), BF),
            VMEM((2, ROWS, D), BF),
            dma((6,)), dma((6,)), dma((6,)), dma((6,)), dma((4, 4)), dma((4, 4)), dma((4,)), dma((4,)),
            *GridSum.scratch(512, False),
        ],
        compiler_params=pltpu.CompilerParams(collective_id=3, has_side_effects=True, vmem_limit_bytes=61 * MIB),
        cost_estimate=pl.CostEstimate(flops=8 * 10**9, bytes_accessed=20 * MIB, transcendentals=0),
        name="back",
    )(heads, lengths, grad_low, wo_all, ctx_rows, reduced, middle, keep)


def streams_kernel(
    grads, rows_in, w_in, keep_in, hist_in, grad_middle, n_in, inv, gain_q, gain_k, gain_v,
    ds, mixed, newest, sums, summed, keep_out, sib_out,
    hist, hist_sem, rows, weights, g, turned, parts, stage, sc_out, sc_pass, sc_got,
    s_send, s_recv, c_send, c_recv, d_send, d_recv, local, *grid_scratch,
):
    enter([(Y1,), (Y3,), (SIB,), (DIAG,), *X_RING, *Z_RING])
    t = lax.axis_index("tensor")
    part = pl.ds(512, 512)
    grid = GridSum([(keep_in.at[:, :, part], None)], grid_scratch)
    moves = {}
    for a in range(3):
        for s in (2, 1, 3, 0):
            for r in range(4):
                place = pl.multiple_of(flip(t, A_MASKS[r] + 2 * s) * ROWS, ROWS)
                src, dst = grads.at[a, pl.ds(place, ROWS)], g.at[a, s, r]
                if r:
                    c = rcopy(src, dst, c_send.at[a, s, r], c_recv.at[a, s, r], (A_MASKS[r],))
                else:
                    c = pltpu.make_async_copy(src, dst, c_send.at[a, s, r])
                c.start()
                moves[a, s, r] = c
    gains = (gain_q, gain_k, gain_v)
    tiles = ROWS // STEP
    lane = lax.broadcasted_iota(jnp.int32, (STEP, 256), 1)
    own = lax.rem(lane, STEP) == lax.broadcasted_iota(jnp.int32, (STEP, 256), 0)
    column = lax.broadcasted_iota(jnp.int32, (STEP, 128), 1)
    newest[...] = jnp.zeros(newest.shape, F32)

    def tile_load(tile):
        at = pl.ds(pl.multiple_of(tile * STEP, STEP), STEP)
        slot = lax.rem(tile, 2)
        return pltpu.make_async_copy(hist_in.at[:, at], hist.at[slot], hist_sem.at[slot])

    def rows_of_mixing(streams):
        tile_load(jnp.int32(0)).start()

        def step(tile, totals):
            at = pl.ds(pl.multiple_of(tile * STEP, STEP), STEP)

            @pl.when(tile < tiles - 1)
            def _():
                tile_load(tile + 1).start()

            totals, values = list(totals), []
            for i, k in enumerate(streams):
                if k == 3:
                    values.append(grad_middle[at])
                    continue
                grad, normal = rings[k].total(at), n_in[k, at].astype(F32)
                product = grad * normal
                totals[i] = totals[i] + product[:8] + product[8:]
                scaled = grad * gains[k][...]
                mean = jnp.sum(scaled * normal, axis=-1, keepdims=True) * (1.0 / D)
                value = (scaled - normal * mean) * inv[k, at, 0:1]
                ds[k, at] = value
                values.append(value)
            split = [halves(value) for value in values]
            left = jnp.concatenate([h for h, _ in split] + [m for _, m in split], axis=0)
            tile_load(tile).wait()
            slot = lax.rem(tile, 2)
            product = nt(left, hist[slot, 0 : HISTORY - 1].reshape(256, D))
            last = hist[slot, HISTORY - 1].astype(F32)
            count = len(streams)
            for i, k in enumerate(streams):
                both = product[i * STEP : (i + 1) * STEP] + product[(count + i) * STEP : (count + i + 1) * STEP]
                mixed[k, at] = jnp.where(own, both, 0.0)
                newest[at] = jnp.where(column == k, jnp.sum(values[i] * last, axis=-1, keepdims=True), newest[at])
            return tuple(totals)

        totals = lax.fori_loop(0, tiles, step, (jnp.zeros((8, D), F32),) * len(streams))
        for total, k in zip(totals, streams):
            if k < 3:
                sums[k : k + 1] = jnp.sum(total, axis=0, keepdims=True)

    loads = []
    for a in range(3):
        c = pltpu.make_async_copy(w_in.at[a], weights.at[a], local.at[a])
        c.start()
        loads.append(c)
    for a in range(3):
        loads.append(pltpu.make_async_copy(rows_in.at[a], rows, local.at[3 + a]))
    loads[3].start()
    grid.load()
    rings = []
    for a in range(3):
        loads[a].wait()
        weight = jnp.concatenate([weights[a, r] for r in range(4)], axis=1)
        ring = Ring(
            lambda s, half, a=a: parts[a, pl.ds({0: 0, 1: 64, 3: 192}[s] + half.start, half.size)],
            sc_out.at[a], sc_pass.at[a], sc_got.at[a], s_send.at[a], s_recv.at[a], (Y1,), (Y3,), ROWS,
        )
        rings.append(ring)
        for s in (2, 1, 3, 0):
            for r in range(4):
                c = moves[a, s, r]
                c.wait_recv() if r else c.wait()
            lhs = jnp.concatenate([g[a, s, r] for r in range(4)], axis=1)
            value = nt(lhs, weight)
            if s == 0:
                parts[a, 0:128] = value
            elif s == 1:
                ring.send(1, ring.lo, value[:64], 2)
                parts[a, 128:192] = value[64:]
            elif s == 3:
                ring.send(2, ring.hi, value[64:], 3)
                parts[a, 192:256] = value[:64]
            else:
                ring.send(0, ring.lo, value[:64], 0)
                ring.send(0, ring.hi, value[64:], 1)
        if a == 0:
            grid.begin()
    for ring in rings:
        ring.relay()
    grid.relay()
    for a in range(3):
        loads[3 + a].wait()
        turned[...] = rows[...].reshape(512, D).T
        if a < 2:
            loads[4 + a].start()
        grad_w = nn(
            turned[...], jnp.concatenate([g[a, :, r].reshape(512, HEAD_DIM) for r in range(4)], axis=1)
        ).astype(BF)
        for n, r in enumerate((1, 3, 0, 2)):
            for d in range(8):
                block = grad_w[d * 256 : (d + 1) * 256, r * HEAD_DIM : (r + 1) * HEAD_DIM]
                if a < 2:
                    stage[n, d, 0:256, a * 128 : (a + 1) * 128] = block
                else:
                    stage[n, d, 256:384, 0:128] = block[:128]
                    stage[n, d, 256:384, 128:256] = block[128:]
        if a == 0:
            grid.turn()
    grid.relay2()
    sends = []
    for n in range(4):
        if n < 2:
            c = rcopy(stage.at[n], sib_out.at[n], d_send.at[n], d_recv.at[n], (SIB,))
        else:
            c = pltpu.make_async_copy(stage.at[n], keep_out.at[n - 2], d_send.at[n])
        c.start()
        sends.append(c)
    for a, ring in enumerate(rings):
        ring.arrive()
        if a == 2:
            summed[...] = grid.result()
            grid.finish()
        if a != 1:
            rows_of_mixing((0, 3) if a == 0 else (1, 2))
    for ring in rings:
        ring.finish()
    for (a, s, r), c in moves.items():
        if r:
            c.wait_send()
    for c in sends:
        c.wait()


def streams_back(grads, rows, w_all, keep, history, grad_middle, n, inv, gains):
    dma = pltpu.SemaphoreType.DMA
    vm, hbm = pl.BlockSpec(memory_space=VMEM), pl.BlockSpec(memory_space=ANY)
    return pl.pallas_call(
        streams_kernel,
        in_specs=[vm] + [hbm] * 4 + [vm] * 6,
        out_specs=[vm] * 5 + [hbm] * 2,
        out_shape=[
            jax.ShapeDtypeStruct((3, ROWS, D), F32),
            jax.ShapeDtypeStruct((4, ROWS, 256), F32),
            jax.ShapeDtypeStruct((ROWS, 128), F32),
            jax.ShapeDtypeStruct((3, D), F32),
            jax.ShapeDtypeStruct((512, 256), F32),
            jax.ShapeDtypeStruct((2, 8, 384, 256), BF),
            jax.ShapeDtypeStruct((2, 8, 384, 256), BF),
        ],
        scratch_shapes=[
            VMEM((2, HISTORY, STEP, D), BF),
            dma((2,)),
            VMEM((4, ROWS, D), BF),
            VMEM((3, 4, D, HEAD_DIM), BF),
            VMEM((3, 4, 4, ROWS, HEAD_DIM), BF),
            VMEM((D, 512), BF),
            VMEM((3, 256, D), F32),
            VMEM((4, 8, 384, 256), BF),
            VMEM((3, 3, ROWS, D), BF),
            VMEM((3, ROWS, D), BF),
            VMEM((3, 2, ROWS, D), BF),
            dma((3, 6)), dma((3, 6)), dma((3, 4, 4)), dma((3, 4, 4)), dma((4,)), dma((4,)), dma((6,)),
            *GridSum.scratch(512, False),
        ],
        compiler_params=pltpu.CompilerParams(collective_id=4, has_side_effects=True, vmem_limit_bytes=61 * MIB),
        cost_estimate=pl.CostEstimate(flops=8 * 10**9, bytes_accessed=20 * MIB, transcendentals=0),
        name="streams_back",
    )(grads, rows, w_all, keep, history, grad_middle, n, inv, *[x[None] for x in gains])


SMALL_ROWS, SMALL_COLS = 80, D + 128
RING_OF = {
    "y": ((Y1, 0), (Y2, 0), (Y3, 0)),
    "x": ((XN, 0), (0, 4), (XN, 4)),
    "z": ((0, 1), (0, 2), (0, 3)),
}


def finish_kernel(
    hist_in, mixed, newest, sums, pre, mix_gain, mix_first, mix_second, gain_mlp,
    keep_q, sib_q, keep_o, sib_o,
    extra, summed, small_out,
    hist, pack, acc, acc1, acc2, acc3, core_out, core_got, y_out, y_got, x_out, x_got, z_out, z_got,
    res, hist_sem, r_send, r_recv, a_send, a_recv, *grid_scratch,
):
    load = pltpu.make_async_copy(hist_in.at[HISTORY - 1], hist, hist_sem)
    load.start()
    enter([(SIB,), *RING_OF["y"], *RING_OF["x"], *RING_OF["z"]])
    grid = GridSum([(keep_q, sib_q), (keep_o, sib_o)], grid_scratch)
    grid.load()
    t, dp = lax.axis_index("tensor"), lax.axis_index("dp")
    core, y, z = lax.rem(t, 2), lax.rem(lax.div(t, 2), 4), lax.rem(dp, 4)
    x = 2 * lax.div(dp, 4) + lax.div(t, 8)
    grid.begin()
    load.wait()

    def exact(a, b, dims):
        return lax.dot_general(a, b, (dims, ((), ())), precision=PRECISE, preferred_element_type=F32)

    place = lax.broadcasted_iota(jnp.int32, (256, MIX), 1)
    entry = lax.div(lax.broadcasted_iota(jnp.int32, (256, MIX), 0), STEP)
    column = lax.broadcasted_iota(jnp.int32, (ROWS, MIX), 1)
    grad_mixing = jnp.zeros((ROWS, MIX), F32)
    for k in range(STREAMS):
        gathered = exact(mixed[k], (place == entry + k * HISTORY).astype(F32), ((1,), (0,)))
        grad_mixing = grad_mixing + gathered
        grad_mixing = jnp.where(column == k * HISTORY + HISTORY - 1, newest[:, k : k + 1], grad_mixing)
    hidden, slope = gelu_parts(pre[...])
    last = hist[...].astype(F32)
    inverse = lax.rsqrt(jnp.mean(last * last, axis=-1, keepdims=True) + NORM_EPS)
    normal = last * inverse
    grad_pre = exact(grad_mixing, mix_second[...], ((1,), (1,))) * slope
    pack[...] = jnp.zeros(pack.shape, F32)
    pack[0:MIX, 0:D] = exact(grad_pre, normal * mix_gain[...], ((0,), (0,)))
    pack[0:MIX, D : D + MIX] = exact(hidden, grad_mixing, ((0,), (0,)))
    grad_latest = exact(grad_pre, mix_first[...], ((1,), (0,)))
    pack[68:69, 0:D] = jnp.sum(grad_latest * normal, axis=0, keepdims=True)
    pack[69:72, 0:D] = sums[...]
    pack[72:73, 0:D] = gain_mlp[...]
    pack[68:69, D : D + MIX] = jnp.sum(grad_mixing, axis=0, keepdims=True)
    scaled = grad_latest * mix_gain[...]
    extra[...] = inverse * (scaled - normal * jnp.mean(scaled * normal, axis=-1, keepdims=True))
    acc[...] = jnp.zeros(acc.shape, F32)
    columns = SMALL_COLS // 128
    for i in range(SMALL_ROWS // 16):
        for j in range(columns):
            b = i * columns + j
            acc[b // 64, b // 16 % 4, b // 4 % 4, b % 4] = pack[i * 16 : (i + 1) * 16, j * 128 : (j + 1) * 128]

    core_out[...] = acc[1 - core].astype(BF)
    over_core = rcopy(core_out, core_got, r_send.at[0, 0], r_recv.at[0, 0], (SIB,))
    over_core.start()
    grid.relay()
    over_core.wait()
    acc1[...] = acc[core] + core_got[...].astype(F32)

    def reduce_over(level, source, out, got, me, axis):
        copies = []
        for i, target in enumerate(RING_OF[axis]):
            out[i] = source[flip(me, i + 1)].astype(BF)
            c = rcopy(out.at[i], got.at[i], r_send.at[level, i], r_recv.at[level, i], target)
            c.start()
            copies.append(c)
        for c in copies:
            c.wait()
        return source[me] + got[0].astype(F32) + got[1].astype(F32) + got[2].astype(F32)

    acc2[...] = reduce_over(1, acc1, y_out, y_got, y, "y")
    grid.turn()
    acc3[...] = reduce_over(2, acc2, x_out, x_got, x, "x")
    total = reduce_over(3, acc3, z_out, z_got, z, "z")
    res[core, y, x, z] = total.astype(BF)

    def spread_over(level, ref, axis):
        copies = []
        for i, target in enumerate(RING_OF[axis] if axis else ((SIB, 0),)):
            c = rcopy(ref, ref, a_send.at[level, i], a_recv.at[level, i], target)
            c.start()
            copies.append(c)
        for c in copies:
            c.wait()

    spread_over(0, res.at[core, y, x, z], "z")
    grid.relay2()
    spread_over(1, res.at[core, y, x], "x")
    spread_over(2, res.at[core, y], "y")
    spread_over(3, res.at[core], "")
    for i in range(SMALL_ROWS // 16):
        for j in range(columns):
            b = i * columns + j
            small_out[i * 16 : (i + 1) * 16, j * 128 : (j + 1) * 128] = res[b // 64, b // 16 % 4, b // 4 % 4, b % 4].astype(F32)
    summed[...] = grid.result()
    grid.finish()


def finish(history, mixed, newest, sums, pre, mix_gain, mix_first, mix_second, gain_mlp, *packs):
    dma = pltpu.SemaphoreType.DMA
    vm, hbm = pl.BlockSpec(memory_space=VMEM), pl.BlockSpec(memory_space=ANY)
    tile = (16, 128)
    return pl.pallas_call(
        finish_kernel,
        in_specs=[hbm] + [vm] * 8 + [hbm] * 4,
        out_specs=[vm] * 3,
        out_shape=[
            jax.ShapeDtypeStruct((ROWS, D), F32),
            jax.ShapeDtypeStruct((512, 256), F32),
            jax.ShapeDtypeStruct((SMALL_ROWS, SMALL_COLS), F32),
        ],
        scratch_shapes=[
            VMEM((ROWS, D), BF),
            VMEM((SMALL_ROWS, SMALL_COLS), F32),
            VMEM((2, 4, 4, 4, *tile), F32),
            VMEM((4, 4, 4, *tile), F32),
            VMEM((4, 4, *tile), F32),
            VMEM((4, *tile), F32),
            VMEM((4, 4, 4, *tile), BF),
            VMEM((4, 4, 4, *tile), BF),
            VMEM((3, 4, 4, *tile), BF),
            VMEM((3, 4, 4, *tile), BF),
            VMEM((3, 4, *tile), BF),
            VMEM((3, 4, *tile), BF),
            VMEM((3, *tile), BF),
            VMEM((3, *tile), BF),
            VMEM((2, 4, 4, 4, *tile), BF),
            dma(()), dma((4, 3)), dma((4, 3)), dma((4, 3)), dma((4, 3)),
            *GridSum.scratch(512),
        ],
        compiler_params=pltpu.CompilerParams(collective_id=5, has_side_effects=True, vmem_limit_bytes=61 * MIB),
        cost_estimate=pl.CostEstimate(flops=10**9, bytes_accessed=30 * MIB, transcendentals=0),
        name="finish",
    )(history, mixed, newest, sums, pre, mix_gain[None], mix_first.T, mix_second, gain_mlp, *packs)


def last_kernel(
    ds, grad_middle, extra, mix, small, sum_a, sum_e, sum_r, low,
    grad_hist, g_first, g_second, g_bias, g_mix, g_query, g_key, g_value, g_mlp, gw_q, gw_k, gw_v, gw_o, gw_e, gw_r, output,
):
    rows = ds.shape[1]

    @pl.when(pl.program_id(0) == 0)
    def _():
        g_first[...] = small[0:MIX, :D]
        g_second[...] = small[0:MIX, D : D + MIX]
        g_bias[...] = small[68:69, D : D + MIX]
        for i, ref in enumerate((g_mix, g_query, g_key, g_value, g_mlp)):
            ref[...] = small[68 + i : 69 + i, :D]
        gw_q[...] = sum_a[:256, :128]
        gw_k[...] = sum_a[:256, 128:]
        gw_v[:128] = sum_a[256:384, :128]
        gw_v[128:] = sum_a[256:384, 128:]
        gw_o[...] = sum_a[384:]
        gw_e[:, :256] = sum_e[:256]
        gw_e[:, 256:] = sum_e[256:]
        gw_r[...] = sum_r[...]
        output[...] = low[...]

    here = mix[...]
    lane = lax.broadcasted_iota(jnp.int32, (rows, 128), 1)
    own = lax.rem(lane, rows) == lax.broadcasted_iota(jnp.int32, (rows, 128), 0)
    stream = lax.rem(lax.div(lane, rows), STREAMS)
    left = []
    for j in range(HISTORY):
        piece = jnp.zeros((rows, 128), F32)
        for k in range(STREAMS):
            i = k * HISTORY + j
            piece = jnp.where(stream == k, here[:, i : i + 1], piece)
        left.append(jnp.concatenate(halves(jnp.where(own, piece, 0.0)), axis=1))
    left = jnp.concatenate(left, axis=0)
    for c in range(D // 512):
        cols = slice(c * 512, (c + 1) * 512)
        split = [halves(ds[k, :, cols] if k < 3 else grad_middle[:, cols]) for k in range(STREAMS)]
        right = jnp.concatenate([h for h, _ in split] + [m for _, m in split], axis=0)
        product = nn(left, jnp.concatenate([right, right], axis=0))
        grad_hist[0 : HISTORY - 1, :, cols] = product[:256].astype(BF).reshape(HISTORY - 1, rows, 512)
        grad_hist[HISTORY - 1, :, cols] = (product[256:] + extra[:, cols]).astype(BF)


def last(ds, grad_middle, extra, mix, small, sum_a, sum_e, sum_r, output):
    rows = 16

    def whole(*shape):
        return pl.BlockSpec(shape, lambda i: (0,) * len(shape))

    shapes = [(MIX, D), (MIX, MIX), (1, MIX)] + [(1, D)] * 5
    shapes += [(256, 128)] * 3 + [(128, 256), (256, 512), (512, 256)]
    return pl.pallas_call(
        last_kernel,
        grid=(ROWS // rows,),
        in_specs=[
            pl.BlockSpec((3, rows, D), lambda i: (0, i, 0)),
            pl.BlockSpec((rows, D), lambda i: (i, 0)),
            pl.BlockSpec((rows, D), lambda i: (i, 0)),
            pl.BlockSpec((rows, MIX), lambda i: (i, 0)),
            whole(SMALL_ROWS, SMALL_COLS),
            whole(512, 256),
            whole(512, 256),
            whole(512, 256),
            whole(ROWS, D),
        ],
        out_specs=[pl.BlockSpec((HISTORY, rows, D), lambda i: (0, i, 0))] + [whole(*x) for x in shapes] + [whole(ROWS, D)],
        out_shape=[jax.ShapeDtypeStruct((HISTORY, ROWS, D), BF)]
        + [jax.ShapeDtypeStruct(x, F32) for x in shapes]
        + [jax.ShapeDtypeStruct((ROWS, D), BF)],
        compiler_params=pltpu.CompilerParams(vmem_limit_bytes=61 * MIB),
        name="last",
    )(ds, grad_middle, extra, mix, small, sum_a, sum_e, sum_r, output)


def on_device(
    history, cotangent, lengths, mix_gain, mix_first, mix_second, mix_bias,
    gain_query, gain_key, gain_value, gain_mlp, w_query, w_key, w_value, w_output, w_expand, w_reduce,
):
    gains = (gain_query, gain_key, gain_value)
    heads, rows, w_all, wo_all, we_two, cot_all, n, inv, resid, mix, pre = qkv(
        history, cotangent, mix_gain, mix_first, mix_second, mix_bias, gains, w_query, w_key, w_value, w_output, w_expand
    )
    heads = heads.reshape(3, 2048, HEAD_DIM)
    ctx_rows, middle, reduced, keep_mlp, g_gain_mlp, grad_middle, grad_low = mlp(
        heads, lengths, wo_all, resid, gain_mlp, cotangent, cot_all, w_expand, we_two, w_reduce
    )
    output, grads, sum_e, keep_o, sib_o = back(heads, lengths, grad_low, wo_all, ctx_rows, reduced, middle, keep_mlp)
    ds, mixed, newest, sums, sum_r, keep_q, sib_q = streams_back(
        grads, rows, w_all, keep_mlp, history, grad_middle, n, inv, gains
    )
    extra, sum_a, small = finish(
        history, mixed, newest, sums, pre, mix_gain, mix_first, mix_second, g_gain_mlp, keep_q, sib_q, keep_o, sib_o
    )
    outs = last(ds, grad_middle, extra, mix, small, sum_a, sum_e, sum_r, output)
    grad_history, g_first, g_second, g_bias, g_mix, g_query, g_key, g_value, g_mlp = outs[:9]
    return (
        outs[15], grad_history, g_mix[0], g_first.T, g_second, g_bias[0], g_query[0], g_key[0], g_value[0], g_mlp[0],
        *outs[9:15],
    )


def solution(mesh):
    rows, cols, both = P("tensor", None), P(None, "tensor"), ("dp", "tensor")
    return jax.shard_map(
        on_device,
        mesh=mesh,
        in_specs=(P(None, both, None), P(both, None)) + (P(),) * 9 + (cols, cols, cols, rows, cols, rows),
        out_specs=(P(both, None), P(None, both, None)) + (P(),) * 8
        + (P("dp", "tensor"),) * 3 + (P("tensor", "dp"), P("dp", "tensor"), P("tensor", "dp")),
        check_vma=False,
    )
```

```python
import functools

import jax
import jax.numpy as jnp
from jax import lax
from jax.experimental import pallas as pl
from jax.experimental.pallas import tpu as pltpu
from jax.sharding import PartitionSpec as P

HEAD_DIM = 128
HISTORY = 17
STREAMS = 4
MIX = HISTORY * STREAMS
D = 2048
ROWS = 128
FF_SHARD = 512
NORM_EPS = 1e-06
MASKED = -1e30
MESH = pl.DeviceIdType.MESH
BF = jnp.bfloat16
F32 = jnp.float32
VMEM = pltpu.VMEM
ANY = pl.ANY
MIB = 2**20

Y1, Y2, Y3 = 2, 4, 6
SIB, XN, DIAG = 1, 8, 9
A_MASKS = (0, SIB, XN, DIAG)
LO, HI = pl.ds(0, 64), pl.ds(64, 64)


def flip(value, mask):
    for bit in (1, 2, 4, 8):
        if mask & bit:
            value = value + bit - 2 * bit * lax.rem(lax.div(value, bit), 2)
    return value


def dev(t_mask, dp_mask=0):
    return (flip(lax.axis_index("dp"), dp_mask), flip(lax.axis_index("tensor"), t_mask))


def enter(partners):
    barrier = pltpu.get_barrier_semaphore()
    for partner in partners:
        pl.semaphore_signal(barrier, inc=1, device_id=dev(*partner), device_id_type=MESH)
    pl.semaphore_wait(barrier, len(partners))


def rcopy(src, dst, send, recv, target):
    return pltpu.make_async_remote_copy(
        src_ref=src, dst_ref=dst, send_sem=send, recv_sem=recv, device_id=dev(*target), device_id_type=MESH
    )


def nt(a, b):
    return lax.dot_general(a, b, (((1,), (1,)), ((), ())), preferred_element_type=F32)


def tn(a, b):
    return lax.dot_general(a, b, (((0,), (0,)), ((), ())), preferred_element_type=F32)


def nn(a, b):
    return jnp.dot(a, b, preferred_element_type=F32)


class Gather:
    def __init__(self, own, rows, send, recv, slots=(0, 1, 2, 3)):
        def c(i, src, dst, target):
            return rcopy(src, dst, send.at[i], recv.at[i], (target,))

        _, one, two, three = slots
        self.copies = [
            c(0, own.at[LO], rows.at[one, LO], Y1),
            c(1, own.at[HI], rows.at[three, HI], Y3),
            c(2, own.at[HI], rows.at[one, HI], Y1),
            c(3, own.at[LO], rows.at[three, LO], Y3),
            c(4, rows.at[one, LO], rows.at[two, LO], Y3),
            c(5, rows.at[three, HI], rows.at[two, HI], Y1),
        ]

    def start(self):
        for i in range(4):
            self.copies[i].start()

    def forward(self):
        self.copies[0].wait_recv()
        self.copies[4].start()
        self.copies[1].wait_recv()
        self.copies[5].start()

    def arrived(self, slot):
        for i in {1: (2,), 3: (3,), 2: (4, 5)}[slot]:
            self.copies[i].wait_recv()

    def finish(self):
        for c in self.copies:
            c.wait_send()


def halves(value):
    high = value.astype(BF)
    return high, (value - high.astype(F32)).astype(BF)


def exact(a, b, dims):
    (ah, am), (bh, bm) = halves(a), halves(b)

    def dot(x, y):
        return lax.dot_general(x, y, (dims, ((), ())), preferred_element_type=F32)

    return dot(ah, bh) + (dot(ah, bm) + dot(am, bh))


def gelu_parts(x):
    cdf = 0.5 * (1.0 + lax.erf(x * (0.5**0.5)))
    return x * cdf, cdf + x * jnp.exp(-0.5 * x * x) * 0.3989422804014327


STEP = 16
WIDE = 256


def mix_tokens(last, mix_gain, mix_first, mix_second, mix_bias, pre_out, mix_out):
    inverse = lax.rsqrt(jnp.mean(last * last, axis=-1, keepdims=True) + NORM_EPS)
    pre = exact(last * inverse * mix_gain[...], mix_first[...], ((1,), (1,)))
    pre_out[...] = pre
    hidden = gelu_parts(pre)[0]
    mix_out[...] = exact(hidden, mix_second[...], ((1,), (0,))) + mix_bias[...]


def make_streams(at, hist, mix, gains, held, x_out, n_out, inv_out, resid_out):
    here = mix[at]
    lane = lax.broadcasted_iota(jnp.int32, (STEP, 128), 1)
    own = lax.rem(lane, STEP) == lax.broadcasted_iota(jnp.int32, (STEP, 128), 0)
    entry = lax.div(lane, STEP)
    high, low = [], []
    for k in range(STREAMS):
        pieces = []
        for part in range(2):
            piece = jnp.zeros((STEP, 128), F32)
            for j in range(8):
                i = k * HISTORY + part * 8 + j
                piece = jnp.where(entry == j, here[:, i : i + 1], piece)
            pieces.append(jnp.where(own, piece, 0.0))
        h, m = halves(jnp.concatenate(pieces, axis=1))
        high.append(h)
        low.append(m)
    left = jnp.concatenate(high + low, axis=0)
    squares = [jnp.zeros((STEP, 1), F32) for _ in range(3)]
    for c in range(D // 512):
        cols = slice(c * 512, (c + 1) * 512)
        product = nn(left, hist[0 : HISTORY - 1, at, cols].reshape(256, 512))
        newest = hist[HISTORY - 1, at, cols].astype(F32)
        for k in range(STREAMS):
            i = k * HISTORY + HISTORY - 1
            value = product[k * STEP : (k + 1) * STEP] + product[(4 + k) * STEP : (5 + k) * STEP]
            value = value + here[:, i : i + 1] * newest
            if k == 3:
                resid_out[at, cols] = value
            else:
                held[k, :, cols] = value
                squares[k] = squares[k] + jnp.sum(value * value, axis=-1, keepdims=True)
    for k in range(3):
        inverse = lax.rsqrt(squares[k] * (1.0 / D) + NORM_EPS)
        inv_out[k, at] = jnp.broadcast_to(inverse, (STEP, 128))
        normal = held[k] * inverse
        n_out[k, at] = normal.astype(BF)
        x_out[k, at] = (normal * gains[k][...]).astype(BF)


def qkv_kernel(
    hist_in, cot, mix_gain, mix_first, mix_second, mix_bias, gain_q, gain_k, gain_v,
    w_query, w_key, w_value, w_output, w_expand,
    heads, rows_out, w_out, wo_all, we_two, cot_all, n_out, inv_out, resid_out, mix, pre,
    hist, held, x, rows, weights, proj, hist_sem, cot_send, cot_recv, g_send, g_recv, w_send, w_recv, f_send, f_recv, h_send, h_recv, local,
):
    tiles = ROWS // STEP
    latest = pltpu.make_async_copy(hist_in.at[HISTORY - 1], hist.at[HISTORY - 1], hist_sem.at[tiles])
    latest.start()
    older = pl.ds(0, HISTORY - 1)

    def tile_load(tile):
        at = pl.ds(pl.multiple_of(tile * STEP, STEP), STEP)
        return pltpu.make_async_copy(hist_in.at[older, at], hist.at[older, at], hist_sem.at[tile])

    for tile in range(tiles):
        tile_load(tile).start()
    enter([(Y1,), (Y3,), (SIB,), (XN,), (XN, 4), (DIAG,)])
    t = lax.axis_index("tensor")
    left = pl.ds(0, D // 2)
    cot_gather = Gather(cot.at[:, left], cot_all, cot_send, cot_recv, (0, 1, 3, 2))
    cot_gather.start()
    cot_keep = pltpu.make_async_copy(cot.at[:, left], cot_all.at[0], hist_sem.at[tiles + 1])
    cot_keep.start()
    sources = [w_query, w_key, w_value, w_output, w_expand]
    slots = [lambda r, i=i: weights.at[i, r] for i in range(3)]
    slots += [lambda r: wo_all.at[r], lambda r: we_two.at[r - 1]]
    to_sib, to_x, onward = [], [], []
    for i, src in enumerate(sources):
        half = src.shape[0] // 2
        lo, hi = pl.ds(0, half), pl.ds(half, half)
        to_x.append(
            (
                rcopy(src.at[lo], slots[i](2).at[lo], w_send.at[i, 0], w_recv.at[i, 0], (XN,)),
                rcopy(src.at[hi], slots[i](2).at[hi], w_send.at[i, 1], w_recv.at[i, 1], (XN, 4)),
            )
        )
        to_sib.append(rcopy(src, slots[i](1), w_send.at[i, 2], w_recv.at[i, 2], (SIB,)))
        if i < 4:
            onward.append(rcopy(slots[i](2), slots[i](3), f_send.at[i], f_recv.at[i], (SIB,)))
    keep = [pltpu.make_async_copy(sources[i], slots[i](0), local.at[i]) for i in range(4)]
    gathers = [Gather(x.at[a], rows.at[a], g_send.at[a], g_recv.at[a]) for a in range(3)]
    for a in range(3):
        to_x[a][0].start()
        to_x[a][1].start()
        to_sib[a].start()
        keep[a].start()
    latest.wait()
    mix_tokens(hist[HISTORY - 1].astype(F32), mix_gain, mix_first, mix_second, mix_bias, pre, mix)

    @pl.loop(0, tiles)
    def _(tile):
        tile_load(tile).wait()
        at = pl.ds(pl.multiple_of(tile * STEP, STEP), STEP)
        make_streams(at, hist, mix, (gain_q, gain_k, gain_v), held, x, n_out, inv_out, resid_out)

    cot_gather.forward()
    gathers[0].start()
    gathers[1].start()
    for i in (3, 4):
        to_x[i][0].start()
        to_x[i][1].start()
        to_sib[i].start()
    keep[3].start()
    for a in range(3):
        for c in to_x[a]:
            c.wait_recv()
        onward[a].start()
        gathers[a].forward()
        if a == 0:
            gathers[2].start()
    sends = []

    def project(a, s):
        block = x[a] if s == 0 else rows[a, s]
        for p in range(2):
            pair = jnp.concatenate([weights[a, 2 * p], weights[a, 2 * p + 1]], axis=1)
            y = nn(block, pair).astype(BF)
            proj[a, s, 2 * p] = y[:, :128]
            proj[a, s, 2 * p + 1] = y[:, 128:]
        place = flip(t, 2 * s)
        for r in range(4):
            src, dst = proj.at[a, s, r], heads.at[a, place]
            if r == 0:
                c = pltpu.make_async_copy(src, dst, h_send.at[a, s, 0])
            else:
                c = rcopy(src, dst, h_send.at[a, s, r], h_recv.at[a, s, r], (A_MASKS[r],))
            c.start()
            sends.append((r, c))

    for a in range(3):
        keep[a].wait()
        to_sib[a].wait_recv()
        onward[a].wait_recv()
        project(a, 0)
    store = []
    for a in range(3):
        c = pltpu.make_async_copy(weights.at[a], w_out.at[a], local.at[4 + a])
        c.start()
        store.append(c)
        c = pltpu.make_async_copy(x.at[a], rows_out.at[a, 0], local.at[7 + a])
        c.start()
        store.append(c)
    for a in range(3):
        for s in (1, 3):
            gathers[a].arrived(s)
            project(a, s)
    for c in to_x[3]:
        c.wait_recv()
    onward[3].start()
    for a in range(3):
        gathers[a].arrived(2)
        project(a, 2)
        c = pltpu.make_async_copy(rows.at[a, pl.ds(1, 3)], rows_out.at[a, pl.ds(1, 3)], local.at[10 + a])
        c.start()
        store.append(c)
    for s in (1, 3, 2):
        cot_gather.arrived(s)
    cot_keep.wait()
    for g in gathers + [cot_gather]:
        g.finish()
    for r, c in sends:
        if r == 0:
            c.wait()
        else:
            c.wait_send()
    for r, c in sends:
        if r:
            c.wait_recv()
    for i in range(5):
        for c in to_x[i]:
            c.wait_send()
            if i > 3:
                c.wait_recv()
        to_sib[i].wait_send()
        if i > 2:
            to_sib[i].wait_recv()
    for i in range(4):
        onward[i].wait_send()
    onward[3].wait_recv()
    keep[3].wait()
    for c in store:
        c.wait()


def qkv(history, cot, mix_gain, mix_first, mix_second, mix_bias, gains, *weights):
    dma = pltpu.SemaphoreType.DMA
    vm, hbm = pl.BlockSpec(memory_space=VMEM), pl.BlockSpec(memory_space=ANY)
    return pl.pallas_call(
        qkv_kernel,
        in_specs=[hbm] * 2 + [vm] * 7 + [hbm] * 5,
        out_specs=[hbm] * 6 + [vm] * 5,
        out_shape=[
            jax.ShapeDtypeStruct((3, 16, ROWS, HEAD_DIM), BF),
            jax.ShapeDtypeStruct((3, 4, ROWS, D), BF),
            jax.ShapeDtypeStruct((3, 4, D, HEAD_DIM), BF),
            jax.ShapeDtypeStruct((4, HEAD_DIM, D), BF),
            jax.ShapeDtypeStruct((2, D, FF_SHARD), BF),
            jax.ShapeDtypeStruct((4, ROWS, D // 2), BF),
            jax.ShapeDtypeStruct((3, ROWS, D), BF),
            jax.ShapeDtypeStruct((3, ROWS, 128), F32),
            jax.ShapeDtypeStruct((ROWS, D), F32),
            jax.ShapeDtypeStruct((ROWS, MIX), F32),
            jax.ShapeDtypeStruct((ROWS, MIX), F32),
        ],
        scratch_shapes=[
            VMEM((HISTORY, ROWS, D), BF),
            VMEM((3, STEP, D), F32),
            VMEM((3, ROWS, D), BF),
            VMEM((3, 4, ROWS, D), BF),
            VMEM((3, 4, D, HEAD_DIM), BF),
            VMEM((3, 4, 4, ROWS, HEAD_DIM), BF),
            dma((ROWS // STEP + 2,)), dma((6,)), dma((6,)),
            dma((3, 6)), dma((3, 6)), dma((5, 3)), dma((5, 3)), dma((4,)), dma((4,)), dma((3, 4, 4)), dma((3, 4, 4)), dma((13,)),
        ],
        compiler_params=pltpu.CompilerParams(collective_id=1, has_side_effects=True, vmem_limit_bytes=61 * MIB),
        cost_estimate=pl.CostEstimate(flops=6 * 512 * 2048 * 512, bytes_accessed=30 * MIB, transcendentals=0),
        name="qkv",
    )(
        history, cot, mix_gain[None], mix_first.T, mix_second, mix_bias[None], *[g[None] for g in gains], *weights
    )


def first_places(lengths, places):
    group = lax.axis_index("dp")
    first, end = jnp.zeros_like(places), jnp.int32(0)
    for i in range(lengths.shape[1]):
        end = end + lengths[group, i]
        first = jnp.where(places >= end, end, first)
    return first


def attend_kernel(q, k, v, lengths, ctx):
    tokens, step = q.shape[0], 256
    scale = HEAD_DIM ** (-0.5)
    for i in range(tokens // step):
        length = (i + 1) * step
        at = slice(i * step, length)
        scores = nt(q[at], k[:length]) * scale
        key_place = lax.broadcasted_iota(jnp.int32, (step, length), 1)
        query_place = lax.broadcasted_iota(jnp.int32, (step, 1), 0) + i * step
        allowed = (key_place >= first_places(lengths, query_place)) & (key_place <= query_place)
        scores = jnp.where(allowed, scores, MASKED)
        top = jnp.max(scores, axis=-1, keepdims=True)
        e = jnp.exp(scores - top)
        low = (e * (1.0 / jnp.sum(e, axis=-1, keepdims=True))).astype(BF)
        ctx[at] = nn(low, v[:length]).astype(BF)


def attend_back_kernel(q, k, v, gc, lengths, dq, dk, dv, dk_sum, dv_sum, hooks):
    tokens, step = q.shape[0], 256
    scale = HEAD_DIM ** (-0.5)
    k_turned = k[...].astype(F32).T.astype(BF)
    for i in range(tokens // step):
        if i in hooks:
            hooks[i]()
        length = (i + 1) * step
        at = slice(i * step, length)
        scores = nt(k[:length], q[at]) * scale
        key_place = lax.broadcasted_iota(jnp.int32, (length, step), 0)
        query_place = lax.broadcasted_iota(jnp.int32, (1, step), 1) + i * step
        allowed = (key_place >= first_places(lengths, query_place)) & (key_place <= query_place)
        scores = jnp.where(allowed, scores, MASKED)
        top = jnp.max(scores, axis=0, keepdims=True)
        e = jnp.exp(scores - top)
        probs = e * (1.0 / jnp.sum(e, axis=0, keepdims=True))
        grad_probs = nt(v[:length], gc[at])
        delta = jnp.sum(grad_probs * probs, axis=0, keepdims=True)
        grad_scores = (probs * (grad_probs - delta)).astype(BF)
        low = probs.astype(BF)
        dq[at] = (nn(k_turned[:, :length], grad_scores) * scale).T.astype(BF)
        key_part = nn(grad_scores, q[at])
        value_part = nn(low, gc[at])
        if i:
            dk_sum[: i * step] += key_part[: i * step]
            dv_sum[: i * step] += value_part[: i * step]
        dk_sum[at] = key_part[i * step :]
        dv_sum[at] = value_part[i * step :]
    dk[...] = (dk_sum[...] * scale).astype(BF)
    dv[...] = dv_sum[...].astype(BF)


def mlp_kernel(
    heads, lengths, wo_all, resid, gain, cot, cot_all, w_expand, we_two, w_reduce,
    ctx_rows, middle_out, reduced_out, keep_out, grad_gain, grad_middle, grad_low,
    ctx, we, wr, mlp_rows, cot_rows, act, gexp, parts, stage, sc_out, sc_pass, sc_got,
    mlp_sib, cot_sib, act_sib, gexp_sib, act_turned,
    g_send, g_recv, s_send, s_recv, w_send, w_recv, c_send, c_recv, d_send, d_recv, local, keep_sem, cot_send, cot_recv,
):
    enter([(Y1,), (Y3,), (SIB,), (XN,), (XN, 4), (DIAG,)])
    t = lax.axis_index("tensor")
    q, k, v = heads.at[0], heads.at[1], heads.at[2]
    slots = (0, 1, 3, 2)
    right = pl.ds(D // 2, D // 2)
    cot_gather = Gather(cot.at[:, right], cot_rows.at[:, :, right], cot_send, cot_recv, slots)
    cot_gather.start()
    half = FF_SHARD // 2
    lo, hi = pl.ds(0, half), pl.ds(half, half)
    loads = [
        pltpu.make_async_copy(w_expand, we.at[0], local.at[0]),
        pltpu.make_async_copy(we_two, we.at[pl.ds(1, 2)], local.at[1]),
        pltpu.make_async_copy(w_reduce, wr.at[0], local.at[2]),
        pltpu.make_async_copy(cot_all, cot_rows.at[:, :, pl.ds(0, D // 2)], local.at[3]),
        pltpu.make_async_copy(cot.at[:, right], cot_rows.at[0, :, right], local.at[4]),
    ]
    for c in loads:
        c.start()
    sib = [
        rcopy(we_two.at[1], we.at[3], w_send.at[0], w_recv.at[0], (SIB,)),
        rcopy(w_reduce, wr.at[1], w_send.at[1], w_recv.at[1], (SIB,)),
        rcopy(wr.at[2], wr.at[3], w_send.at[2], w_recv.at[2], (SIB,)),
    ]
    across = [
        rcopy(w_reduce.at[lo], wr.at[2, lo], w_send.at[3], w_recv.at[3], (XN,)),
        rcopy(w_reduce.at[hi], wr.at[2, hi], w_send.at[4], w_recv.at[4], (XN, 4)),
    ]
    sib[0].start()
    sib[1].start()
    attend_kernel(q, k, v, lengths, ctx)
    cot_gather.forward()
    back = {}
    for s in (2, 1, 3, 0):
        for r in range(4):
            place = pl.multiple_of(flip(t, A_MASKS[r] + 2 * s) * ROWS, ROWS)
            src, dst = ctx.at[pl.ds(place, ROWS)], ctx_rows.at[s, r]
            if r:
                back[s, r] = rcopy(src, dst, c_send.at[s, r], c_recv.at[s, r], (A_MASKS[r],))
            else:
                back[s, r] = pltpu.make_async_copy(src, dst, c_send.at[s, r])
            back[s, r].start()
    for c in across:
        c.start()

    def rows_of(s):
        for r in range(4):
            back[s, r].wait_recv() if r else back[s, r].wait()
        return jnp.concatenate([ctx_rows[s, r] for r in range(4)], axis=1)

    weight = wo_all[...].reshape(4 * HEAD_DIM, D)

    def ring(index):
        return Ring(
            lambda s, half: parts[{1: 0, 3: 1, 0: 2, 2: 3}[s], half],
            sc_out, sc_pass, sc_got, s_send.at[index], s_recv.at[index], (Y1,), (Y3,), ROWS,
        )

    ring1 = ring(0)
    parts[3] = nn(rows_of(2), weight)
    ring1.opposite()
    three = jnp.concatenate([rows_of(1), rows_of(3), rows_of(0)], axis=0)
    parts[0:3] = nn(three, weight).reshape(3, ROWS, D)
    ring1.neighbours()
    ring1.relay()
    for c in across:
        c.wait_recv()
    sib[2].start()
    for c in loads:
        c.wait()
    ring1.arrive()
    middle = resid[...] + ring1.total(pl.ds(0, ROWS))
    middle_out[...] = middle
    inverse = lax.rsqrt(jnp.mean(middle * middle, axis=-1, keepdims=True) + NORM_EPS)
    mlp_rows[0] = (middle * inverse * gain[...]).astype(BF)
    mlp_gather = Gather(mlp_rows.at[0], mlp_rows, g_send, g_recv, slots)
    mlp_gather.start()
    for s in (1, 3, 2):
        cot_gather.arrived(s)
    shares = [
        rcopy(cot_rows, cot_sib, d_send.at[0], d_recv.at[0], (SIB,)),
        rcopy(mlp_rows, mlp_sib, d_send.at[1], d_recv.at[1], (SIB,)),
    ]
    shares[0].start()
    for c in sib:
        c.wait_recv()

    def block(start, count):
        at, m = pl.ds(start, count), count * ROWS

        @pl.loop(0, 4)
        def _(r):
            expanded = nn(mlp_rows[at].reshape(m, D), we[r])
            grad_active = nt(cot_rows[at].reshape(m, D), wr[r])
            value, slope = gelu_parts(expanded)
            act[r, at] = value.astype(BF).reshape(count, ROWS, FF_SHARD)
            gexp[r, at] = (grad_active * slope).astype(BF).reshape(count, ROWS, FF_SHARD)

    def reduce_rows(start, count):
        at, m = pl.ds(start, count), count * ROWS
        total = nn(act[0, at].reshape(m, FF_SHARD), wr[0])
        for r in range(1, 4):
            total += nn(act[r, at].reshape(m, FF_SHARD), wr[r])
        for i in range(count):
            reduced_out[(0, 1, 3, 2)[start + i]] = total[i * ROWS : (i + 1) * ROWS].astype(BF)

    block(0, 1)
    mlp_gather.forward()
    reduce_rows(0, 1)
    for s in (1, 3):
        mlp_gather.arrived(s)
    block(1, 2)
    mlp_gather.arrived(2)
    shares[1].start()
    block(3, 1)
    for n, r in enumerate((1, 3)):
        shares.append(rcopy(act.at[r], act_sib.at[n], d_send.at[2 + n], d_recv.at[2 + n], (SIB,)))
        shares.append(rcopy(gexp.at[r], gexp_sib.at[n], d_send.at[4 + n], d_recv.at[4 + n], (SIB,)))
    def grad_mlp(start, count):
        at, m = pl.ds(start, count), count * ROWS
        parts[at] = jnp.zeros((count, ROWS, D), F32)

        @pl.loop(0, 4)
        def _(r):
            parts[at] += nt(gexp[r, at].reshape(m, FF_SHARD), we[r]).reshape(count, ROWS, D)

    ring1.finish()
    ring2 = ring(1)
    grad_mlp(3, 1)
    ring2.opposite()
    parts[0:3] = jnp.zeros((3, ROWS, D), F32)

    @pl.loop(0, 4)
    def _(r):
        lhs = jnp.concatenate([gexp[r, 1], gexp[r, 2], gexp[r, 0]], axis=0)
        parts[0:3] += nt(lhs, we[r]).reshape(3, ROWS, D)

    ring2.neighbours()
    for c in shares[2:]:
        c.start()
    ring2.relay()
    reduce_rows(1, 3)
    for c in shares:
        c.wait_recv()
    @pl.loop(0, 8)
    def _(d):
        cols = pl.ds(pl.multiple_of(d * 256, 256), 256)
        own, other = mlp_rows[:, :, cols].reshape(512, 256).T, mlp_sib[:, :, cols].reshape(512, 256).T
        for n, r in enumerate((0, 2)):
            grad_e = nn(own, gexp[r].reshape(512, FF_SHARD)) + nn(other, gexp_sib[n].reshape(512, FF_SHARD))
            for c in range(2):
                stage[n, d, c * 256 : (c + 1) * 256] = grad_e[:, c * 256 : (c + 1) * 256].astype(BF)

    for n, r in enumerate((0, 2)):
        act_turned[n] = jnp.concatenate([act[r].reshape(512, FF_SHARD), act_sib[n].reshape(512, FF_SHARD)], axis=0).T

    @pl.loop(0, 8)
    def _(d):
        cols = pl.ds(pl.multiple_of(d * 256, 256), 256)
        rhs = jnp.concatenate([cot_rows[:, :, cols].reshape(512, 256), cot_sib[:, :, cols].reshape(512, 256)], axis=0)
        for n in range(2):
            stage[n, d, 512:1024] = nn(act_turned[n], rhs).astype(BF)

    keeps = [pltpu.make_async_copy(stage, keep_out, keep_sem)]
    keeps[0].start()
    ring2.arrive()
    got = ring2.total(pl.ds(0, ROWS))
    middle = middle_out[...]
    inverse = lax.rsqrt(jnp.mean(middle * middle, axis=-1, keepdims=True) + NORM_EPS)
    normal = middle * inverse
    grad_gain[...] = jnp.sum(got * normal, axis=0, keepdims=True)
    scaled = got * gain[...]
    grad = cot_rows[0].astype(F32) + inverse * (scaled - normal * jnp.mean(scaled * normal, axis=-1, keepdims=True))
    grad_middle[...] = grad
    grad_low[...] = grad.astype(BF)
    ring2.finish()
    cot_gather.finish()
    mlp_gather.finish()
    for c in sib + across + shares:
        c.wait_send()
    for (s, r), c in back.items():
        if r:
            c.wait_send()
    for c in keeps:
        c.wait()


def mlp(heads, lengths, wo_all, resid, gain_mlp, cot, cot_all, w_expand, we_two, w_reduce):
    dma = pltpu.SemaphoreType.DMA
    vm, hbm, sm = [pl.BlockSpec(memory_space=m) for m in (VMEM, ANY, pltpu.SMEM)]
    return pl.pallas_call(
        mlp_kernel,
        in_specs=[vm, sm] + [vm] * 3 + [hbm] * 5,
        out_specs=[vm, vm, vm, hbm, vm, vm, vm],
        out_shape=[
            jax.ShapeDtypeStruct((4, 4, ROWS, HEAD_DIM), BF),
            jax.ShapeDtypeStruct((ROWS, D), F32),
            jax.ShapeDtypeStruct((4, ROWS, D), BF),
            jax.ShapeDtypeStruct((2, 8, 1024, 256), BF),
            jax.ShapeDtypeStruct((1, D), F32),
            jax.ShapeDtypeStruct((ROWS, D), F32),
            jax.ShapeDtypeStruct((ROWS, D), BF),
        ],
        scratch_shapes=[
            VMEM((2048, HEAD_DIM), BF),
            VMEM((4, D, FF_SHARD), BF),
            VMEM((4, FF_SHARD, D), BF),
            VMEM((4, ROWS, D), BF),
            VMEM((4, ROWS, D), BF),
            VMEM((4, 4, ROWS, FF_SHARD), BF),
            VMEM((4, 4, ROWS, FF_SHARD), BF),
            VMEM((4, ROWS, D), F32),
            VMEM((2, 8, 1024, 256), BF),
            VMEM((3, ROWS, D), BF),
            VMEM((ROWS, D), BF),
            VMEM((2, ROWS, D), BF),
            VMEM((4, ROWS, D), BF),
            VMEM((4, ROWS, D), BF),
            VMEM((2, 4, ROWS, FF_SHARD), BF),
            VMEM((2, 4, ROWS, FF_SHARD), BF),
            VMEM((2, FF_SHARD, 1024), BF),
            dma((6,)), dma((6,)), dma((2, 6)), dma((2, 6)), dma((5,)), dma((5,)), dma((4, 4)), dma((4, 4)),
            dma((6,)), dma((6,)), dma((5,)), dma(()), dma((6,)), dma((6,)),
        ],
        compiler_params=pltpu.CompilerParams(collective_id=2, has_side_effects=True, vmem_limit_bytes=61 * MIB),
        cost_estimate=pl.CostEstimate(flops=30 * 10**9, bytes_accessed=50 * MIB, transcendentals=0),
        name="mlp",
    )(heads, lengths, wo_all, resid, gain_mlp[None], cot, cot_all, w_expand, we_two, w_reduce)


class Ring:
    def __init__(self, part, out, passed, got, send, recv, near, far, size):
        half = size // 2
        lo, hi = pl.ds(0, half), pl.ds(half, half)

        def c(i, src, dst, target):
            return rcopy(src, dst, send.at[i], recv.at[i], target)

        self.part, self.out, self.passed, self.got, self.lo, self.hi = part, out, passed, got, lo, hi
        self.copies = [
            c(0, out.at[0, lo], passed.at[lo], near),
            c(1, out.at[0, hi], passed.at[hi], far),
            c(2, out.at[1, lo], got.at[0, lo], near),
            c(3, out.at[2, hi], got.at[1, hi], far),
            c(4, out.at[2, lo], got.at[1, lo], far),
            c(5, out.at[1, hi], got.at[0, hi], near),
        ]

    def opposite(self):
        self.send(0, self.lo, self.part(2, self.lo), 0)
        self.send(0, self.hi, self.part(2, self.hi), 1)

    def neighbours(self):
        self.send(1, self.lo, self.part(1, self.lo), 2)
        self.send(2, self.hi, self.part(3, self.hi), 3)

    def begin(self):
        self.opposite()
        self.neighbours()

    def send(self, slot, half, value, i):
        self.out[slot, half] = value.astype(BF)
        self.copies[i].start()

    def relay(self):
        for i, slot, s, half in ((0, 2, 3, self.lo), (1, 1, 1, self.hi)):
            self.copies[i].wait_recv()
            self.out[slot, half] = (self.part(s, half) + self.passed[half].astype(F32)).astype(BF)
            self.copies[4 + i].start()

    def arrive(self):
        for i in (2, 3, 4, 5):
            self.copies[i].wait_recv()

    def total(self, index):
        return self.part(0, index) + self.got[0, index].astype(F32) + self.got[1, index].astype(F32)

    def finish(self):
        for c in self.copies:
            c.wait_send()


X_RING = ((XN,), (XN, 4))
Z_RING = ((0, 1), (0, 3))


class GridSum:
    @staticmethod
    def scratch(rows, pair=True):
        half, dma = rows // 2, pltpu.SemaphoreType.DMA
        return [
            VMEM((2, 8, rows, 256), BF),
            VMEM((2, 8, rows, 256) if pair else (16, 128), BF),
            VMEM((2, 3, 4, half, 256), BF),
            VMEM((2, 4, half, 256), BF),
            VMEM((2, 2, 4, half, 256), BF),
            VMEM((2, 4, half, 256), F32),
            VMEM((2, 3, half, 256), BF),
            VMEM((2, half, 256), BF),
            VMEM((2, 2, half, 256), BF),
            dma((4, 6)),
            dma((4, 6)),
            dma((4,)),
        ]

    def __init__(self, pieces, scratch):
        (self.a, self.b, out1, pass1, got1, self.mid, out2, pass2, got2, send, recv, load) = scratch
        rows = self.a.shape[2]
        self.half = half = rows // 2
        self.loads, start = [], 0
        for i, (kept, given) in enumerate(pieces):
            at = pl.ds(start, kept.shape[2])
            start += kept.shape[2]
            self.loads.append(pltpu.make_async_copy(kept, self.a.at[:, :, at], load.at[2 * i]))
            if given is not None:
                self.loads.append(pltpu.make_async_copy(given, self.b.at[:, :, at], load.at[2 * i + 1]))
        dp = lax.axis_index("dp")
        place = {(sx, sz): flip(dp, (4 if sx in (2, 3) else 0) + sz) for sx in range(4) for sz in range(4)}

        def block(sx, sz, path):
            shard = 0 if sx in (0, 2) else 1
            at = slice(path * half, (path + 1) * half)
            d = place[sx, sz]
            own = self.a[shard, d, at].astype(F32)
            return own if given is None else own + self.b[shard, d, at].astype(F32)

        def span(ds):
            return range(ds.start, ds.start + ds.size)

        def over_x(s, half_):
            return jnp.stack([block(s, z, 0) for z in span(half_)])

        def over_z(s, half_):
            return jnp.stack([block(x, s, 1) for x in span(half_)])

        rings = (X_RING, Z_RING)
        self.first, self.second = [], []
        for path, part in enumerate((over_x, over_z)):
            near, far = rings[path]
            self.first.append(
                Ring(part, out1.at[path], pass1.at[path], got1.at[path], send.at[path], recv.at[path], near, far, 4)
            )
            near, far = rings[1 - path]
            mid = self.mid.at[path]

            def later(s, half_, mid=mid):
                return mid[s, half_]

            self.second.append(
                Ring(
                    later, out2.at[path], pass2.at[path], got2.at[path], send.at[2 + path], recv.at[2 + path], near, far, half
                )
            )

    def load(self):
        for c in self.loads:
            c.start()

    def begin(self):
        for c in self.loads:
            c.wait()
        for ring in self.first:
            ring.begin()

    def relay(self):
        for ring in self.first:
            ring.relay()

    def turn(self):
        for path in range(2):
            ring = self.first[path]
            ring.arrive()
            for s in (2, 1, 3, 0):
                self.mid[path, s] = ring.total(pl.ds(s, 1))[0]
            self.second[path].begin()

    def relay2(self):
        for ring in self.second:
            ring.relay()

    def result(self):
        parts = []
        for ring in self.second:
            ring.arrive()
            parts.append(ring.total(pl.ds(0, self.half)))
        return jnp.concatenate(parts, axis=0)

    def finish(self):
        for ring in self.first + self.second:
            ring.finish()


def back_kernel(
    heads, lengths, grad_low, wo_all, ctx_rows, reduced, middle, keep_in,
    output, grads, summed, keep_out, sib_out,
    rows, proj, gc, dk_sum, dv_sum, stage, sc_out, sc_pass, sc_got,
    g_send, g_recv, s_send, s_recv, c_send, c_recv, d_send, d_recv, *grid_scratch,
):
    enter([(Y1,), (Y3,), (SIB,), (DIAG,), *X_RING, *Z_RING])
    t = lax.axis_index("tensor")
    gather = Gather(grad_low, rows, g_send, g_recv)
    gather.start()
    part = pl.ds(0, 512)
    grid = GridSum([(keep_in.at[:, :, part], None)], grid_scratch)
    grid.load()
    q, k, v = heads.at[0], heads.at[1], heads.at[2]
    ring = Ring(
        lambda s, half: reduced[s, half].astype(F32), sc_out, sc_pass, sc_got, s_send, s_recv, (Y1,), (Y3,), ROWS
    )
    rows[0] = grad_low[...]
    weight = wo_all[...].reshape(4 * HEAD_DIM, D)
    moves = []

    def project(s):
        y = nt(rows[s], weight).astype(BF)
        place = pl.multiple_of(flip(t, 2 * s) * ROWS, ROWS)
        for r in range(4):
            proj[s, r] = y[:, r * HEAD_DIM : (r + 1) * HEAD_DIM]
            src, dst = proj.at[s, r], gc.at[pl.ds(place, ROWS)]
            if r:
                c = rcopy(src, dst, c_send.at[s, r], c_recv.at[s, r], (A_MASKS[r],))
            else:
                c = pltpu.make_async_copy(src, dst, c_send.at[s, r])
            c.start()
            moves.append((r, c))

    project(0)
    gather.forward()
    ring.begin()
    grid.begin()
    for s in (1, 3, 2):
        gather.arrived(s)
        project(s)
    ring.relay()
    grid.relay()
    all_rows = rows[...].reshape(4 * ROWS, D)
    sends = []
    for n, r in enumerate((1, 3, 0, 2)):
        lhs = jnp.concatenate([ctx_rows[s, r] for s in range(4)], axis=0)
        grad_o = tn(lhs, all_rows).astype(BF)
        for d in range(8):
            stage[n, d] = grad_o[:, d * 256 : (d + 1) * 256]
        if n < 2:
            c = rcopy(stage.at[n], sib_out.at[n], d_send.at[n], d_recv.at[n], (SIB,))
        else:
            c = pltpu.make_async_copy(stage.at[n], keep_out.at[n - 2], d_send.at[n])
        c.start()
        sends.append(c)
    for r, c in moves:
        c.wait_recv() if r else c.wait()
    hooks = {4: grid.turn, 7: grid.relay2}
    attend_back_kernel(q, k, v, gc, lengths, grads.at[0], grads.at[1], grads.at[2], dk_sum, dv_sum, hooks)
    summed[...] = grid.result()
    grid.finish()
    ring.arrive()
    output[...] = (middle[...] + ring.total(pl.ds(0, ROWS))).astype(BF)
    gather.finish()
    ring.finish()
    for r, c in moves:
        if r:
            c.wait_send()
    for n, c in enumerate(sends):
        c.wait()


def back(heads, lengths, grad_low, wo_all, ctx_rows, reduced, middle, keep):
    dma = pltpu.SemaphoreType.DMA
    vm, hbm, sm = [pl.BlockSpec(memory_space=m) for m in (VMEM, ANY, pltpu.SMEM)]
    return pl.pallas_call(
        back_kernel,
        in_specs=[vm, sm] + [vm] * 5 + [hbm],
        out_specs=[vm, vm, vm, hbm, hbm],
        out_shape=[
            jax.ShapeDtypeStruct((ROWS, D), BF),
            jax.ShapeDtypeStruct((3, 2048, HEAD_DIM), BF),
            jax.ShapeDtypeStruct((512, 256), F32),
            jax.ShapeDtypeStruct((2, 8, ROWS, 256), BF),
            jax.ShapeDtypeStruct((2, 8, ROWS, 256), BF),
        ],
        scratch_shapes=[
            VMEM((4, ROWS, D), BF),
            VMEM((4, 4, ROWS, HEAD_DIM), BF),
            VMEM((2048, HEAD_DIM), BF),
            VMEM((2048, HEAD_DIM), F32),
            VMEM((2048, HEAD_DIM), F32),
            VMEM((4, 8, ROWS, 256), BF),
            VMEM((3, ROWS, D), BF),
            VMEM((ROWS, D), BF),
            VMEM((2, ROWS, D), BF),
            dma((6,)), dma((6,)), dma((6,)), dma((6,)), dma((4, 4)), dma((4, 4)), dma((4,)), dma((4,)),
            *GridSum.scratch(512, False),
        ],
        compiler_params=pltpu.CompilerParams(collective_id=3, has_side_effects=True, vmem_limit_bytes=61 * MIB),
        cost_estimate=pl.CostEstimate(flops=8 * 10**9, bytes_accessed=20 * MIB, transcendentals=0),
        name="back",
    )(heads, lengths, grad_low, wo_all, ctx_rows, reduced, middle, keep)


def streams_kernel(
    grads, rows_in, w_in, keep_in, hist_in, grad_middle, n_in, inv, gain_q, gain_k, gain_v,
    ds, mixed, newest, sums, summed, keep_out, sib_out,
    hist, hist_sem, rows, weights, g, turned, parts, stage, sc_out, sc_pass, sc_got,
    s_send, s_recv, c_send, c_recv, d_send, d_recv, local, *grid_scratch,
):
    enter([(Y1,), (Y3,), (SIB,), (DIAG,), *X_RING, *Z_RING])
    t = lax.axis_index("tensor")
    part = pl.ds(512, 512)
    grid = GridSum([(keep_in.at[:, :, part], None)], grid_scratch)
    moves = {}
    for a in range(3):
        for s in (2, 1, 3, 0):
            for r in range(4):
                place = pl.multiple_of(flip(t, A_MASKS[r] + 2 * s) * ROWS, ROWS)
                src, dst = grads.at[a, pl.ds(place, ROWS)], g.at[a, s, r]
                if r:
                    c = rcopy(src, dst, c_send.at[a, s, r], c_recv.at[a, s, r], (A_MASKS[r],))
                else:
                    c = pltpu.make_async_copy(src, dst, c_send.at[a, s, r])
                c.start()
                moves[a, s, r] = c
    gains = (gain_q, gain_k, gain_v)
    tiles = ROWS // STEP
    lane = lax.broadcasted_iota(jnp.int32, (STEP, 256), 1)
    own = lax.rem(lane, STEP) == lax.broadcasted_iota(jnp.int32, (STEP, 256), 0)
    column = lax.broadcasted_iota(jnp.int32, (STEP, 128), 1)
    newest[...] = jnp.zeros(newest.shape, F32)

    def tile_load(tile):
        at = pl.ds(pl.multiple_of(tile * STEP, STEP), STEP)
        slot = lax.rem(tile, 2)
        return pltpu.make_async_copy(hist_in.at[:, at], hist.at[slot], hist_sem.at[slot])

    def rows_of_mixing(streams):
        tile_load(jnp.int32(0)).start()

        def step(tile, totals):
            at = pl.ds(pl.multiple_of(tile * STEP, STEP), STEP)

            @pl.when(tile < tiles - 1)
            def _():
                tile_load(tile + 1).start()

            totals, values = list(totals), []
            for i, k in enumerate(streams):
                if k == 3:
                    values.append(grad_middle[at])
                    continue
                grad, normal = rings[k].total(at), n_in[k, at].astype(F32)
                product = grad * normal
                totals[i] = totals[i] + product[:8] + product[8:]
                scaled = grad * gains[k][...]
                mean = jnp.sum(scaled * normal, axis=-1, keepdims=True) * (1.0 / D)
                value = (scaled - normal * mean) * inv[k, at, 0:1]
                ds[k, at] = value.astype(BF)
                values.append(value)
            split = [halves(value) for value in values]
            left = jnp.concatenate([h for h, _ in split] + [m for _, m in split], axis=0)
            tile_load(tile).wait()
            slot = lax.rem(tile, 2)
            product = nt(left, hist[slot, 0 : HISTORY - 1].reshape(256, D))
            last = hist[slot, HISTORY - 1].astype(F32)
            count = len(streams)
            for i, k in enumerate(streams):
                both = product[i * STEP : (i + 1) * STEP] + product[(count + i) * STEP : (count + i + 1) * STEP]
                mixed[k, at] = jnp.where(own, both, 0.0)
                newest[at] = jnp.where(column == k, jnp.sum(values[i] * last, axis=-1, keepdims=True), newest[at])
            return tuple(totals)

        totals = lax.fori_loop(0, tiles, step, (jnp.zeros((8, D), F32),) * len(streams))
        for total, k in zip(totals, streams):
            if k < 3:
                sums[k : k + 1] = jnp.sum(total, axis=0, keepdims=True)

    loads = []
    for a in range(3):
        c = pltpu.make_async_copy(w_in.at[a], weights.at[a], local.at[a])
        c.start()
        loads.append(c)
    for a in range(3):
        loads.append(pltpu.make_async_copy(rows_in.at[a], rows, local.at[3 + a]))
    loads[3].start()
    grid.load()
    rings = [
        Ring(
            lambda s, half, a=a: parts[a, pl.ds({0: 0, 1: 64, 3: 192}[s] + half.start, half.size)],
            sc_out.at[a], sc_pass.at[a], sc_got.at[a], s_send.at[a], s_recv.at[a], (Y1,), (Y3,), ROWS,
        )
        for a in range(3)
    ]

    def left_of(a, s):
        for r in range(4):
            c = moves[a, s, r]
            c.wait_recv() if r else c.wait()
        return jnp.concatenate([g[a, s, r] for r in range(4)], axis=1)

    def opposite(a):
        loads[a].wait()
        weight = jnp.concatenate([weights[a, r] for r in range(4)], axis=1)
        value, ring = nt(left_of(a, 2), weight), rings[a]
        ring.send(0, ring.lo, value[:64], 0)
        ring.send(0, ring.hi, value[64:], 1)

    def neighbours(a):
        weight = jnp.concatenate([weights[a, r] for r in range(4)], axis=1)
        ring = rings[a]
        value = nt(jnp.concatenate([left_of(a, 1), left_of(a, 3), left_of(a, 0)], axis=0), weight)
        ring.send(1, ring.lo, value[:64], 2)
        ring.send(2, ring.hi, value[192:256], 3)
        parts[a, 128:192] = value[64:128]
        parts[a, 192:256] = value[128:192]
        parts[a, 0:128] = value[256:384]

    def weight_gradient(a):
        loads[3 + a].wait()
        turned[...] = rows[...].reshape(512, D).T
        if a < 2:
            loads[4 + a].start()
        grad_w = nn(
            turned[...], jnp.concatenate([g[a, :, r].reshape(512, HEAD_DIM) for r in range(4)], axis=1)
        ).astype(BF)
        for n, r in enumerate((1, 3, 0, 2)):
            for d in range(8):
                block = grad_w[d * 256 : (d + 1) * 256, r * HEAD_DIM : (r + 1) * HEAD_DIM]
                if a < 2:
                    stage[n, d, 0:256, a * 128 : (a + 1) * 128] = block
                else:
                    stage[n, d, 256:384, 0:128] = block[:128]
                    stage[n, d, 256:384, 128:256] = block[128:]

    opposite(0)
    neighbours(0)
    opposite(1)
    grid.begin()
    rings[0].relay()
    neighbours(1)
    opposite(2)
    weight_gradient(0)
    weight_gradient(1)
    rings[1].relay()
    neighbours(2)
    grid.relay()
    weight_gradient(2)
    rings[0].arrive()
    rows_of_mixing((0, 3))
    grid.turn()
    rings[2].relay()
    sends = []
    for n in range(4):
        if n < 2:
            c = rcopy(stage.at[n], sib_out.at[n], d_send.at[n], d_recv.at[n], (SIB,))
        else:
            c = pltpu.make_async_copy(stage.at[n], keep_out.at[n - 2], d_send.at[n])
        c.start()
        sends.append(c)
    grid.relay2()
    rings[1].arrive()
    rows_of_mixing((1,))
    summed[...] = grid.result()
    grid.finish()
    rings[2].arrive()
    rows_of_mixing((2,))
    for ring in rings:
        ring.finish()
    for (a, s, r), c in moves.items():
        if r:
            c.wait_send()
    for c in sends:
        c.wait()


def streams_back(grads, rows, w_all, keep, history, grad_middle, n, inv, gains):
    dma = pltpu.SemaphoreType.DMA
    vm, hbm = pl.BlockSpec(memory_space=VMEM), pl.BlockSpec(memory_space=ANY)
    return pl.pallas_call(
        streams_kernel,
        in_specs=[vm] + [hbm] * 4 + [vm] * 6,
        out_specs=[vm] * 5 + [hbm] * 2,
        out_shape=[
            jax.ShapeDtypeStruct((3, ROWS, D), BF),
            jax.ShapeDtypeStruct((4, ROWS, 256), F32),
            jax.ShapeDtypeStruct((ROWS, 128), F32),
            jax.ShapeDtypeStruct((3, D), F32),
            jax.ShapeDtypeStruct((512, 256), F32),
            jax.ShapeDtypeStruct((2, 8, 384, 256), BF),
            jax.ShapeDtypeStruct((2, 8, 384, 256), BF),
        ],
        scratch_shapes=[
            VMEM((2, HISTORY, STEP, D), BF),
            dma((2,)),
            VMEM((4, ROWS, D), BF),
            VMEM((3, 4, D, HEAD_DIM), BF),
            VMEM((3, 4, 4, ROWS, HEAD_DIM), BF),
            VMEM((D, 512), BF),
            VMEM((3, 256, D), F32),
            VMEM((4, 8, 384, 256), BF),
            VMEM((3, 3, ROWS, D), BF),
            VMEM((3, ROWS, D), BF),
            VMEM((3, 2, ROWS, D), BF),
            dma((3, 6)), dma((3, 6)), dma((3, 4, 4)), dma((3, 4, 4)), dma((4,)), dma((4,)), dma((6,)),
            *GridSum.scratch(512, False),
        ],
        compiler_params=pltpu.CompilerParams(collective_id=4, has_side_effects=True, vmem_limit_bytes=61 * MIB),
        cost_estimate=pl.CostEstimate(flops=8 * 10**9, bytes_accessed=20 * MIB, transcendentals=0),
        name="streams_back",
    )(grads, rows, w_all, keep, history, grad_middle, n, inv, *[x[None] for x in gains])


SMALL_ROWS, SMALL_COLS = 80, D + 128
NEAR = [(m, 0) for m in range(1, 8)]
FAR = [(XN if m // 4 in (1, 3) else 0, (4 if m // 4 in (2, 3) else 0) + m % 4) for m in range(1, 16)]
TILES = 11


def finish_kernel(
    hist_in, mixed, newest, sums, pre, mix_gain, mix_first, mix_second, gain_mlp,
    keep_q, sib_q, keep_o, sib_o,
    extra, summed, small_out,
    hist, pack, acc, acc1, near_out, near_got, far_out, far_got,
    res, hist_sem, r_send, r_recv, a_send, a_recv, *grid_scratch,
):
    load = pltpu.make_async_copy(hist_in.at[HISTORY - 1], hist, hist_sem)
    load.start()
    enter(NEAR + FAR)
    grid = GridSum([(keep_q, sib_q), (keep_o, sib_o)], grid_scratch)
    grid.load()
    t, dp = lax.axis_index("tensor"), lax.axis_index("dp")
    near = lax.rem(t, 8)
    far = 4 * (2 * lax.div(dp, 4) + lax.div(t, 8)) + lax.rem(dp, 4)
    grid.begin()
    load.wait()

    place = lax.broadcasted_iota(jnp.int32, (256, MIX), 1)
    entry = lax.div(lax.broadcasted_iota(jnp.int32, (256, MIX), 0), STEP)
    column = lax.broadcasted_iota(jnp.int32, (ROWS, MIX), 1)
    grad_mixing = jnp.zeros((ROWS, MIX), F32)
    for k in range(STREAMS):
        gathered = exact(mixed[k], (place == entry + k * HISTORY).astype(F32), ((1,), (0,)))
        grad_mixing = grad_mixing + gathered
        grad_mixing = jnp.where(column == k * HISTORY + HISTORY - 1, newest[:, k : k + 1], grad_mixing)
    hidden, slope = gelu_parts(pre[...])
    last = hist[...].astype(F32)
    inverse = lax.rsqrt(jnp.mean(last * last, axis=-1, keepdims=True) + NORM_EPS)
    normal = last * inverse
    grad_pre = exact(grad_mixing, mix_second[...], ((1,), (1,))) * slope
    pack[...] = jnp.zeros(pack.shape, F32)
    pack[0:MIX, 0:D] = exact(grad_pre, normal * mix_gain[...], ((0,), (0,)))
    pack[0:MIX, D : D + MIX] = exact(hidden, grad_mixing, ((0,), (0,)))
    grad_latest = exact(grad_pre, mix_first[...], ((1,), (0,)))
    pack[68:69, 0:D] = jnp.sum(grad_latest * normal, axis=0, keepdims=True)
    pack[69:72, 0:D] = sums[...]
    pack[72:73, 0:D] = gain_mlp[...]
    pack[68:69, D : D + MIX] = jnp.sum(grad_mixing, axis=0, keepdims=True)
    scaled = grad_latest * mix_gain[...]
    extra[...] = inverse * (scaled - normal * jnp.mean(scaled * normal, axis=-1, keepdims=True))
    acc[7, TILES - 3 : TILES] = jnp.zeros((3, 16, 128), F32)
    acc1[TILES:16] = jnp.zeros((16 - TILES, 16, 128), F32)
    columns = SMALL_COLS // 128
    for i in range(SMALL_ROWS // 16):
        for j in range(columns):
            b = i * columns + j
            acc[b // TILES, b % TILES] = pack[i * 16 : (i + 1) * 16, j * 128 : (j + 1) * 128]

    def exchange(targets, sources, places, level):
        copies = []
        for i, target in enumerate(targets):
            c = rcopy(sources(i), places(i), level[0].at[i], level[1].at[i], target)
            c.start()
            copies.append(c)
        return copies

    near_out[...] = acc[...].astype(BF)
    copies = exchange(NEAR, lambda i: near_out.at[flip(near, i + 1)], lambda i: near_got.at[i], (r_send.at[0], r_recv.at[0]))
    grid.relay()
    for c in copies:
        c.wait()
    total = acc[near]
    for i in range(7):
        total = total + near_got[i].astype(F32)
    acc1[0:TILES] = total
    far_out[...] = acc1[...].astype(BF)
    copies = exchange(FAR, lambda i: far_out.at[flip(far, i + 1)], lambda i: far_got.at[i], (r_send.at[1], r_recv.at[1]))
    for c in copies:
        c.wait()
    total = acc1[far]
    for i in range(15):
        total = total + far_got[i].astype(F32)
    res[near, far] = total.astype(BF)
    mine = res.at[near, far]
    copies = exchange(FAR, lambda i: mine, lambda i: mine, (a_send.at[1], a_recv.at[1]))
    grid.turn()
    for c in copies:
        c.wait()
    mine_all = res.at[near, pl.ds(0, TILES)]
    copies = exchange(NEAR, lambda i: mine_all, lambda i: mine_all, (a_send.at[0], a_recv.at[0]))
    grid.relay2()
    for c in copies:
        c.wait()
    for i in range(SMALL_ROWS // 16):
        for j in range(columns):
            b = i * columns + j
            small_out[i * 16 : (i + 1) * 16, j * 128 : (j + 1) * 128] = res[b // TILES, b % TILES].astype(F32)
    summed[...] = grid.result()
    grid.finish()


def finish(history, mixed, newest, sums, pre, mix_gain, mix_first, mix_second, gain_mlp, *packs):
    dma = pltpu.SemaphoreType.DMA
    vm, hbm = pl.BlockSpec(memory_space=VMEM), pl.BlockSpec(memory_space=ANY)
    tile = (16, 128)
    return pl.pallas_call(
        finish_kernel,
        in_specs=[hbm] + [vm] * 8 + [hbm] * 4,
        out_specs=[vm] * 3,
        out_shape=[
            jax.ShapeDtypeStruct((ROWS, D), F32),
            jax.ShapeDtypeStruct((512, 256), F32),
            jax.ShapeDtypeStruct((SMALL_ROWS, SMALL_COLS), F32),
        ],
        scratch_shapes=[
            VMEM((ROWS, D), BF),
            VMEM((SMALL_ROWS, SMALL_COLS), F32),
            VMEM((8, TILES, *tile), F32),
            VMEM((16, *tile), F32),
            VMEM((8, TILES, *tile), BF),
            VMEM((7, TILES, *tile), BF),
            VMEM((16, *tile), BF),
            VMEM((15, *tile), BF),
            VMEM((8, 16, *tile), BF),
            dma(()), dma((2, 15)), dma((2, 15)), dma((2, 15)), dma((2, 15)),
            *GridSum.scratch(512),
        ],
        compiler_params=pltpu.CompilerParams(collective_id=5, has_side_effects=True, vmem_limit_bytes=61 * MIB),
        cost_estimate=pl.CostEstimate(flops=10**9, bytes_accessed=30 * MIB, transcendentals=0),
        name="finish",
    )(history, mixed, newest, sums, pre, mix_gain[None], mix_first.T, mix_second, gain_mlp, *packs)


def last_kernel(
    ds, grad_low, extra, mix, small, sum_a, sum_e, sum_r, low,
    grad_hist, g_first, g_second, g_bias, g_mix, g_query, g_key, g_value, g_mlp, gw_q, gw_k, gw_v, gw_o, gw_e, gw_r, output,
):
    rows = ds.shape[1]

    @pl.when(pl.program_id(0) == 0)
    def _():
        g_first[...] = small[0:MIX, :D]
        g_second[...] = small[0:MIX, D : D + MIX]
        g_bias[...] = small[68:69, D : D + MIX]
        for i, ref in enumerate((g_mix, g_query, g_key, g_value, g_mlp)):
            ref[...] = small[68 + i : 69 + i, :D]
        gw_q[...] = sum_a[:256, :128]
        gw_k[...] = sum_a[:256, 128:]
        gw_v[:128] = sum_a[256:384, :128]
        gw_v[128:] = sum_a[256:384, 128:]
        gw_o[...] = sum_a[384:]
        gw_e[:, :256] = sum_e[:256]
        gw_e[:, 256:] = sum_e[256:]
        gw_r[...] = sum_r[...]
        output[...] = low[...]

    here = mix[...]
    lane = lax.broadcasted_iota(jnp.int32, (rows, 128), 1)
    own = lax.rem(lane, rows) == lax.broadcasted_iota(jnp.int32, (rows, 128), 0)
    stream = lax.rem(lax.div(lane, rows), STREAMS)
    left = []
    for j in range(HISTORY):
        piece = jnp.zeros((rows, 128), F32)
        for k in range(STREAMS):
            i = k * HISTORY + j
            piece = jnp.where(stream == k, here[:, i : i + 1], piece)
        high, low = halves(jnp.where(own, piece, 0.0))
        left.append(jnp.where(lane < 64, high.astype(F32), low.astype(F32)).astype(BF))
    left = jnp.concatenate(left, axis=0)
    for c in range(D // 512):
        cols = slice(c * 512, (c + 1) * 512)
        right = jnp.concatenate([ds[k, :, cols] if k < 3 else grad_low[:, cols] for k in range(STREAMS)], axis=0)
        product = nn(left, jnp.concatenate([right, right], axis=0))
        grad_hist[0 : HISTORY - 1, :, cols] = product[:256].astype(BF).reshape(HISTORY - 1, rows, 512)
        grad_hist[HISTORY - 1, :, cols] = (product[256:] + extra[:, cols]).astype(BF)


def last(ds, grad_low, extra, mix, small, sum_a, sum_e, sum_r, output):
    rows = 16

    def whole(*shape):
        return pl.BlockSpec(shape, lambda i: (0,) * len(shape))

    shapes = [(MIX, D), (MIX, MIX), (1, MIX)] + [(1, D)] * 5
    shapes += [(256, 128)] * 3 + [(128, 256), (256, 512), (512, 256)]
    return pl.pallas_call(
        last_kernel,
        grid=(ROWS // rows,),
        in_specs=[
            pl.BlockSpec((3, rows, D), lambda i: (0, i, 0)),
            pl.BlockSpec((rows, D), lambda i: (i, 0)),
            pl.BlockSpec((rows, D), lambda i: (i, 0)),
            pl.BlockSpec((rows, MIX), lambda i: (i, 0)),
            whole(SMALL_ROWS, SMALL_COLS),
            whole(512, 256),
            whole(512, 256),
            whole(512, 256),
            whole(ROWS, D),
        ],
        out_specs=[pl.BlockSpec((HISTORY, rows, D), lambda i: (0, i, 0))] + [whole(*x) for x in shapes] + [whole(ROWS, D)],
        out_shape=[jax.ShapeDtypeStruct((HISTORY, ROWS, D), BF)]
        + [jax.ShapeDtypeStruct(x, F32) for x in shapes]
        + [jax.ShapeDtypeStruct((ROWS, D), BF)],
        compiler_params=pltpu.CompilerParams(vmem_limit_bytes=61 * MIB),
        name="last",
    )(ds, grad_low, extra, mix, small, sum_a, sum_e, sum_r, output)


def on_device(
    history, cotangent, lengths, mix_gain, mix_first, mix_second, mix_bias,
    gain_query, gain_key, gain_value, gain_mlp, w_query, w_key, w_value, w_output, w_expand, w_reduce,
):
    gains = (gain_query, gain_key, gain_value)
    heads, rows, w_all, wo_all, we_two, cot_all, n, inv, resid, mix, pre = qkv(
        history, cotangent, mix_gain, mix_first, mix_second, mix_bias, gains, w_query, w_key, w_value, w_output, w_expand
    )
    heads = heads.reshape(3, 2048, HEAD_DIM)
    ctx_rows, middle, reduced, keep_mlp, g_gain_mlp, grad_middle, grad_low = mlp(
        heads, lengths, wo_all, resid, gain_mlp, cotangent, cot_all, w_expand, we_two, w_reduce
    )
    output, grads, sum_e, keep_o, sib_o = back(heads, lengths, grad_low, wo_all, ctx_rows, reduced, middle, keep_mlp)
    ds, mixed, newest, sums, sum_r, keep_q, sib_q = streams_back(
        grads, rows, w_all, keep_mlp, history, grad_middle, n, inv, gains
    )
    extra, sum_a, small = finish(
        history, mixed, newest, sums, pre, mix_gain, mix_first, mix_second, g_gain_mlp, keep_q, sib_q, keep_o, sib_o
    )
    outs = last(ds, grad_low, extra, mix, small, sum_a, sum_e, sum_r, output)
    grad_history, g_first, g_second, g_bias, g_mix, g_query, g_key, g_value, g_mlp = outs[:9]
    return (
        outs[15], grad_history, g_mix[0], g_first.T, g_second, g_bias[0], g_query[0], g_key[0], g_value[0], g_mlp[0],
        *outs[9:15],
    )


def solution(mesh):
    rows, cols, both = P("tensor", None), P(None, "tensor"), ("dp", "tensor")
    return jax.shard_map(
        on_device,
        mesh=mesh,
        in_specs=(P(None, both, None), P(both, None)) + (P(),) * 9 + (cols, cols, cols, rows, cols, rows),
        out_specs=(P(both, None), P(None, both, None)) + (P(),) * 8
        + (P("dp", "tensor"),) * 3 + (P("tensor", "dp"), P("dp", "tensor"), P("tensor", "dp")),
        check_vma=False,
    )
```

```python
import functools

import jax
import jax.numpy as jnp
from jax import lax
from jax.experimental import pallas as pl
from jax.experimental.pallas import tpu as pltpu
from jax.sharding import PartitionSpec as P

HEAD_DIM = 128
HISTORY = 17
STREAMS = 4
MIX = HISTORY * STREAMS
D = 2048
ROWS = 128
FF_SHARD = 512
NORM_EPS = 1e-06
MASKED = -1e30
EXPONENT = HEAD_DIM ** (-0.5) * 1.4426950408889634
MESH = pl.DeviceIdType.MESH
BF = jnp.bfloat16
F32 = jnp.float32
VMEM = pltpu.VMEM
ANY = pl.ANY
MIB = 2**20

Y1, Y2, Y3 = 2, 4, 6
SIB, XN, DIAG = 1, 8, 9
A_MASKS = (0, SIB, XN, DIAG)
LO, HI = pl.ds(0, 64), pl.ds(64, 64)


def flip(value, mask):
    for bit in (1, 2, 4, 8):
        if mask & bit:
            value = value + bit - 2 * bit * lax.rem(lax.div(value, bit), 2)
    return value


def dev(t_mask, dp_mask=0):
    return (flip(lax.axis_index("dp"), dp_mask), flip(lax.axis_index("tensor"), t_mask))


def enter(partners):
    barrier = pltpu.get_barrier_semaphore()
    for partner in partners:
        pl.semaphore_signal(barrier, inc=1, device_id=dev(*partner), device_id_type=MESH)
    pl.semaphore_wait(barrier, len(partners))


def rcopy(src, dst, send, recv, target):
    return pltpu.make_async_remote_copy(
        src_ref=src, dst_ref=dst, send_sem=send, recv_sem=recv, device_id=dev(*target), device_id_type=MESH
    )


def nt(a, b):
    return lax.dot_general(a, b, (((1,), (1,)), ((), ())), preferred_element_type=F32)


def tn(a, b):
    return lax.dot_general(a, b, (((0,), (0,)), ((), ())), preferred_element_type=F32)


def nn(a, b):
    return jnp.dot(a, b, preferred_element_type=F32)


class Gather:
    def __init__(self, own, rows, send, recv, slots=(0, 1, 2, 3)):
        def c(i, src, dst, target):
            return rcopy(src, dst, send.at[i], recv.at[i], (target,))

        _, one, two, three = slots
        self.copies = [
            c(0, own.at[LO], rows.at[one, LO], Y1),
            c(1, own.at[HI], rows.at[three, HI], Y3),
            c(2, own.at[HI], rows.at[one, HI], Y1),
            c(3, own.at[LO], rows.at[three, LO], Y3),
            c(4, rows.at[one, LO], rows.at[two, LO], Y3),
            c(5, rows.at[three, HI], rows.at[two, HI], Y1),
        ]

    def start(self):
        for i in range(4):
            self.copies[i].start()

    def forward(self):
        self.copies[0].wait_recv()
        self.copies[4].start()
        self.copies[1].wait_recv()
        self.copies[5].start()

    def arrived(self, slot):
        for i in {1: (2,), 3: (3,), 2: (4, 5)}[slot]:
            self.copies[i].wait_recv()

    def finish(self):
        for c in self.copies:
            c.wait_send()


def halves(value):
    high = value.astype(BF)
    return high, (value - high.astype(F32)).astype(BF)


def exact(a, b, dims):
    (ah, am), (bh, bm) = halves(a), halves(b)

    def dot(x, y):
        return lax.dot_general(x, y, (dims, ((), ())), preferred_element_type=F32)

    return dot(ah, bh) + (dot(ah, bm) + dot(am, bh))


def gelu_parts(x):
    cdf = 0.5 * (1.0 + lax.erf(x * (0.5**0.5)))
    return x * cdf, cdf + x * jnp.exp(-0.5 * x * x) * 0.3989422804014327


STEP = 16
WIDE = 256


def mix_tokens(last, mix_gain, mix_first, mix_second, mix_bias, pre_out, mix_out):
    inverse = lax.rsqrt(jnp.mean(last * last, axis=-1, keepdims=True) + NORM_EPS)
    pre = exact(last * inverse * mix_gain[...], mix_first[...], ((1,), (1,)))
    pre_out[...] = pre
    hidden = gelu_parts(pre)[0]
    mix_out[...] = exact(hidden, mix_second[...], ((1,), (0,))) + mix_bias[...]


def make_streams(at, hist, mix, gains, held, x_out, n_out, inv_out, resid_out):
    here = mix[at]
    lane = lax.broadcasted_iota(jnp.int32, (STEP, 128), 1)
    own = lax.rem(lane, STEP) == lax.broadcasted_iota(jnp.int32, (STEP, 128), 0)
    entry = lax.div(lane, STEP)
    high, low = [], []
    for k in range(STREAMS):
        pieces = []
        for part in range(2):
            piece = jnp.zeros((STEP, 128), F32)
            for j in range(8):
                i = k * HISTORY + part * 8 + j
                piece = jnp.where(entry == j, here[:, i : i + 1], piece)
            pieces.append(jnp.where(own, piece, 0.0))
        h, m = halves(jnp.concatenate(pieces, axis=1))
        high.append(h)
        low.append(m)
    left = jnp.concatenate(high + low, axis=0)
    squares = [jnp.zeros((STEP, 1), F32) for _ in range(3)]
    for c in range(D // 512):
        cols = slice(c * 512, (c + 1) * 512)
        product = nn(left, hist[0 : HISTORY - 1, at, cols].reshape(256, 512))
        newest = hist[HISTORY - 1, at, cols].astype(F32)
        for k in range(STREAMS):
            i = k * HISTORY + HISTORY - 1
            value = product[k * STEP : (k + 1) * STEP] + product[(4 + k) * STEP : (5 + k) * STEP]
            value = value + here[:, i : i + 1] * newest
            if k == 3:
                resid_out[at, cols] = value
            else:
                held[k, :, cols] = value
                squares[k] = squares[k] + jnp.sum(value * value, axis=-1, keepdims=True)
    for k in range(3):
        inverse = lax.rsqrt(squares[k] * (1.0 / D) + NORM_EPS)
        inv_out[k, at] = jnp.broadcast_to(inverse, (STEP, 128))
        normal = held[k] * inverse
        n_out[k, at] = normal.astype(BF)
        x_out[k, at] = (normal * gains[k][...]).astype(BF)


def qkv_kernel(
    hist_in, cot, mix_gain, mix_first, mix_second, mix_bias, gain_q, gain_k, gain_v,
    w_query, w_key, w_value, w_output, w_expand,
    heads, rows_out, w_out, wo_all, we_two, cot_all, n_out, inv_out, resid_out, mix, pre,
    hist, held, x, rows, weights, proj, hist_sem, cot_send, cot_recv, g_send, g_recv, w_send, w_recv, f_send, f_recv, h_send, h_recv, local,
):
    tiles = ROWS // STEP
    latest = pltpu.make_async_copy(hist_in.at[HISTORY - 1], hist.at[HISTORY - 1], hist_sem.at[tiles])
    latest.start()
    older = pl.ds(0, HISTORY - 1)

    def tile_load(tile):
        at = pl.ds(pl.multiple_of(tile * STEP, STEP), STEP)
        return pltpu.make_async_copy(hist_in.at[older, at], hist.at[older, at], hist_sem.at[tile])

    for tile in range(tiles):
        tile_load(tile).start()
    enter([(Y1,), (Y3,), (SIB,), (XN,), (XN, 4), (DIAG,)])
    t = lax.axis_index("tensor")
    left = pl.ds(0, D // 2)
    cot_gather = Gather(cot.at[:, left], cot_all, cot_send, cot_recv, (0, 1, 3, 2))
    cot_gather.start()
    cot_keep = pltpu.make_async_copy(cot.at[:, left], cot_all.at[0], hist_sem.at[tiles + 1])
    cot_keep.start()
    sources = [w_query, w_key, w_value, w_output, w_expand]
    slots = [lambda r, i=i: weights.at[i, r] for i in range(3)]
    slots += [lambda r: wo_all.at[r], lambda r: we_two.at[r - 1]]
    to_sib, to_x, onward = [], [], []
    for i, src in enumerate(sources):
        half = src.shape[0] // 2
        lo, hi = pl.ds(0, half), pl.ds(half, half)
        to_x.append(
            (
                rcopy(src.at[lo], slots[i](2).at[lo], w_send.at[i, 0], w_recv.at[i, 0], (XN,)),
                rcopy(src.at[hi], slots[i](2).at[hi], w_send.at[i, 1], w_recv.at[i, 1], (XN, 4)),
            )
        )
        to_sib.append(rcopy(src, slots[i](1), w_send.at[i, 2], w_recv.at[i, 2], (SIB,)))
        if i < 4:
            onward.append(rcopy(slots[i](2), slots[i](3), f_send.at[i], f_recv.at[i], (SIB,)))
    keep = [pltpu.make_async_copy(sources[i], slots[i](0), local.at[i]) for i in range(4)]
    gathers = [Gather(x.at[a], rows.at[a], g_send.at[a], g_recv.at[a]) for a in range(3)]
    for a in range(3):
        to_x[a][0].start()
        to_x[a][1].start()
        to_sib[a].start()
        keep[a].start()
    latest.wait()
    mix_tokens(hist[HISTORY - 1].astype(F32), mix_gain, mix_first, mix_second, mix_bias, pre, mix)

    @pl.loop(0, tiles)
    def _(tile):
        tile_load(tile).wait()
        at = pl.ds(pl.multiple_of(tile * STEP, STEP), STEP)
        make_streams(at, hist, mix, (gain_q, gain_k, gain_v), held, x, n_out, inv_out, resid_out)

    cot_gather.forward()
    gathers[0].start()
    gathers[1].start()
    for i in (3, 4):
        to_x[i][0].start()
        to_x[i][1].start()
        to_sib[i].start()
    keep[3].start()
    for a in range(3):
        for c in to_x[a]:
            c.wait_recv()
        onward[a].start()
        gathers[a].forward()
        if a == 0:
            gathers[2].start()
    sends = []

    def project(a, s):
        block = x[a] if s == 0 else rows[a, s]
        for p in range(2):
            pair = jnp.concatenate([weights[a, 2 * p], weights[a, 2 * p + 1]], axis=1)
            y = nn(block, pair).astype(BF)
            proj[a, s, 2 * p] = y[:, :128]
            proj[a, s, 2 * p + 1] = y[:, 128:]
        place = flip(t, 2 * s)
        for r in range(4):
            src, dst = proj.at[a, s, r], heads.at[a, place]
            if r == 0:
                c = pltpu.make_async_copy(src, dst, h_send.at[a, s, 0])
            else:
                c = rcopy(src, dst, h_send.at[a, s, r], h_recv.at[a, s, r], (A_MASKS[r],))
            c.start()
            sends.append((r, c))

    for a in range(3):
        keep[a].wait()
        to_sib[a].wait_recv()
        onward[a].wait_recv()
        project(a, 0)
    store = []
    for a in range(3):
        c = pltpu.make_async_copy(weights.at[a], w_out.at[a], local.at[4 + a])
        c.start()
        store.append(c)
        c = pltpu.make_async_copy(x.at[a], rows_out.at[a, 0], local.at[7 + a])
        c.start()
        store.append(c)
    for a in range(3):
        for s in (1, 3):
            gathers[a].arrived(s)
            project(a, s)
    for c in to_x[3]:
        c.wait_recv()
    onward[3].start()
    for a in range(3):
        gathers[a].arrived(2)
        project(a, 2)
        c = pltpu.make_async_copy(rows.at[a, pl.ds(1, 3)], rows_out.at[a, pl.ds(1, 3)], local.at[10 + a])
        c.start()
        store.append(c)
    for s in (1, 3, 2):
        cot_gather.arrived(s)
    cot_keep.wait()
    for g in gathers + [cot_gather]:
        g.finish()
    for r, c in sends:
        if r == 0:
            c.wait()
        else:
            c.wait_send()
    for r, c in sends:
        if r:
            c.wait_recv()
    for i in range(5):
        for c in to_x[i]:
            c.wait_send()
            if i > 3:
                c.wait_recv()
        to_sib[i].wait_send()
        if i > 2:
            to_sib[i].wait_recv()
    for i in range(4):
        onward[i].wait_send()
    onward[3].wait_recv()
    keep[3].wait()
    for c in store:
        c.wait()


def qkv(history, cot, mix_gain, mix_first, mix_second, mix_bias, gains, *weights):
    dma = pltpu.SemaphoreType.DMA
    vm, hbm = pl.BlockSpec(memory_space=VMEM), pl.BlockSpec(memory_space=ANY)
    return pl.pallas_call(
        qkv_kernel,
        in_specs=[hbm] * 2 + [vm] * 7 + [hbm] * 5,
        out_specs=[hbm] * 6 + [vm] * 5,
        out_shape=[
            jax.ShapeDtypeStruct((3, 16, ROWS, HEAD_DIM), BF),
            jax.ShapeDtypeStruct((3, 4, ROWS, D), BF),
            jax.ShapeDtypeStruct((3, 4, D, HEAD_DIM), BF),
            jax.ShapeDtypeStruct((4, HEAD_DIM, D), BF),
            jax.ShapeDtypeStruct((2, D, FF_SHARD), BF),
            jax.ShapeDtypeStruct((4, ROWS, D // 2), BF),
            jax.ShapeDtypeStruct((3, ROWS, D), BF),
            jax.ShapeDtypeStruct((3, ROWS, 128), F32),
            jax.ShapeDtypeStruct((ROWS, D), F32),
            jax.ShapeDtypeStruct((ROWS, MIX), F32),
            jax.ShapeDtypeStruct((ROWS, MIX), F32),
        ],
        scratch_shapes=[
            VMEM((HISTORY, ROWS, D), BF),
            VMEM((3, STEP, D), F32),
            VMEM((3, ROWS, D), BF),
            VMEM((3, 4, ROWS, D), BF),
            VMEM((3, 4, D, HEAD_DIM), BF),
            VMEM((3, 4, 4, ROWS, HEAD_DIM), BF),
            dma((ROWS // STEP + 2,)), dma((6,)), dma((6,)),
            dma((3, 6)), dma((3, 6)), dma((5, 3)), dma((5, 3)), dma((4,)), dma((4,)), dma((3, 4, 4)), dma((3, 4, 4)), dma((13,)),
        ],
        compiler_params=pltpu.CompilerParams(collective_id=1, has_side_effects=True, vmem_limit_bytes=61 * MIB),
        cost_estimate=pl.CostEstimate(flops=6 * 512 * 2048 * 512, bytes_accessed=30 * MIB, transcendentals=0),
        name="qkv",
    )(
        history, cot, mix_gain[None], mix_first.T, mix_second, mix_bias[None], *[g[None] for g in gains], *weights
    )


def first_places(lengths, places):
    group = lax.axis_index("dp")
    first, end = jnp.zeros_like(places), jnp.int32(0)
    for i in range(lengths.shape[1]):
        end = end + lengths[group, i]
        first = jnp.where(places >= end, end, first)
    return first


def attend_kernel(q, k, v, lengths, ctx, hooks):
    tokens, step = q.shape[0], 256
    for i in range(tokens // step):
        if i in hooks:
            hooks[i]()
        length = (i + 1) * step
        at = slice(i * step, length)
        scores = nt(q[at], k[:length])
        key_place = lax.broadcasted_iota(jnp.int32, (step, length), 1)
        query_place = lax.broadcasted_iota(jnp.int32, (step, 1), 0) + i * step
        allowed = (key_place >= first_places(lengths, query_place)) & (key_place <= query_place)
        scores = jnp.where(allowed, scores, MASKED)
        top = jnp.max(scores, axis=-1, keepdims=True)
        e = jnp.exp2((scores - top) * EXPONENT)
        low = (e * (1.0 / jnp.sum(e, axis=-1, keepdims=True))).astype(BF)
        ctx[at] = nn(low, v[:length]).astype(BF)


def attend_back_kernel(q, k, v, gc, lengths, dq, dk, dv, dk_sum, dv_sum, hooks):
    tokens, step = q.shape[0], 256
    scale = HEAD_DIM ** (-0.5)
    k_turned = k[...].astype(F32).T.astype(BF)
    for i in range(tokens // step):
        if i in hooks:
            hooks[i]()
        length = (i + 1) * step
        at = slice(i * step, length)
        scores = nt(k[:length], q[at])
        key_place = lax.broadcasted_iota(jnp.int32, (length, step), 0)
        query_place = lax.broadcasted_iota(jnp.int32, (1, step), 1) + i * step
        allowed = (key_place >= first_places(lengths, query_place)) & (key_place <= query_place)
        scores = jnp.where(allowed, scores, MASKED)
        top = jnp.max(scores, axis=0, keepdims=True)
        e = jnp.exp2((scores - top) * EXPONENT)
        probs = e * (1.0 / jnp.sum(e, axis=0, keepdims=True))
        grad_probs = nt(v[:length], gc[at])
        delta = jnp.sum(grad_probs * probs, axis=0, keepdims=True)
        grad_scores = (probs * (grad_probs - delta)).astype(BF)
        low = probs.astype(BF)
        dq[at] = (nn(k_turned[:, :length], grad_scores) * scale).T.astype(BF)
        key_part = nn(grad_scores, q[at])
        value_part = nn(low, gc[at])
        if i:
            dk_sum[: i * step] += key_part[: i * step]
            dv_sum[: i * step] += value_part[: i * step]
        dk_sum[at] = key_part[i * step :]
        dv_sum[at] = value_part[i * step :]
    dk[...] = (dk_sum[...] * scale).astype(BF)
    dv[...] = dv_sum[...].astype(BF)


def mlp_kernel(
    heads, lengths, gain, wo_in, resid_in, cot, cot_all, w_expand, we_two, w_reduce,
    ctx_rows, middle_out, reduced_out, keep_out, grad_gain, grad_middle, grad_low,
    ctx, we, wr, mlp_rows, cot_rows, act, gexp, parts, stage, sc_out, sc_pass, sc_got,
    mlp_sib, cot_sib, act_sib, gexp_sib, act_turned,
    g_send, g_recv, s_send, s_recv, w_send, w_recv, c_send, c_recv, d_send, d_recv, local, keep_sem, cot_send, cot_recv,
    wo_all, resid, late_sem,
):
    late = [
        pltpu.make_async_copy(wo_in, wo_all, late_sem.at[0]),
        pltpu.make_async_copy(resid_in, resid, late_sem.at[1]),
    ]
    for c in late:
        c.start()
    enter([(Y1,), (Y3,), (SIB,), (XN,), (XN, 4), (DIAG,)])
    t = lax.axis_index("tensor")
    q, k, v = heads.at[0], heads.at[1], heads.at[2]
    slots = (0, 1, 3, 2)
    right = pl.ds(D // 2, D // 2)
    cot_gather = Gather(cot.at[:, right], cot_rows.at[:, :, right], cot_send, cot_recv, slots)
    cot_gather.start()
    half = FF_SHARD // 2
    lo, hi = pl.ds(0, half), pl.ds(half, half)
    loads = [
        pltpu.make_async_copy(w_expand, we.at[0], local.at[0]),
        pltpu.make_async_copy(we_two, we.at[pl.ds(1, 2)], local.at[1]),
        pltpu.make_async_copy(w_reduce, wr.at[0], local.at[2]),
        pltpu.make_async_copy(cot_all, cot_rows.at[:, :, pl.ds(0, D // 2)], local.at[3]),
        pltpu.make_async_copy(cot.at[:, right], cot_rows.at[0, :, right], local.at[4]),
    ]
    for c in loads:
        c.start()
    sib = [
        rcopy(we_two.at[1], we.at[3], w_send.at[0], w_recv.at[0], (SIB,)),
        rcopy(w_reduce, wr.at[1], w_send.at[1], w_recv.at[1], (SIB,)),
        rcopy(wr.at[2], wr.at[3], w_send.at[2], w_recv.at[2], (SIB,)),
    ]
    across = [
        rcopy(w_reduce.at[lo], wr.at[2, lo], w_send.at[3], w_recv.at[3], (XN,)),
        rcopy(w_reduce.at[hi], wr.at[2, hi], w_send.at[4], w_recv.at[4], (XN, 4)),
    ]
    sib[0].start()
    sib[1].start()
    back = {}
    for s in (2, 1, 3, 0):
        for r in range(4):
            place = pl.multiple_of(flip(t, A_MASKS[r] + 2 * s) * ROWS, ROWS)
            src, dst = ctx.at[pl.ds(place, ROWS)], ctx_rows.at[s, r]
            if r:
                back[s, r] = rcopy(src, dst, c_send.at[s, r], c_recv.at[s, r], (A_MASKS[r],))
            else:
                back[s, r] = pltpu.make_async_copy(src, dst, c_send.at[s, r])
    x_low = lax.div(t, 8)

    def start_for(x):
        for own_x, members in ((x, (0, 1)), (1 - x, (2, 3))):

            @pl.when(x_low == own_x)
            def _(members=members):
                for s in (2, 1, 3, 0):
                    for r in members:
                        back[s, r].start()

    attend_kernel(q, k, v, lengths, ctx, {4: lambda: start_for(0)})
    start_for(1)
    cot_gather.forward()
    for c in across:
        c.start()

    def rows_of(s):
        for r in range(4):
            back[s, r].wait_recv() if r else back[s, r].wait()
        return jnp.concatenate([ctx_rows[s, r] for r in range(4)], axis=1)

    for c in late:
        c.wait()
    weight = wo_all[...].reshape(4 * HEAD_DIM, D)

    def ring(index):
        return Ring(
            lambda s, half: parts[{1: 0, 3: 1, 0: 2, 2: 3}[s], half],
            sc_out, sc_pass, sc_got, s_send.at[index], s_recv.at[index], (Y1,), (Y3,), ROWS,
        )

    ring1 = ring(0)
    parts[3] = nn(rows_of(2), weight)
    ring1.opposite()
    three = jnp.concatenate([rows_of(1), rows_of(3), rows_of(0)], axis=0)
    parts[0:3] = nn(three, weight).reshape(3, ROWS, D)
    ring1.neighbours()
    ring1.relay()
    for c in across:
        c.wait_recv()
    sib[2].start()
    for c in loads:
        c.wait()
    ring1.arrive()
    middle = resid[...] + ring1.total(pl.ds(0, ROWS))
    middle_out[...] = middle
    inverse = lax.rsqrt(jnp.mean(middle * middle, axis=-1, keepdims=True) + NORM_EPS)
    mlp_rows[0] = (middle * inverse * gain[...]).astype(BF)
    mlp_gather = Gather(mlp_rows.at[0], mlp_rows, g_send, g_recv, slots)
    mlp_gather.start()
    for s in (1, 3, 2):
        cot_gather.arrived(s)
    shares = [
        rcopy(cot_rows, cot_sib, d_send.at[0], d_recv.at[0], (SIB,)),
        rcopy(mlp_rows, mlp_sib, d_send.at[1], d_recv.at[1], (SIB,)),
    ]
    shares[0].start()
    for c in sib:
        c.wait_recv()

    def block(start, count):
        at, m = pl.ds(start, count), count * ROWS

        @pl.loop(0, 4)
        def _(r):
            expanded = nn(mlp_rows[at].reshape(m, D), we[r])
            grad_active = nt(cot_rows[at].reshape(m, D), wr[r])
            value, slope = gelu_parts(expanded)
            act[r, at] = value.astype(BF).reshape(count, ROWS, FF_SHARD)
            gexp[r, at] = (grad_active * slope).astype(BF).reshape(count, ROWS, FF_SHARD)

    def reduce_rows(start, count):
        at, m = pl.ds(start, count), count * ROWS
        total = nn(act[0, at].reshape(m, FF_SHARD), wr[0])
        for r in range(1, 4):
            total += nn(act[r, at].reshape(m, FF_SHARD), wr[r])
        for i in range(count):
            reduced_out[(0, 1, 3, 2)[start + i]] = total[i * ROWS : (i + 1) * ROWS].astype(BF)

    block(0, 1)
    mlp_gather.forward()
    reduce_rows(0, 1)
    for s in (1, 3):
        mlp_gather.arrived(s)
    block(1, 2)
    mlp_gather.arrived(2)
    shares[1].start()
    block(3, 1)
    for n, r in enumerate((1, 3)):
        shares.append(rcopy(act.at[r], act_sib.at[n], d_send.at[2 + n], d_recv.at[2 + n], (SIB,)))
        shares.append(rcopy(gexp.at[r], gexp_sib.at[n], d_send.at[4 + n], d_recv.at[4 + n], (SIB,)))
    def grad_mlp(start, count):
        at, m = pl.ds(start, count), count * ROWS
        parts[at] = jnp.zeros((count, ROWS, D), F32)

        @pl.loop(0, 4)
        def _(r):
            parts[at] += nt(gexp[r, at].reshape(m, FF_SHARD), we[r]).reshape(count, ROWS, D)

    ring1.finish()
    ring2 = ring(1)
    grad_mlp(3, 1)
    ring2.opposite()
    parts[0:3] = jnp.zeros((3, ROWS, D), F32)

    @pl.loop(0, 4)
    def _(r):
        lhs = jnp.concatenate([gexp[r, 1], gexp[r, 2], gexp[r, 0]], axis=0)
        parts[0:3] += nt(lhs, we[r]).reshape(3, ROWS, D)

    ring2.neighbours()
    for c in shares[2:]:
        c.start()
    ring2.relay()
    reduce_rows(1, 3)
    for c in shares:
        c.wait_recv()
    @pl.loop(0, 8)
    def _(d):
        cols = pl.ds(pl.multiple_of(d * 256, 256), 256)
        own, other = mlp_rows[:, :, cols].reshape(512, 256).T, mlp_sib[:, :, cols].reshape(512, 256).T
        for n, r in enumerate((0, 2)):
            grad_e = nn(own, gexp[r].reshape(512, FF_SHARD)) + nn(other, gexp_sib[n].reshape(512, FF_SHARD))
            for c in range(2):
                stage[n, d, c * 256 : (c + 1) * 256] = grad_e[:, c * 256 : (c + 1) * 256].astype(BF)

    for n, r in enumerate((0, 2)):
        act_turned[n] = jnp.concatenate([act[r].reshape(512, FF_SHARD), act_sib[n].reshape(512, FF_SHARD)], axis=0).T

    @pl.loop(0, 8)
    def _(d):
        cols = pl.ds(pl.multiple_of(d * 256, 256), 256)
        rhs = jnp.concatenate([cot_rows[:, :, cols].reshape(512, 256), cot_sib[:, :, cols].reshape(512, 256)], axis=0)
        for n in range(2):
            stage[n, d, 512:1024] = nn(act_turned[n], rhs).astype(BF)

    keeps = [pltpu.make_async_copy(stage, keep_out, keep_sem)]
    keeps[0].start()
    ring2.arrive()
    got = ring2.total(pl.ds(0, ROWS))
    middle = middle_out[...]
    inverse = lax.rsqrt(jnp.mean(middle * middle, axis=-1, keepdims=True) + NORM_EPS)
    normal = middle * inverse
    grad_gain[...] = jnp.sum(got * normal, axis=0, keepdims=True)
    scaled = got * gain[...]
    grad = cot_rows[0].astype(F32) + inverse * (scaled - normal * jnp.mean(scaled * normal, axis=-1, keepdims=True))
    grad_middle[...] = grad
    grad_low[...] = grad.astype(BF)
    ring2.finish()
    cot_gather.finish()
    mlp_gather.finish()
    for c in sib + across + shares:
        c.wait_send()
    for (s, r), c in back.items():
        if r:
            c.wait_send()
    for c in keeps:
        c.wait()


def mlp(heads, lengths, wo_all, resid, gain_mlp, cot, cot_all, w_expand, we_two, w_reduce):
    dma = pltpu.SemaphoreType.DMA
    vm, hbm, sm = [pl.BlockSpec(memory_space=m) for m in (VMEM, ANY, pltpu.SMEM)]
    return pl.pallas_call(
        mlp_kernel,
        in_specs=[vm, sm, vm] + [hbm] * 7,
        out_specs=[vm, vm, vm, hbm, vm, vm, vm],
        out_shape=[
            jax.ShapeDtypeStruct((4, 4, ROWS, HEAD_DIM), BF),
            jax.ShapeDtypeStruct((ROWS, D), F32),
            jax.ShapeDtypeStruct((4, ROWS, D), BF),
            jax.ShapeDtypeStruct((2, 8, 1024, 256), BF),
            jax.ShapeDtypeStruct((1, D), F32),
            jax.ShapeDtypeStruct((ROWS, D), F32),
            jax.ShapeDtypeStruct((ROWS, D), BF),
        ],
        scratch_shapes=[
            VMEM((2048, HEAD_DIM), BF),
            VMEM((4, D, FF_SHARD), BF),
            VMEM((4, FF_SHARD, D), BF),
            VMEM((4, ROWS, D), BF),
            VMEM((4, ROWS, D), BF),
            VMEM((4, 4, ROWS, FF_SHARD), BF),
            VMEM((4, 4, ROWS, FF_SHARD), BF),
            VMEM((4, ROWS, D), F32),
            VMEM((2, 8, 1024, 256), BF),
            VMEM((3, ROWS, D), BF),
            VMEM((ROWS, D), BF),
            VMEM((2, ROWS, D), BF),
            VMEM((4, ROWS, D), BF),
            VMEM((4, ROWS, D), BF),
            VMEM((2, 4, ROWS, FF_SHARD), BF),
            VMEM((2, 4, ROWS, FF_SHARD), BF),
            VMEM((2, FF_SHARD, 1024), BF),
            dma((6,)), dma((6,)), dma((2, 6)), dma((2, 6)), dma((5,)), dma((5,)), dma((4, 4)), dma((4, 4)),
            dma((6,)), dma((6,)), dma((5,)), dma(()), dma((6,)), dma((6,)),
            VMEM((4, HEAD_DIM, D), BF),
            VMEM((ROWS, D), F32),
            dma((2,)),
        ],
        compiler_params=pltpu.CompilerParams(collective_id=2, has_side_effects=True, vmem_limit_bytes=61 * MIB),
        cost_estimate=pl.CostEstimate(flops=30 * 10**9, bytes_accessed=50 * MIB, transcendentals=0),
        name="mlp",
    )(heads, lengths, gain_mlp[None], wo_all, resid, cot, cot_all, w_expand, we_two, w_reduce)


class Ring:
    def __init__(self, part, out, passed, got, send, recv, near, far, size):
        half = size // 2
        lo, hi = pl.ds(0, half), pl.ds(half, half)

        def c(i, src, dst, target):
            return rcopy(src, dst, send.at[i], recv.at[i], target)

        self.part, self.out, self.passed, self.got, self.lo, self.hi = part, out, passed, got, lo, hi
        self.copies = [
            c(0, out.at[0, lo], passed.at[lo], near),
            c(1, out.at[0, hi], passed.at[hi], far),
            c(2, out.at[1, lo], got.at[0, lo], near),
            c(3, out.at[2, hi], got.at[1, hi], far),
            c(4, out.at[2, lo], got.at[1, lo], far),
            c(5, out.at[1, hi], got.at[0, hi], near),
        ]

    def opposite(self):
        self.send(0, self.lo, self.part(2, self.lo), 0)
        self.send(0, self.hi, self.part(2, self.hi), 1)

    def neighbours(self):
        self.send(1, self.lo, self.part(1, self.lo), 2)
        self.send(2, self.hi, self.part(3, self.hi), 3)

    def begin(self):
        self.opposite()
        self.neighbours()

    def send(self, slot, half, value, i):
        self.out[slot, half] = value.astype(BF)
        self.copies[i].start()

    def relay(self):
        for i, slot, s, half in ((0, 2, 3, self.lo), (1, 1, 1, self.hi)):
            self.copies[i].wait_recv()
            self.out[slot, half] = (self.part(s, half) + self.passed[half].astype(F32)).astype(BF)
            self.copies[4 + i].start()

    def arrive(self):
        for i in (2, 3, 4, 5):
            self.copies[i].wait_recv()

    def total(self, index):
        return self.part(0, index) + self.got[0, index].astype(F32) + self.got[1, index].astype(F32)

    def finish(self):
        for c in self.copies:
            c.wait_send()


X_RING = ((XN,), (XN, 4))
Z_RING = ((0, 1), (0, 3))


class GridSum:
    @staticmethod
    def scratch(rows, pair=True):
        half, dma = rows // 2, pltpu.SemaphoreType.DMA
        return [
            VMEM((2, 8, rows, 256), BF),
            VMEM((2, 8, rows, 256) if pair else (16, 128), BF),
            VMEM((2, 3, 4, half, 256), BF),
            VMEM((2, 4, half, 256), BF),
            VMEM((2, 2, 4, half, 256), BF),
            VMEM((2, 4, half, 256), F32),
            VMEM((2, 3, half, 256), BF),
            VMEM((2, half, 256), BF),
            VMEM((2, 2, half, 256), BF),
            dma((4, 6)),
            dma((4, 6)),
            dma((4,)),
        ]

    def __init__(self, pieces, scratch):
        (self.a, self.b, out1, pass1, got1, self.mid, out2, pass2, got2, send, recv, load) = scratch
        rows = self.a.shape[2]
        self.half = half = rows // 2
        self.loads, start = [], 0
        for i, (kept, given) in enumerate(pieces):
            at = pl.ds(start, kept.shape[2])
            start += kept.shape[2]
            self.loads.append(pltpu.make_async_copy(kept, self.a.at[:, :, at], load.at[2 * i]))
            if given is not None:
                self.loads.append(pltpu.make_async_copy(given, self.b.at[:, :, at], load.at[2 * i + 1]))
        dp = lax.axis_index("dp")
        place = {(sx, sz): flip(dp, (4 if sx in (2, 3) else 0) + sz) for sx in range(4) for sz in range(4)}

        def block(sx, sz, path):
            shard = 0 if sx in (0, 2) else 1
            at = slice(path * half, (path + 1) * half)
            d = place[sx, sz]
            own = self.a[shard, d, at].astype(F32)
            return own if given is None else own + self.b[shard, d, at].astype(F32)

        def span(ds):
            return range(ds.start, ds.start + ds.size)

        def over_x(s, half_):
            return jnp.stack([block(s, z, 0) for z in span(half_)])

        def over_z(s, half_):
            return jnp.stack([block(x, s, 1) for x in span(half_)])

        rings = (X_RING, Z_RING)
        self.first, self.second = [], []
        for path, part in enumerate((over_x, over_z)):
            near, far = rings[path]
            self.first.append(
                Ring(part, out1.at[path], pass1.at[path], got1.at[path], send.at[path], recv.at[path], near, far, 4)
            )
            near, far = rings[1 - path]
            mid = self.mid.at[path]

            def later(s, half_, mid=mid):
                return mid[s, half_]

            self.second.append(
                Ring(
                    later, out2.at[path], pass2.at[path], got2.at[path], send.at[2 + path], recv.at[2 + path], near, far, half
                )
            )

    def load(self):
        for c in self.loads:
            c.start()

    def begin(self):
        for c in self.loads:
            c.wait()
        for ring in self.first:
            ring.begin()

    def relay(self):
        for ring in self.first:
            ring.relay()

    def turn(self):
        for path in range(2):
            ring = self.first[path]
            ring.arrive()
            for s in (2, 1, 3, 0):
                self.mid[path, s] = ring.total(pl.ds(s, 1))[0]
            self.second[path].begin()

    def relay2(self):
        for ring in self.second:
            ring.relay()

    def result(self):
        parts = []
        for ring in self.second:
            ring.arrive()
            parts.append(ring.total(pl.ds(0, self.half)))
        return jnp.concatenate(parts, axis=0)

    def finish(self):
        for ring in self.first + self.second:
            ring.finish()


def back_kernel(
    lengths, grad_low, wo_all, heads_in, ctx_in, reduced_in, middle_in, keep_in,
    output, grads, summed, keep_out, sib_out,
    rows, proj, gc, dk_sum, dv_sum, stage, sc_out, sc_pass, sc_got,
    g_send, g_recv, s_send, s_recv, c_send, c_recv, d_send, d_recv, heads, ctx_rows, reduced, middle, late_sem,
    *grid_scratch,
):
    late = [
        pltpu.make_async_copy(src, dst, late_sem.at[i])
        for i, (src, dst) in enumerate(
            ((heads_in, heads), (ctx_in, ctx_rows), (reduced_in, reduced), (middle_in, middle))
        )
    ]
    for c in late:
        c.start()
    enter([(Y1,), (Y3,), (SIB,), (DIAG,), *X_RING, *Z_RING])
    t = lax.axis_index("tensor")
    gather = Gather(grad_low, rows, g_send, g_recv)
    gather.start()
    part = pl.ds(0, 512)
    grid = GridSum([(keep_in.at[:, :, part], None)], grid_scratch)
    grid.load()
    q, k, v = heads.at[0], heads.at[1], heads.at[2]
    ring = Ring(
        lambda s, half: reduced[s, half].astype(F32), sc_out, sc_pass, sc_got, s_send, s_recv, (Y1,), (Y3,), ROWS
    )
    rows[0] = grad_low[...]
    weight = wo_all[...].reshape(4 * HEAD_DIM, D)
    moves = []

    def project(s):
        y = nt(rows[s], weight).astype(BF)
        place = pl.multiple_of(flip(t, 2 * s) * ROWS, ROWS)
        for r in range(4):
            proj[s, r] = y[:, r * HEAD_DIM : (r + 1) * HEAD_DIM]
            src, dst = proj.at[s, r], gc.at[pl.ds(place, ROWS)]
            if r:
                c = rcopy(src, dst, c_send.at[s, r], c_recv.at[s, r], (A_MASKS[r],))
            else:
                c = pltpu.make_async_copy(src, dst, c_send.at[s, r])
            c.start()
            moves.append((r, c))

    project(0)
    gather.forward()
    for c in late:
        c.wait()
    ring.begin()
    grid.begin()
    for s in (1, 3, 2):
        gather.arrived(s)
        project(s)
    ring.relay()
    grid.relay()
    all_rows = rows[...].reshape(4 * ROWS, D)
    sends = []
    for n, r in enumerate((1, 3, 0, 2)):
        lhs = jnp.concatenate([ctx_rows[s, r] for s in range(4)], axis=0)
        grad_o = tn(lhs, all_rows).astype(BF)
        for d in range(8):
            stage[n, d] = grad_o[:, d * 256 : (d + 1) * 256]
        if n < 2:
            c = rcopy(stage.at[n], sib_out.at[n], d_send.at[n], d_recv.at[n], (SIB,))
        else:
            c = pltpu.make_async_copy(stage.at[n], keep_out.at[n - 2], d_send.at[n])
        c.start()
        sends.append(c)
    for r, c in moves:
        c.wait_recv() if r else c.wait()
    hooks = {4: grid.turn, 7: grid.relay2}
    attend_back_kernel(q, k, v, gc, lengths, grads.at[0], grads.at[1], grads.at[2], dk_sum, dv_sum, hooks)
    summed[...] = grid.result()
    grid.finish()
    ring.arrive()
    output[...] = (middle[...] + ring.total(pl.ds(0, ROWS))).astype(BF)
    gather.finish()
    ring.finish()
    for r, c in moves:
        if r:
            c.wait_send()
    for n, c in enumerate(sends):
        c.wait()


def back(heads, lengths, grad_low, wo_all, ctx_rows, reduced, middle, keep):
    dma = pltpu.SemaphoreType.DMA
    vm, hbm, sm = [pl.BlockSpec(memory_space=m) for m in (VMEM, ANY, pltpu.SMEM)]
    return pl.pallas_call(
        back_kernel,
        in_specs=[sm, vm, vm] + [hbm] * 5,
        out_specs=[vm, vm, vm, hbm, hbm],
        out_shape=[
            jax.ShapeDtypeStruct((ROWS, D), BF),
            jax.ShapeDtypeStruct((3, 2048, HEAD_DIM), BF),
            jax.ShapeDtypeStruct((512, 256), F32),
            jax.ShapeDtypeStruct((2, 8, ROWS, 256), BF),
            jax.ShapeDtypeStruct((2, 8, ROWS, 256), BF),
        ],
        scratch_shapes=[
            VMEM((4, ROWS, D), BF),
            VMEM((4, 4, ROWS, HEAD_DIM), BF),
            VMEM((2048, HEAD_DIM), BF),
            VMEM((2048, HEAD_DIM), F32),
            VMEM((2048, HEAD_DIM), F32),
            VMEM((4, 8, ROWS, 256), BF),
            VMEM((3, ROWS, D), BF),
            VMEM((ROWS, D), BF),
            VMEM((2, ROWS, D), BF),
            dma((6,)), dma((6,)), dma((6,)), dma((6,)), dma((4, 4)), dma((4, 4)), dma((4,)), dma((4,)),
            VMEM((3, 2048, HEAD_DIM), BF),
            VMEM((4, 4, ROWS, HEAD_DIM), BF),
            VMEM((4, ROWS, D), BF),
            VMEM((ROWS, D), F32),
            dma((4,)),
            *GridSum.scratch(512, False),
        ],
        compiler_params=pltpu.CompilerParams(collective_id=3, has_side_effects=True, vmem_limit_bytes=61 * MIB),
        cost_estimate=pl.CostEstimate(flops=8 * 10**9, bytes_accessed=20 * MIB, transcendentals=0),
        name="back",
    )(lengths, grad_low, wo_all, heads, ctx_rows, reduced, middle, keep)


def streams_kernel(
    grads, rows_in, w_in, keep_in, hist_in, middle_in, normal_in, inv, gain_q, gain_k, gain_v,
    ds, mixed, newest, sums, summed, keep_out, sib_out,
    hist, hist_sem, rows, weights, g, turned, parts, stage, sc_out, sc_pass, sc_got,
    s_send, s_recv, c_send, c_recv, d_send, d_recv, local, grad_middle, n_in, late_sem, *grid_scratch,
):
    late = [
        pltpu.make_async_copy(middle_in, grad_middle, late_sem.at[0]),
        pltpu.make_async_copy(normal_in, n_in, late_sem.at[1]),
    ]
    for c in late:
        c.start()
    enter([(Y1,), (Y3,), (SIB,), (DIAG,), *X_RING, *Z_RING])
    t = lax.axis_index("tensor")
    part = pl.ds(512, 512)
    grid = GridSum([(keep_in.at[:, :, part], None)], grid_scratch)
    moves = {}
    for a in range(3):
        for s in (2, 1, 3, 0):
            for r in range(4):
                place = pl.multiple_of(flip(t, A_MASKS[r] + 2 * s) * ROWS, ROWS)
                src, dst = grads.at[a, pl.ds(place, ROWS)], g.at[a, s, r]
                if r:
                    c = rcopy(src, dst, c_send.at[a, s, r], c_recv.at[a, s, r], (A_MASKS[r],))
                else:
                    c = pltpu.make_async_copy(src, dst, c_send.at[a, s, r])
                c.start()
                moves[a, s, r] = c
    gains = (gain_q, gain_k, gain_v)
    tiles = ROWS // STEP
    lane = lax.broadcasted_iota(jnp.int32, (STEP, 256), 1)
    own = lax.rem(lane, STEP) == lax.broadcasted_iota(jnp.int32, (STEP, 256), 0)
    column = lax.broadcasted_iota(jnp.int32, (STEP, 128), 1)
    newest[...] = jnp.zeros(newest.shape, F32)

    def tile_load(tile):
        at = pl.ds(pl.multiple_of(tile * STEP, STEP), STEP)
        slot = lax.rem(tile, 2)
        return pltpu.make_async_copy(hist_in.at[:, at], hist.at[slot], hist_sem.at[slot])

    def rows_of_mixing(streams):
        tile_load(jnp.int32(0)).start()

        def step(tile, totals):
            at = pl.ds(pl.multiple_of(tile * STEP, STEP), STEP)

            @pl.when(tile < tiles - 1)
            def _():
                tile_load(tile + 1).start()

            totals, values = list(totals), []
            for i, k in enumerate(streams):
                if k == 3:
                    values.append(grad_middle[at])
                    continue
                grad, normal = rings[k].total(at), n_in[k, at].astype(F32)
                product = grad * normal
                totals[i] = totals[i] + product[:8] + product[8:]
                scaled = grad * gains[k][...]
                mean = jnp.sum(scaled * normal, axis=-1, keepdims=True) * (1.0 / D)
                value = (scaled - normal * mean) * inv[k, at, 0:1]
                ds[k, at] = value.astype(BF)
                values.append(value)
            split = [halves(value) for value in values]
            left = jnp.concatenate([h for h, _ in split] + [m for _, m in split], axis=0)
            tile_load(tile).wait()
            slot = lax.rem(tile, 2)
            product = nt(left, hist[slot, 0 : HISTORY - 1].reshape(256, D))
            last = hist[slot, HISTORY - 1].astype(F32)
            count = len(streams)
            for i, k in enumerate(streams):
                both = product[i * STEP : (i + 1) * STEP] + product[(count + i) * STEP : (count + i + 1) * STEP]
                mixed[k, at] = jnp.where(own, both, 0.0)
                newest[at] = jnp.where(column == k, jnp.sum(values[i] * last, axis=-1, keepdims=True), newest[at])
            return tuple(totals)

        totals = lax.fori_loop(0, tiles, step, (jnp.zeros((8, D), F32),) * len(streams))
        for total, k in zip(totals, streams):
            if k < 3:
                sums[k : k + 1] = jnp.sum(total, axis=0, keepdims=True)

    loads = []
    for a in range(3):
        c = pltpu.make_async_copy(w_in.at[a], weights.at[a], local.at[a])
        c.start()
        loads.append(c)
    for a in range(3):
        loads.append(pltpu.make_async_copy(rows_in.at[a], rows, local.at[3 + a]))
    loads[3].start()
    grid.load()
    rings = [
        Ring(
            lambda s, half, a=a: parts[a, pl.ds({0: 0, 1: 64, 3: 192}[s] + half.start, half.size)],
            sc_out.at[a], sc_pass.at[a], sc_got.at[a], s_send.at[a], s_recv.at[a], (Y1,), (Y3,), ROWS,
        )
        for a in range(3)
    ]

    def left_of(a, s):
        for r in range(4):
            c = moves[a, s, r]
            c.wait_recv() if r else c.wait()
        return jnp.concatenate([g[a, s, r] for r in range(4)], axis=1)

    def opposite(a):
        loads[a].wait()
        weight = jnp.concatenate([weights[a, r] for r in range(4)], axis=1)
        value, ring = nt(left_of(a, 2), weight), rings[a]
        ring.send(0, ring.lo, value[:64], 0)
        ring.send(0, ring.hi, value[64:], 1)

    def neighbours(a):
        weight = jnp.concatenate([weights[a, r] for r in range(4)], axis=1)
        ring = rings[a]
        value = nt(jnp.concatenate([left_of(a, 1), left_of(a, 3), left_of(a, 0)], axis=0), weight)
        ring.send(1, ring.lo, value[:64], 2)
        ring.send(2, ring.hi, value[192:256], 3)
        parts[a, 128:192] = value[64:128]
        parts[a, 192:256] = value[128:192]
        parts[a, 0:128] = value[256:384]

    def weight_gradient(a):
        loads[3 + a].wait()
        turned[...] = rows[...].reshape(512, D).T
        if a < 2:
            loads[4 + a].start()
        grad_w = nn(
            turned[...], jnp.concatenate([g[a, :, r].reshape(512, HEAD_DIM) for r in range(4)], axis=1)
        ).astype(BF)
        for n, r in enumerate((1, 3, 0, 2)):
            for d in range(8):
                block = grad_w[d * 256 : (d + 1) * 256, r * HEAD_DIM : (r + 1) * HEAD_DIM]
                if a < 2:
                    stage[n, d, 0:256, a * 128 : (a + 1) * 128] = block
                else:
                    stage[n, d, 256:384, 0:128] = block[:128]
                    stage[n, d, 256:384, 128:256] = block[128:]

    opposite(0)
    neighbours(0)
    opposite(1)
    grid.begin()
    rings[0].relay()
    neighbours(1)
    opposite(2)
    weight_gradient(0)
    weight_gradient(1)
    rings[1].relay()
    neighbours(2)
    grid.relay()
    weight_gradient(2)
    for c in late:
        c.wait()
    rings[0].arrive()
    rows_of_mixing((0, 3))
    grid.turn()
    rings[2].relay()
    sends = []
    for n in range(4):
        if n < 2:
            c = rcopy(stage.at[n], sib_out.at[n], d_send.at[n], d_recv.at[n], (SIB,))
        else:
            c = pltpu.make_async_copy(stage.at[n], keep_out.at[n - 2], d_send.at[n])
        c.start()
        sends.append(c)
    grid.relay2()
    rings[1].arrive()
    rows_of_mixing((1,))
    summed[...] = grid.result()
    grid.finish()
    rings[2].arrive()
    rows_of_mixing((2,))
    for ring in rings:
        ring.finish()
    for (a, s, r), c in moves.items():
        if r:
            c.wait_send()
    for c in sends:
        c.wait()


def streams_back(grads, rows, w_all, keep, history, grad_middle, n, inv, gains):
    dma = pltpu.SemaphoreType.DMA
    vm, hbm = pl.BlockSpec(memory_space=VMEM), pl.BlockSpec(memory_space=ANY)
    return pl.pallas_call(
        streams_kernel,
        in_specs=[vm] + [hbm] * 6 + [vm] * 4,
        out_specs=[vm] * 5 + [hbm] * 2,
        out_shape=[
            jax.ShapeDtypeStruct((3, ROWS, D), BF),
            jax.ShapeDtypeStruct((4, ROWS, 256), F32),
            jax.ShapeDtypeStruct((ROWS, 128), F32),
            jax.ShapeDtypeStruct((3, D), F32),
            jax.ShapeDtypeStruct((512, 256), F32),
            jax.ShapeDtypeStruct((2, 8, 384, 256), BF),
            jax.ShapeDtypeStruct((2, 8, 384, 256), BF),
        ],
        scratch_shapes=[
            VMEM((2, HISTORY, STEP, D), BF),
            dma((2,)),
            VMEM((4, ROWS, D), BF),
            VMEM((3, 4, D, HEAD_DIM), BF),
            VMEM((3, 4, 4, ROWS, HEAD_DIM), BF),
            VMEM((D, 512), BF),
            VMEM((3, 256, D), F32),
            VMEM((4, 8, 384, 256), BF),
            VMEM((3, 3, ROWS, D), BF),
            VMEM((3, ROWS, D), BF),
            VMEM((3, 2, ROWS, D), BF),
            dma((3, 6)), dma((3, 6)), dma((3, 4, 4)), dma((3, 4, 4)), dma((4,)), dma((4,)), dma((6,)),
            VMEM((ROWS, D), F32),
            VMEM((3, ROWS, D), BF),
            dma((2,)),
            *GridSum.scratch(512, False),
        ],
        compiler_params=pltpu.CompilerParams(collective_id=4, has_side_effects=True, vmem_limit_bytes=61 * MIB),
        cost_estimate=pl.CostEstimate(flops=8 * 10**9, bytes_accessed=20 * MIB, transcendentals=0),
        name="streams_back",
    )(grads, rows, w_all, keep, history, grad_middle, n, inv, *[x[None] for x in gains])


SMALL_ROWS, SMALL_COLS = 80, D + 128
NEAR = [(m, 0) for m in range(1, 8)]
FAR = [(XN if m // 4 in (1, 3) else 0, (4 if m // 4 in (2, 3) else 0) + m % 4) for m in range(1, 16)]
TILES = 11


def finish_kernel(
    hist_in, mixed, newest, sums, pre, mix_gain, mix_first, mix_second, gain_mlp,
    keep_q, sib_q, keep_o, sib_o,
    extra, summed, small_out,
    hist, pack, acc, acc1, near_out, near_got, far_out, far_got,
    res, hist_sem, r_send, r_recv, a_send, a_recv, *grid_scratch,
):
    load = pltpu.make_async_copy(hist_in.at[HISTORY - 1], hist, hist_sem)
    load.start()
    enter(NEAR + FAR)
    grid = GridSum([(keep_q, sib_q), (keep_o, sib_o)], grid_scratch)
    grid.load()
    t, dp = lax.axis_index("tensor"), lax.axis_index("dp")
    near = lax.rem(t, 8)
    far = 4 * (2 * lax.div(dp, 4) + lax.div(t, 8)) + lax.rem(dp, 4)
    grid.begin()
    load.wait()

    place = lax.broadcasted_iota(jnp.int32, (256, MIX), 1)
    entry = lax.div(lax.broadcasted_iota(jnp.int32, (256, MIX), 0), STEP)
    column = lax.broadcasted_iota(jnp.int32, (ROWS, MIX), 1)
    grad_mixing = jnp.zeros((ROWS, MIX), F32)
    for k in range(STREAMS):
        gathered = exact(mixed[k], (place == entry + k * HISTORY).astype(F32), ((1,), (0,)))
        grad_mixing = grad_mixing + gathered
        grad_mixing = jnp.where(column == k * HISTORY + HISTORY - 1, newest[:, k : k + 1], grad_mixing)
    hidden, slope = gelu_parts(pre[...])
    last = hist[...].astype(F32)
    inverse = lax.rsqrt(jnp.mean(last * last, axis=-1, keepdims=True) + NORM_EPS)
    normal = last * inverse
    grad_pre = exact(grad_mixing, mix_second[...], ((1,), (1,))) * slope
    pack[...] = jnp.zeros(pack.shape, F32)
    pack[0:MIX, 0:D] = exact(grad_pre, normal * mix_gain[...], ((0,), (0,)))
    pack[0:MIX, D : D + MIX] = exact(hidden, grad_mixing, ((0,), (0,)))
    grad_latest = exact(grad_pre, mix_first[...], ((1,), (0,)))
    pack[68:69, 0:D] = jnp.sum(grad_latest * normal, axis=0, keepdims=True)
    pack[69:72, 0:D] = sums[...]
    pack[72:73, 0:D] = gain_mlp[...]
    pack[68:69, D : D + MIX] = jnp.sum(grad_mixing, axis=0, keepdims=True)
    scaled = grad_latest * mix_gain[...]
    extra[...] = inverse * (scaled - normal * jnp.mean(scaled * normal, axis=-1, keepdims=True))
    acc[7, TILES - 3 : TILES] = jnp.zeros((3, 16, 128), F32)
    acc1[TILES:16] = jnp.zeros((16 - TILES, 16, 128), F32)
    columns = SMALL_COLS // 128
    for i in range(SMALL_ROWS // 16):
        for j in range(columns):
            b = i * columns + j
            acc[b // TILES, b % TILES] = pack[i * 16 : (i + 1) * 16, j * 128 : (j + 1) * 128]

    def exchange(targets, sources, places, level):
        copies = []
        for i, target in enumerate(targets):
            c = rcopy(sources(i), places(i), level[0].at[i], level[1].at[i], target)
            c.start()
            copies.append(c)
        return copies

    near_out[...] = acc[...].astype(BF)
    copies = exchange(NEAR, lambda i: near_out.at[flip(near, i + 1)], lambda i: near_got.at[i], (r_send.at[0], r_recv.at[0]))
    grid.relay()
    for c in copies:
        c.wait()
    total = acc[near]
    for i in range(7):
        total = total + near_got[i].astype(F32)
    acc1[0:TILES] = total
    far_out[...] = acc1[...].astype(BF)
    copies = exchange(FAR, lambda i: far_out.at[flip(far, i + 1)], lambda i: far_got.at[i], (r_send.at[1], r_recv.at[1]))
    for c in copies:
        c.wait()
    total = acc1[far]
    for i in range(15):
        total = total + far_got[i].astype(F32)
    res[near, far] = total.astype(BF)
    mine = res.at[near, far]
    copies = exchange(FAR, lambda i: mine, lambda i: mine, (a_send.at[1], a_recv.at[1]))
    grid.turn()
    for c in copies:
        c.wait()
    mine_all = res.at[near, pl.ds(0, TILES)]
    copies = exchange(NEAR, lambda i: mine_all, lambda i: mine_all, (a_send.at[0], a_recv.at[0]))
    grid.relay2()
    for c in copies:
        c.wait()
    for i in range(SMALL_ROWS // 16):
        for j in range(columns):
            b = i * columns + j
            small_out[i * 16 : (i + 1) * 16, j * 128 : (j + 1) * 128] = res[b // TILES, b % TILES].astype(F32)
    summed[...] = grid.result()
    grid.finish()


def finish(history, mixed, newest, sums, pre, mix_gain, mix_first, mix_second, gain_mlp, *packs):
    dma = pltpu.SemaphoreType.DMA
    vm, hbm = pl.BlockSpec(memory_space=VMEM), pl.BlockSpec(memory_space=ANY)
    tile = (16, 128)
    return pl.pallas_call(
        finish_kernel,
        in_specs=[hbm] + [vm] * 8 + [hbm] * 4,
        out_specs=[vm] * 3,
        out_shape=[
            jax.ShapeDtypeStruct((ROWS, D), F32),
            jax.ShapeDtypeStruct((512, 256), F32),
            jax.ShapeDtypeStruct((SMALL_ROWS, SMALL_COLS), F32),
        ],
        scratch_shapes=[
            VMEM((ROWS, D), BF),
            VMEM((SMALL_ROWS, SMALL_COLS), F32),
            VMEM((8, TILES, *tile), F32),
            VMEM((16, *tile), F32),
            VMEM((8, TILES, *tile), BF),
            VMEM((7, TILES, *tile), BF),
            VMEM((16, *tile), BF),
            VMEM((15, *tile), BF),
            VMEM((8, 16, *tile), BF),
            dma(()), dma((2, 15)), dma((2, 15)), dma((2, 15)), dma((2, 15)),
            *GridSum.scratch(512),
        ],
        compiler_params=pltpu.CompilerParams(collective_id=5, has_side_effects=True, vmem_limit_bytes=61 * MIB),
        cost_estimate=pl.CostEstimate(flops=10**9, bytes_accessed=30 * MIB, transcendentals=0),
        name="finish",
    )(history, mixed, newest, sums, pre, mix_gain[None], mix_first.T, mix_second, gain_mlp, *packs)


def last_kernel(
    ds, grad_low, extra, mix, small, sum_a, sum_e, sum_r, low,
    grad_hist, g_first, g_second, g_bias, g_mix, g_query, g_key, g_value, g_mlp, gw_q, gw_k, gw_v, gw_o, gw_e, gw_r, output,
):
    rows = ds.shape[1]

    @pl.when(pl.program_id(0) == 0)
    def _():
        g_first[...] = small[0:MIX, :D]
        g_second[...] = small[0:MIX, D : D + MIX]
        g_bias[...] = small[68:69, D : D + MIX]
        for i, ref in enumerate((g_mix, g_query, g_key, g_value, g_mlp)):
            ref[...] = small[68 + i : 69 + i, :D]
        gw_q[...] = sum_a[:256, :128]
        gw_k[...] = sum_a[:256, 128:]
        gw_v[:128] = sum_a[256:384, :128]
        gw_v[128:] = sum_a[256:384, 128:]
        gw_o[...] = sum_a[384:]
        gw_e[:, :256] = sum_e[:256]
        gw_e[:, 256:] = sum_e[256:]
        gw_r[...] = sum_r[...]
        output[...] = low[...]

    here = mix[...]
    lane = lax.broadcasted_iota(jnp.int32, (rows, 128), 1)
    own = lax.rem(lane, rows) == lax.broadcasted_iota(jnp.int32, (rows, 128), 0)
    stream = lax.rem(lax.div(lane, rows), STREAMS)
    left = []
    for j in range(HISTORY):
        piece = jnp.zeros((rows, 128), F32)
        for k in range(STREAMS):
            i = k * HISTORY + j
            piece = jnp.where(stream == k, here[:, i : i + 1], piece)
        high, low = halves(jnp.where(own, piece, 0.0))
        left.append(jnp.where(lane < 64, high.astype(F32), low.astype(F32)).astype(BF))
    left = jnp.concatenate(left, axis=0)
    for c in range(D // 512):
        cols = slice(c * 512, (c + 1) * 512)
        right = jnp.concatenate([ds[k, :, cols] if k < 3 else grad_low[:, cols] for k in range(STREAMS)], axis=0)
        product = nn(left, jnp.concatenate([right, right], axis=0))
        grad_hist[0 : HISTORY - 1, :, cols] = product[:256].astype(BF).reshape(HISTORY - 1, rows, 512)
        grad_hist[HISTORY - 1, :, cols] = (product[256:] + extra[:, cols]).astype(BF)


def last(ds, grad_low, extra, mix, small, sum_a, sum_e, sum_r, output):
    rows = 16

    def whole(*shape):
        return pl.BlockSpec(shape, lambda i: (0,) * len(shape))

    shapes = [(MIX, D), (MIX, MIX), (1, MIX)] + [(1, D)] * 5
    shapes += [(256, 128)] * 3 + [(128, 256), (256, 512), (512, 256)]
    return pl.pallas_call(
        last_kernel,
        grid=(ROWS // rows,),
        in_specs=[
            pl.BlockSpec((3, rows, D), lambda i: (0, i, 0)),
            pl.BlockSpec((rows, D), lambda i: (i, 0)),
            pl.BlockSpec((rows, D), lambda i: (i, 0)),
            pl.BlockSpec((rows, MIX), lambda i: (i, 0)),
            whole(SMALL_ROWS, SMALL_COLS),
            whole(512, 256),
            whole(512, 256),
            whole(512, 256),
            whole(ROWS, D),
        ],
        out_specs=[pl.BlockSpec((HISTORY, rows, D), lambda i: (0, i, 0))] + [whole(*x) for x in shapes] + [whole(ROWS, D)],
        out_shape=[jax.ShapeDtypeStruct((HISTORY, ROWS, D), BF)]
        + [jax.ShapeDtypeStruct(x, F32) for x in shapes]
        + [jax.ShapeDtypeStruct((ROWS, D), BF)],
        compiler_params=pltpu.CompilerParams(vmem_limit_bytes=61 * MIB),
        name="last",
    )(ds, grad_low, extra, mix, small, sum_a, sum_e, sum_r, output)


def on_device(
    history, cotangent, lengths, mix_gain, mix_first, mix_second, mix_bias,
    gain_query, gain_key, gain_value, gain_mlp, w_query, w_key, w_value, w_output, w_expand, w_reduce,
):
    gains = (gain_query, gain_key, gain_value)
    heads, rows, w_all, wo_all, we_two, cot_all, n, inv, resid, mix, pre = qkv(
        history, cotangent, mix_gain, mix_first, mix_second, mix_bias, gains, w_query, w_key, w_value, w_output, w_expand
    )
    heads = heads.reshape(3, 2048, HEAD_DIM)
    ctx_rows, middle, reduced, keep_mlp, g_gain_mlp, grad_middle, grad_low = mlp(
        heads, lengths, wo_all, resid, gain_mlp, cotangent, cot_all, w_expand, we_two, w_reduce
    )
    output, grads, sum_e, keep_o, sib_o = back(heads, lengths, grad_low, wo_all, ctx_rows, reduced, middle, keep_mlp)
    ds, mixed, newest, sums, sum_r, keep_q, sib_q = streams_back(
        grads, rows, w_all, keep_mlp, history, grad_middle, n, inv, gains
    )
    extra, sum_a, small = finish(
        history, mixed, newest, sums, pre, mix_gain, mix_first, mix_second, g_gain_mlp, keep_q, sib_q, keep_o, sib_o
    )
    outs = last(ds, grad_low, extra, mix, small, sum_a, sum_e, sum_r, output)
    grad_history, g_first, g_second, g_bias, g_mix, g_query, g_key, g_value, g_mlp = outs[:9]
    return (
        outs[15], grad_history, g_mix[0], g_first.T, g_second, g_bias[0], g_query[0], g_key[0], g_value[0], g_mlp[0],
        *outs[9:15],
    )


def solution(mesh):
    rows, cols, both = P("tensor", None), P(None, "tensor"), ("dp", "tensor")
    return jax.shard_map(
        on_device,
        mesh=mesh,
        in_specs=(P(None, both, None), P(both, None)) + (P(),) * 9 + (cols, cols, cols, rows, cols, rows),
        out_specs=(P(both, None), P(None, both, None)) + (P(),) * 8
        + (P("dp", "tensor"),) * 3 + (P("tensor", "dp"), P("dp", "tensor"), P("tensor", "dp")),
        check_vma=False,
    )
```

```python
import functools

import jax
import jax.numpy as jnp
from jax import lax
from jax.experimental import pallas as pl
from jax.experimental.pallas import tpu as pltpu
from jax.sharding import PartitionSpec as P

HEAD_DIM = 128
HISTORY = 17
STREAMS = 4
MIX = HISTORY * STREAMS
D = 2048
ROWS = 128
FF_SHARD = 512
NORM_EPS = 1e-06
MASKED = -1e30
EXPONENT = HEAD_DIM ** (-0.5) * 1.4426950408889634
MESH = pl.DeviceIdType.MESH
BF = jnp.bfloat16
F32 = jnp.float32
VMEM = pltpu.VMEM
ANY = pl.ANY
MIB = 2**20

Y1, Y2, Y3 = 2, 4, 6
SIB, XN, DIAG = 1, 8, 9
A_MASKS = (0, SIB, XN, DIAG)
LO, HI = pl.ds(0, 64), pl.ds(64, 64)


def flip(value, mask):
    for bit in (1, 2, 4, 8):
        if mask & bit:
            value = value + bit - 2 * bit * lax.rem(lax.div(value, bit), 2)
    return value


def dev(t_mask, dp_mask=0):
    return (flip(lax.axis_index("dp"), dp_mask), flip(lax.axis_index("tensor"), t_mask))


def enter(partners):
    barrier = pltpu.get_barrier_semaphore()
    for partner in partners:
        pl.semaphore_signal(barrier, inc=1, device_id=dev(*partner), device_id_type=MESH)
    pl.semaphore_wait(barrier, len(partners))


def rcopy(src, dst, send, recv, target):
    return pltpu.make_async_remote_copy(
        src_ref=src, dst_ref=dst, send_sem=send, recv_sem=recv, device_id=dev(*target), device_id_type=MESH
    )


def nt(a, b):
    return lax.dot_general(a, b, (((1,), (1,)), ((), ())), preferred_element_type=F32)


def tn(a, b):
    return lax.dot_general(a, b, (((0,), (0,)), ((), ())), preferred_element_type=F32)


def nn(a, b):
    return jnp.dot(a, b, preferred_element_type=F32)


class Gather:
    def __init__(self, own, rows, send, recv, slots=(0, 1, 2, 3)):
        def c(i, src, dst, target):
            return rcopy(src, dst, send.at[i], recv.at[i], (target,))

        _, one, two, three = slots
        self.copies = [
            c(0, own.at[LO], rows.at[one, LO], Y1),
            c(1, own.at[HI], rows.at[three, HI], Y3),
            c(2, own.at[HI], rows.at[one, HI], Y1),
            c(3, own.at[LO], rows.at[three, LO], Y3),
            c(4, rows.at[one, LO], rows.at[two, LO], Y3),
            c(5, rows.at[three, HI], rows.at[two, HI], Y1),
        ]

    def start(self):
        for i in range(4):
            self.copies[i].start()

    def forward(self):
        self.copies[0].wait_recv()
        self.copies[4].start()
        self.copies[1].wait_recv()
        self.copies[5].start()

    def arrived(self, slot):
        for i in {1: (2,), 3: (3,), 2: (4, 5)}[slot]:
            self.copies[i].wait_recv()

    def finish(self):
        for c in self.copies:
            c.wait_send()


def halves(value):
    high = value.astype(BF)
    return high, (value - high.astype(F32)).astype(BF)


def exact(a, b, dims):
    (ah, am), (bh, bm) = halves(a), halves(b)

    def dot(x, y):
        return lax.dot_general(x, y, (dims, ((), ())), preferred_element_type=F32)

    return dot(ah, bh) + (dot(ah, bm) + dot(am, bh))


def gelu_parts(x):
    cdf = 0.5 * (1.0 + lax.erf(x * (0.5**0.5)))
    return x * cdf, cdf + x * jnp.exp(-0.5 * x * x) * 0.3989422804014327


STEP = 16
WIDE = 256


def mix_tokens(last, mix_gain, mix_first, mix_second, mix_bias, pre_out, mix_out):
    inverse = lax.rsqrt(jnp.mean(last * last, axis=-1, keepdims=True) + NORM_EPS)
    pre = exact(last * inverse * mix_gain[...], mix_first[...], ((1,), (1,)))
    pre_out[...] = pre
    hidden = gelu_parts(pre)[0]
    mix_out[...] = exact(hidden, mix_second[...], ((1,), (0,))) + mix_bias[...]


def make_streams(at, hist, mix, gains, held, x_out, n_out, inv_out, resid_out):
    here = mix[at]
    lane = lax.broadcasted_iota(jnp.int32, (STEP, 128), 1)
    own = lax.rem(lane, STEP) == lax.broadcasted_iota(jnp.int32, (STEP, 128), 0)
    entry = lax.div(lane, STEP)
    high, low = [], []
    for k in range(STREAMS):
        pieces = []
        for part in range(2):
            piece = jnp.zeros((STEP, 128), F32)
            for j in range(8):
                i = k * HISTORY + part * 8 + j
                piece = jnp.where(entry == j, here[:, i : i + 1], piece)
            pieces.append(jnp.where(own, piece, 0.0))
        h, m = halves(jnp.concatenate(pieces, axis=1))
        high.append(h)
        low.append(m)
    left = jnp.concatenate(high + low, axis=0)
    squares = [jnp.zeros((STEP, 1), F32) for _ in range(3)]
    for c in range(D // 512):
        cols = slice(c * 512, (c + 1) * 512)
        product = nn(left, hist[0 : HISTORY - 1, at, cols].reshape(256, 512))
        newest = hist[HISTORY - 1, at, cols].astype(F32)
        for k in range(STREAMS):
            i = k * HISTORY + HISTORY - 1
            value = product[k * STEP : (k + 1) * STEP] + product[(4 + k) * STEP : (5 + k) * STEP]
            value = value + here[:, i : i + 1] * newest
            if k == 3:
                resid_out[at, cols] = value
            else:
                held[k, :, cols] = value
                squares[k] = squares[k] + jnp.sum(value * value, axis=-1, keepdims=True)
    for k in range(3):
        inverse = lax.rsqrt(squares[k] * (1.0 / D) + NORM_EPS)
        inv_out[k, at] = jnp.broadcast_to(inverse, (STEP, 128))
        normal = held[k] * inverse
        n_out[k, at] = normal.astype(BF)
        x_out[k, at] = (normal * gains[k][...]).astype(BF)


def qkv_kernel(
    hist_in, cot, mix_gain, mix_first, mix_second, mix_bias, gain_q, gain_k, gain_v,
    w_query, w_key, w_value, w_output, w_expand,
    heads, rows_out, w_out, wo_all, we_two, cot_all, n_out, inv_out, resid_out, mix, pre,
    hist, held, x, rows, weights, proj, hist_sem, cot_send, cot_recv, g_send, g_recv, w_send, w_recv, f_send, f_recv, h_send, h_recv, local,
):
    tiles = ROWS // STEP
    latest = pltpu.make_async_copy(hist_in.at[HISTORY - 1], hist.at[HISTORY - 1], hist_sem.at[tiles])
    latest.start()
    older = pl.ds(0, HISTORY - 1)

    def tile_load(tile):
        at = pl.ds(pl.multiple_of(tile * STEP, STEP), STEP)
        return pltpu.make_async_copy(hist_in.at[older, at], hist.at[older, at], hist_sem.at[tile])

    for tile in range(tiles):
        tile_load(tile).start()
    enter([(Y1,), (Y3,), (SIB,), (XN,), (XN, 4), (DIAG,)])
    t = lax.axis_index("tensor")
    left = pl.ds(0, D // 2)
    cot_gather = Gather(cot.at[:, left], cot_all, cot_send, cot_recv, (0, 1, 3, 2))
    cot_gather.start()
    cot_keep = pltpu.make_async_copy(cot.at[:, left], cot_all.at[0], hist_sem.at[tiles + 1])
    cot_keep.start()
    sources = [w_query, w_key, w_value, w_output, w_expand]
    slots = [lambda r, i=i: weights.at[i, r] for i in range(3)]
    slots += [lambda r: wo_all.at[r], lambda r: we_two.at[r - 1]]
    to_sib, to_x, onward = [], [], []
    for i, src in enumerate(sources):
        half = src.shape[0] // 2
        lo, hi = pl.ds(0, half), pl.ds(half, half)
        to_x.append(
            (
                rcopy(src.at[lo], slots[i](2).at[lo], w_send.at[i, 0], w_recv.at[i, 0], (XN,)),
                rcopy(src.at[hi], slots[i](2).at[hi], w_send.at[i, 1], w_recv.at[i, 1], (XN, 4)),
            )
        )
        to_sib.append(rcopy(src, slots[i](1), w_send.at[i, 2], w_recv.at[i, 2], (SIB,)))
        if i < 4:
            onward.append(rcopy(slots[i](2), slots[i](3), f_send.at[i], f_recv.at[i], (SIB,)))
    keep = [pltpu.make_async_copy(sources[i], slots[i](0), local.at[i]) for i in range(4)]
    gathers = [Gather(x.at[a], rows.at[a], g_send.at[a], g_recv.at[a]) for a in range(3)]
    for a in range(3):
        to_x[a][0].start()
        to_x[a][1].start()
        to_sib[a].start()
        keep[a].start()
    latest.wait()
    mix_tokens(hist[HISTORY - 1].astype(F32), mix_gain, mix_first, mix_second, mix_bias, pre, mix)

    @pl.loop(0, tiles)
    def _(tile):
        tile_load(tile).wait()
        at = pl.ds(pl.multiple_of(tile * STEP, STEP), STEP)
        make_streams(at, hist, mix, (gain_q, gain_k, gain_v), held, x, n_out, inv_out, resid_out)

    cot_gather.forward()
    gathers[0].start()
    gathers[1].start()
    for i in (3, 4):
        to_x[i][0].start()
        to_x[i][1].start()
        to_sib[i].start()
    keep[3].start()
    for a in range(3):
        for c in to_x[a]:
            c.wait_recv()
        onward[a].start()
        gathers[a].forward()
        if a == 0:
            gathers[2].start()
    sends = []

    def project(a, s):
        block = x[a] if s == 0 else rows[a, s]
        for p in range(2):
            pair = jnp.concatenate([weights[a, 2 * p], weights[a, 2 * p + 1]], axis=1)
            y = nn(block, pair).astype(BF)
            proj[a, s, 2 * p] = y[:, :128]
            proj[a, s, 2 * p + 1] = y[:, 128:]
        place = flip(t, 2 * s)
        for r in range(4):
            src, dst = proj.at[a, s, r], heads.at[a, place]
            if r == 0:
                c = pltpu.make_async_copy(src, dst, h_send.at[a, s, 0])
            else:
                c = rcopy(src, dst, h_send.at[a, s, r], h_recv.at[a, s, r], (A_MASKS[r],))
            c.start()
            sends.append((r, c))

    for a in range(3):
        keep[a].wait()
        to_sib[a].wait_recv()
        onward[a].wait_recv()
        project(a, 0)
    store = []
    for a in range(3):
        c = pltpu.make_async_copy(weights.at[a], w_out.at[a], local.at[4 + a])
        c.start()
        store.append(c)
        c = pltpu.make_async_copy(x.at[a], rows_out.at[a, 0], local.at[7 + a])
        c.start()
        store.append(c)
    for a in range(3):
        for s in (1, 3):
            gathers[a].arrived(s)
            project(a, s)
    for c in to_x[3]:
        c.wait_recv()
    onward[3].start()
    for a in range(3):
        gathers[a].arrived(2)
        project(a, 2)
        c = pltpu.make_async_copy(rows.at[a, pl.ds(1, 3)], rows_out.at[a, pl.ds(1, 3)], local.at[10 + a])
        c.start()
        store.append(c)
    for s in (1, 3, 2):
        cot_gather.arrived(s)
    cot_keep.wait()
    for g in gathers + [cot_gather]:
        g.finish()
    for r, c in sends:
        if r == 0:
            c.wait()
        else:
            c.wait_send()
    for r, c in sends:
        if r:
            c.wait_recv()
    for i in range(5):
        for c in to_x[i]:
            c.wait_send()
            if i > 3:
                c.wait_recv()
        to_sib[i].wait_send()
        if i > 2:
            to_sib[i].wait_recv()
    for i in range(4):
        onward[i].wait_send()
    onward[3].wait_recv()
    keep[3].wait()
    for c in store:
        c.wait()


def qkv(history, cot, mix_gain, mix_first, mix_second, mix_bias, gains, *weights):
    dma = pltpu.SemaphoreType.DMA
    vm, hbm = pl.BlockSpec(memory_space=VMEM), pl.BlockSpec(memory_space=ANY)
    return pl.pallas_call(
        qkv_kernel,
        in_specs=[hbm] * 2 + [vm] * 7 + [hbm] * 5,
        out_specs=[hbm] * 6 + [vm] * 5,
        out_shape=[
            jax.ShapeDtypeStruct((3, 16, ROWS, HEAD_DIM), BF),
            jax.ShapeDtypeStruct((3, 4, ROWS, D), BF),
            jax.ShapeDtypeStruct((3, 4, D, HEAD_DIM), BF),
            jax.ShapeDtypeStruct((4, HEAD_DIM, D), BF),
            jax.ShapeDtypeStruct((2, D, FF_SHARD), BF),
            jax.ShapeDtypeStruct((4, ROWS, D // 2), BF),
            jax.ShapeDtypeStruct((3, ROWS, D), BF),
            jax.ShapeDtypeStruct((3, ROWS, 128), F32),
            jax.ShapeDtypeStruct((ROWS, D), F32),
            jax.ShapeDtypeStruct((ROWS, MIX), F32),
            jax.ShapeDtypeStruct((ROWS, MIX), F32),
        ],
        scratch_shapes=[
            VMEM((HISTORY, ROWS, D), BF),
            VMEM((3, STEP, D), F32),
            VMEM((3, ROWS, D), BF),
            VMEM((3, 4, ROWS, D), BF),
            VMEM((3, 4, D, HEAD_DIM), BF),
            VMEM((3, 4, 4, ROWS, HEAD_DIM), BF),
            dma((ROWS // STEP + 2,)), dma((6,)), dma((6,)),
            dma((3, 6)), dma((3, 6)), dma((5, 3)), dma((5, 3)), dma((4,)), dma((4,)), dma((3, 4, 4)), dma((3, 4, 4)), dma((13,)),
        ],
        compiler_params=pltpu.CompilerParams(collective_id=1, has_side_effects=True, vmem_limit_bytes=61 * MIB),
        cost_estimate=pl.CostEstimate(flops=6 * 512 * 2048 * 512, bytes_accessed=30 * MIB, transcendentals=0),
        name="qkv",
    )(
        history, cot, mix_gain[None], mix_first.T, mix_second, mix_bias[None], *[g[None] for g in gains], *weights
    )


def first_places(lengths, places):
    group = lax.axis_index("dp")
    first, end = jnp.zeros_like(places), jnp.int32(0)
    for i in range(lengths.shape[1]):
        end = end + lengths[group, i]
        first = jnp.where(places >= end, end, first)
    return first


def attend_kernel(q, k, v, lengths, ctx, hooks):
    tokens, step = q.shape[0], 256
    for i in range(tokens // step):
        if i in hooks:
            hooks[i]()
        length = (i + 1) * step
        at = slice(i * step, length)
        scores = nt(q[at], k[:length])
        key_place = lax.broadcasted_iota(jnp.int32, (step, length), 1)
        query_place = lax.broadcasted_iota(jnp.int32, (step, 1), 0) + i * step
        allowed = (key_place >= first_places(lengths, query_place)) & (key_place <= query_place)
        scores = jnp.where(allowed, scores, MASKED)
        top = jnp.max(scores, axis=-1, keepdims=True)
        e = jnp.exp2((scores - top) * EXPONENT)
        low = (e * (1.0 / jnp.sum(e, axis=-1, keepdims=True))).astype(BF)
        ctx[at] = nn(low, v[:length]).astype(BF)


def attend_back_kernel(q, k, v, gc, lengths, dq, dk, dv, dk_sum, dv_sum, hooks):
    tokens, step = q.shape[0], 256
    scale = HEAD_DIM ** (-0.5)
    k_turned = k[...].astype(F32).T.astype(BF)
    for i in range(tokens // step):
        if i in hooks:
            hooks[i]()
        length = (i + 1) * step
        at = slice(i * step, length)
        scores = nt(k[:length], q[at])
        key_place = lax.broadcasted_iota(jnp.int32, (length, step), 0)
        query_place = lax.broadcasted_iota(jnp.int32, (1, step), 1) + i * step
        allowed = (key_place >= first_places(lengths, query_place)) & (key_place <= query_place)
        scores = jnp.where(allowed, scores, MASKED)
        top = jnp.max(scores, axis=0, keepdims=True)
        e = jnp.exp2((scores - top) * EXPONENT)
        probs = e * (1.0 / jnp.sum(e, axis=0, keepdims=True))
        grad_probs = nt(v[:length], gc[at])
        delta = jnp.sum(grad_probs * probs, axis=0, keepdims=True)
        grad_scores = (probs * (grad_probs - delta)).astype(BF)
        low = probs.astype(BF)
        dq[at] = (nn(k_turned[:, :length], grad_scores) * scale).T.astype(BF)
        key_part = nn(grad_scores, q[at])
        value_part = nn(low, gc[at])
        if i:
            dk_sum[: i * step] += key_part[: i * step]
            dv_sum[: i * step] += value_part[: i * step]
        dk_sum[at] = key_part[i * step :]
        dv_sum[at] = value_part[i * step :]
    dk[...] = (dk_sum[...] * scale).astype(BF)
    dv[...] = dv_sum[...].astype(BF)


def mlp_kernel(
    heads, lengths, gain, wo_in, resid_in, cot, cot_all, w_expand, we_two, w_reduce,
    ctx_rows, middle_out, reduced_out, keep_out, grad_gain, grad_middle, grad_low,
    ctx, we, wr, mlp_rows, cot_rows, act, gexp, parts, stage, sc_out, sc_pass, sc_got,
    mlp_sib, cot_sib, act_sib, gexp_sib, act_turned,
    g_send, g_recv, s_send, s_recv, w_send, w_recv, c_send, c_recv, d_send, d_recv, local, keep_sem, cot_send, cot_recv,
    wo_all, resid, late_sem,
):
    late = [
        pltpu.make_async_copy(wo_in, wo_all, late_sem.at[0]),
        pltpu.make_async_copy(resid_in, resid, late_sem.at[1]),
    ]
    for c in late:
        c.start()
    enter([(Y1,), (Y3,), (SIB,), (XN,), (XN, 4), (DIAG,)])
    t = lax.axis_index("tensor")
    q, k, v = heads.at[0], heads.at[1], heads.at[2]
    slots = (0, 1, 3, 2)
    right = pl.ds(D // 2, D // 2)
    cot_gather = Gather(cot.at[:, right], cot_rows.at[:, :, right], cot_send, cot_recv, slots)
    cot_gather.start()
    half = FF_SHARD // 2
    lo, hi = pl.ds(0, half), pl.ds(half, half)
    loads = [
        pltpu.make_async_copy(w_expand, we.at[0], local.at[0]),
        pltpu.make_async_copy(we_two, we.at[pl.ds(1, 2)], local.at[1]),
        pltpu.make_async_copy(w_reduce, wr.at[0], local.at[2]),
        pltpu.make_async_copy(cot_all, cot_rows.at[:, :, pl.ds(0, D // 2)], local.at[3]),
        pltpu.make_async_copy(cot.at[:, right], cot_rows.at[0, :, right], local.at[4]),
    ]
    for c in loads:
        c.start()
    sib = [
        rcopy(we_two.at[1], we.at[3], w_send.at[0], w_recv.at[0], (SIB,)),
        rcopy(w_reduce, wr.at[1], w_send.at[1], w_recv.at[1], (SIB,)),
        rcopy(wr.at[2], wr.at[3], w_send.at[2], w_recv.at[2], (SIB,)),
    ]
    across = [
        rcopy(w_reduce.at[lo], wr.at[2, lo], w_send.at[3], w_recv.at[3], (XN,)),
        rcopy(w_reduce.at[hi], wr.at[2, hi], w_send.at[4], w_recv.at[4], (XN, 4)),
    ]
    sib[0].start()
    sib[1].start()
    back = {}
    for s in (2, 1, 3, 0):
        for r in range(4):
            place = pl.multiple_of(flip(t, A_MASKS[r] + 2 * s) * ROWS, ROWS)
            src, dst = ctx.at[pl.ds(place, ROWS)], ctx_rows.at[s, r]
            if r:
                back[s, r] = rcopy(src, dst, c_send.at[s, r], c_recv.at[s, r], (A_MASKS[r],))
            else:
                back[s, r] = pltpu.make_async_copy(src, dst, c_send.at[s, r])
    x_low = lax.div(t, 8)

    def start_for(x):
        for own_x, members in ((x, (0, 1)), (1 - x, (2, 3))):

            @pl.when(x_low == own_x)
            def _(members=members):
                for s in (2, 1, 3, 0):
                    for r in members:
                        back[s, r].start()

    attend_kernel(q, k, v, lengths, ctx, {4: lambda: start_for(0)})
    start_for(1)
    cot_gather.forward()
    for c in across:
        c.start()

    def rows_of(s):
        for r in range(4):
            back[s, r].wait_recv() if r else back[s, r].wait()
        return jnp.concatenate([ctx_rows[s, r] for r in range(4)], axis=1)

    for c in late:
        c.wait()
    weight = wo_all[...].reshape(4 * HEAD_DIM, D)

    def ring(index):
        return Ring(
            lambda s, half: parts[{1: 0, 3: 1, 0: 2, 2: 3}[s], half],
            sc_out, sc_pass, sc_got, s_send.at[index], s_recv.at[index], (Y1,), (Y3,), ROWS,
        )

    ring1 = ring(0)
    parts[3] = nn(rows_of(2), weight)
    ring1.opposite()
    three = jnp.concatenate([rows_of(1), rows_of(3), rows_of(0)], axis=0)
    parts[0:3] = nn(three, weight).reshape(3, ROWS, D)
    ring1.neighbours()
    ring1.relay()
    for c in across:
        c.wait_recv()
    sib[2].start()
    for c in loads:
        c.wait()
    ring1.arrive()
    middle = resid[...] + ring1.total(pl.ds(0, ROWS))
    middle_out[...] = middle
    inverse = lax.rsqrt(jnp.mean(middle * middle, axis=-1, keepdims=True) + NORM_EPS)
    mlp_rows[0] = (middle * inverse * gain[...]).astype(BF)
    mlp_gather = Gather(mlp_rows.at[0], mlp_rows, g_send, g_recv, slots)
    mlp_gather.start()
    for s in (1, 3, 2):
        cot_gather.arrived(s)
    shares = [
        rcopy(cot_rows, cot_sib, d_send.at[0], d_recv.at[0], (SIB,)),
        rcopy(mlp_rows, mlp_sib, d_send.at[1], d_recv.at[1], (SIB,)),
    ]
    shares[0].start()
    for c in sib:
        c.wait_recv()

    def block(start, count):
        at, m = pl.ds(start, count), count * ROWS

        @pl.loop(0, 4)
        def _(r):
            expanded = nn(mlp_rows[at].reshape(m, D), we[r])
            grad_active = nt(cot_rows[at].reshape(m, D), wr[r])
            value, slope = gelu_parts(expanded)
            act[r, at] = value.astype(BF).reshape(count, ROWS, FF_SHARD)
            gexp[r, at] = (grad_active * slope).astype(BF).reshape(count, ROWS, FF_SHARD)

    def reduce_rows(start, count):
        at, m = pl.ds(start, count), count * ROWS
        total = nn(act[0, at].reshape(m, FF_SHARD), wr[0])
        for r in range(1, 4):
            total += nn(act[r, at].reshape(m, FF_SHARD), wr[r])
        for i in range(count):
            reduced_out[(0, 1, 3, 2)[start + i]] = total[i * ROWS : (i + 1) * ROWS].astype(BF)

    block(0, 1)
    mlp_gather.forward()
    reduce_rows(0, 1)
    for s in (1, 3):
        mlp_gather.arrived(s)
    block(1, 2)
    reduce_rows(1, 2)
    mlp_gather.arrived(2)
    shares[1].start()
    block(3, 1)
    for n, r in enumerate((1, 3)):
        shares.append(rcopy(act.at[r], act_sib.at[n], d_send.at[2 + n], d_recv.at[2 + n], (SIB,)))
        shares.append(rcopy(gexp.at[r], gexp_sib.at[n], d_send.at[4 + n], d_recv.at[4 + n], (SIB,)))
    def grad_mlp(start, count):
        at, m = pl.ds(start, count), count * ROWS
        parts[at] = jnp.zeros((count, ROWS, D), F32)

        @pl.loop(0, 4)
        def _(r):
            parts[at] += nt(gexp[r, at].reshape(m, FF_SHARD), we[r]).reshape(count, ROWS, D)

    ring1.finish()
    ring2 = ring(1)
    grad_mlp(3, 1)
    ring2.opposite()
    parts[0:3] = jnp.zeros((3, ROWS, D), F32)

    @pl.loop(0, 4)
    def _(r):
        lhs = jnp.concatenate([gexp[r, 1], gexp[r, 2], gexp[r, 0]], axis=0)
        parts[0:3] += nt(lhs, we[r]).reshape(3, ROWS, D)

    ring2.neighbours()
    for c in shares[2:]:
        c.start()
    ring2.relay()
    reduce_rows(3, 1)
    for c in shares:
        c.wait_recv()
    @pl.loop(0, 8)
    def _(d):
        cols = pl.ds(pl.multiple_of(d * 256, 256), 256)
        own, other = mlp_rows[:, :, cols].reshape(512, 256).T, mlp_sib[:, :, cols].reshape(512, 256).T
        for n, r in enumerate((0, 2)):
            grad_e = nn(own, gexp[r].reshape(512, FF_SHARD)) + nn(other, gexp_sib[n].reshape(512, FF_SHARD))
            for c in range(2):
                stage[n, d, c * 256 : (c + 1) * 256] = grad_e[:, c * 256 : (c + 1) * 256].astype(BF)

    for n, r in enumerate((0, 2)):
        act_turned[n] = jnp.concatenate([act[r].reshape(512, FF_SHARD), act_sib[n].reshape(512, FF_SHARD)], axis=0).T

    @pl.loop(0, 8)
    def _(d):
        cols = pl.ds(pl.multiple_of(d * 256, 256), 256)
        rhs = jnp.concatenate([cot_rows[:, :, cols].reshape(512, 256), cot_sib[:, :, cols].reshape(512, 256)], axis=0)
        for n in range(2):
            stage[n, d, 512:1024] = nn(act_turned[n], rhs).astype(BF)

    keeps = [pltpu.make_async_copy(stage, keep_out, keep_sem)]
    keeps[0].start()
    ring2.arrive()
    got = ring2.total(pl.ds(0, ROWS))
    middle = middle_out[...]
    inverse = lax.rsqrt(jnp.mean(middle * middle, axis=-1, keepdims=True) + NORM_EPS)
    normal = middle * inverse
    grad_gain[...] = jnp.sum(got * normal, axis=0, keepdims=True)
    scaled = got * gain[...]
    grad = cot_rows[0].astype(F32) + inverse * (scaled - normal * jnp.mean(scaled * normal, axis=-1, keepdims=True))
    grad_middle[...] = grad
    grad_low[...] = grad.astype(BF)
    ring2.finish()
    cot_gather.finish()
    mlp_gather.finish()
    for c in sib + across + shares:
        c.wait_send()
    for (s, r), c in back.items():
        if r:
            c.wait_send()
    for c in keeps:
        c.wait()


def mlp(heads, lengths, wo_all, resid, gain_mlp, cot, cot_all, w_expand, we_two, w_reduce):
    dma = pltpu.SemaphoreType.DMA
    vm, hbm, sm = [pl.BlockSpec(memory_space=m) for m in (VMEM, ANY, pltpu.SMEM)]
    return pl.pallas_call(
        mlp_kernel,
        in_specs=[vm, sm, vm] + [hbm] * 7,
        out_specs=[vm, vm, vm, hbm, vm, vm, vm],
        out_shape=[
            jax.ShapeDtypeStruct((4, 4, ROWS, HEAD_DIM), BF),
            jax.ShapeDtypeStruct((ROWS, D), F32),
            jax.ShapeDtypeStruct((4, ROWS, D), BF),
            jax.ShapeDtypeStruct((2, 8, 1024, 256), BF),
            jax.ShapeDtypeStruct((1, D), F32),
            jax.ShapeDtypeStruct((ROWS, D), F32),
            jax.ShapeDtypeStruct((ROWS, D), BF),
        ],
        scratch_shapes=[
            VMEM((2048, HEAD_DIM), BF),
            VMEM((4, D, FF_SHARD), BF),
            VMEM((4, FF_SHARD, D), BF),
            VMEM((4, ROWS, D), BF),
            VMEM((4, ROWS, D), BF),
            VMEM((4, 4, ROWS, FF_SHARD), BF),
            VMEM((4, 4, ROWS, FF_SHARD), BF),
            VMEM((4, ROWS, D), F32),
            VMEM((2, 8, 1024, 256), BF),
            VMEM((3, ROWS, D), BF),
            VMEM((ROWS, D), BF),
            VMEM((2, ROWS, D), BF),
            VMEM((4, ROWS, D), BF),
            VMEM((4, ROWS, D), BF),
            VMEM((2, 4, ROWS, FF_SHARD), BF),
            VMEM((2, 4, ROWS, FF_SHARD), BF),
            VMEM((2, FF_SHARD, 1024), BF),
            dma((6,)), dma((6,)), dma((2, 6)), dma((2, 6)), dma((5,)), dma((5,)), dma((4, 4)), dma((4, 4)),
            dma((6,)), dma((6,)), dma((5,)), dma(()), dma((6,)), dma((6,)),
            VMEM((4, HEAD_DIM, D), BF),
            VMEM((ROWS, D), F32),
            dma((2,)),
        ],
        compiler_params=pltpu.CompilerParams(collective_id=2, has_side_effects=True, vmem_limit_bytes=61 * MIB),
        cost_estimate=pl.CostEstimate(flops=30 * 10**9, bytes_accessed=50 * MIB, transcendentals=0),
        name="mlp",
    )(heads, lengths, gain_mlp[None], wo_all, resid, cot, cot_all, w_expand, we_two, w_reduce)


class Ring:
    def __init__(self, part, out, passed, got, send, recv, near, far, size):
        half = size // 2
        lo, hi = pl.ds(0, half), pl.ds(half, half)

        def c(i, src, dst, target):
            return rcopy(src, dst, send.at[i], recv.at[i], target)

        self.part, self.out, self.passed, self.got, self.lo, self.hi = part, out, passed, got, lo, hi
        self.copies = [
            c(0, out.at[0, lo], passed.at[lo], near),
            c(1, out.at[0, hi], passed.at[hi], far),
            c(2, out.at[1, lo], got.at[0, lo], near),
            c(3, out.at[2, hi], got.at[1, hi], far),
            c(4, out.at[2, lo], got.at[1, lo], far),
            c(5, out.at[1, hi], got.at[0, hi], near),
        ]

    def opposite(self):
        self.send(0, self.lo, self.part(2, self.lo), 0)
        self.send(0, self.hi, self.part(2, self.hi), 1)

    def neighbours(self):
        self.send(1, self.lo, self.part(1, self.lo), 2)
        self.send(2, self.hi, self.part(3, self.hi), 3)

    def begin(self):
        self.opposite()
        self.neighbours()

    def send(self, slot, half, value, i):
        self.out[slot, half] = value.astype(BF)
        self.copies[i].start()

    def relay(self):
        for i, slot, s, half in ((0, 2, 3, self.lo), (1, 1, 1, self.hi)):
            self.copies[i].wait_recv()
            self.out[slot, half] = (self.part(s, half) + self.passed[half].astype(F32)).astype(BF)
            self.copies[4 + i].start()

    def arrive(self):
        for i in (2, 3, 4, 5):
            self.copies[i].wait_recv()

    def total(self, index):
        return self.part(0, index) + self.got[0, index].astype(F32) + self.got[1, index].astype(F32)

    def finish(self):
        for c in self.copies:
            c.wait_send()


X_RING = ((XN,), (XN, 4))
Z_RING = ((0, 1), (0, 3))


class GridSum:
    @staticmethod
    def scratch(rows, pair=True):
        half, dma = rows // 2, pltpu.SemaphoreType.DMA
        return [
            VMEM((2, 8, rows, 256), BF),
            VMEM((2, 8, rows, 256) if pair else (16, 128), BF),
            VMEM((2, 3, 4, half, 256), BF),
            VMEM((2, 4, half, 256), BF),
            VMEM((2, 2, 4, half, 256), BF),
            VMEM((2, 4, half, 256), F32),
            VMEM((2, 3, half, 256), BF),
            VMEM((2, half, 256), BF),
            VMEM((2, 2, half, 256), BF),
            dma((4, 6)),
            dma((4, 6)),
            dma((4,)),
        ]

    def __init__(self, pieces, scratch):
        (self.a, self.b, out1, pass1, got1, self.mid, out2, pass2, got2, send, recv, load) = scratch
        rows = self.a.shape[2]
        self.half = half = rows // 2
        self.loads, start = [], 0
        for i, (kept, given) in enumerate(pieces):
            at = pl.ds(start, kept.shape[2])
            start += kept.shape[2]
            self.loads.append(pltpu.make_async_copy(kept, self.a.at[:, :, at], load.at[2 * i]))
            if given is not None:
                self.loads.append(pltpu.make_async_copy(given, self.b.at[:, :, at], load.at[2 * i + 1]))
        dp = lax.axis_index("dp")
        place = {(sx, sz): flip(dp, (4 if sx in (2, 3) else 0) + sz) for sx in range(4) for sz in range(4)}

        def block(sx, sz, path):
            shard = 0 if sx in (0, 2) else 1
            at = slice(path * half, (path + 1) * half)
            d = place[sx, sz]
            own = self.a[shard, d, at].astype(F32)
            return own if given is None else own + self.b[shard, d, at].astype(F32)

        def span(ds):
            return range(ds.start, ds.start + ds.size)

        def over_x(s, half_):
            return jnp.stack([block(s, z, 0) for z in span(half_)])

        def over_z(s, half_):
            return jnp.stack([block(x, s, 1) for x in span(half_)])

        rings = (X_RING, Z_RING)
        self.first, self.second = [], []
        for path, part in enumerate((over_x, over_z)):
            near, far = rings[path]
            self.first.append(
                Ring(part, out1.at[path], pass1.at[path], got1.at[path], send.at[path], recv.at[path], near, far, 4)
            )
            near, far = rings[1 - path]
            mid = self.mid.at[path]

            def later(s, half_, mid=mid):
                return mid[s, half_]

            self.second.append(
                Ring(
                    later, out2.at[path], pass2.at[path], got2.at[path], send.at[2 + path], recv.at[2 + path], near, far, half
                )
            )

    def load(self):
        for c in self.loads:
            c.start()

    def begin(self):
        for c in self.loads:
            c.wait()
        for ring in self.first:
            ring.begin()

    def relay(self):
        for ring in self.first:
            ring.relay()

    def turn(self):
        for path in range(2):
            ring = self.first[path]
            ring.arrive()
            for s in (2, 1, 3, 0):
                self.mid[path, s] = ring.total(pl.ds(s, 1))[0]
            self.second[path].begin()

    def relay2(self):
        for ring in self.second:
            ring.relay()

    def result(self):
        parts = []
        for ring in self.second:
            ring.arrive()
            parts.append(ring.total(pl.ds(0, self.half)))
        return jnp.concatenate(parts, axis=0)

    def finish(self):
        for ring in self.first + self.second:
            ring.finish()


def back_kernel(
    lengths, grad_low, wo_all, heads_in, ctx_in, reduced_in, middle_in, keep_in,
    output, grads, summed, keep_out, sib_out,
    rows, proj, gc, dk_sum, dv_sum, stage, sc_out, sc_pass, sc_got,
    g_send, g_recv, s_send, s_recv, c_send, c_recv, d_send, d_recv, heads, ctx_rows, reduced, middle, late_sem,
    *grid_scratch,
):
    late = [
        pltpu.make_async_copy(src, dst, late_sem.at[i])
        for i, (src, dst) in enumerate(
            ((heads_in, heads), (ctx_in, ctx_rows), (reduced_in, reduced), (middle_in, middle))
        )
    ]
    for c in late:
        c.start()
    enter([(Y1,), (Y3,), (SIB,), (DIAG,), *X_RING, *Z_RING])
    t = lax.axis_index("tensor")
    gather = Gather(grad_low, rows, g_send, g_recv)
    gather.start()
    part = pl.ds(0, 512)
    grid = GridSum([(keep_in.at[:, :, part], None)], grid_scratch)
    grid.load()
    q, k, v = heads.at[0], heads.at[1], heads.at[2]
    ring = Ring(
        lambda s, half: reduced[s, half].astype(F32), sc_out, sc_pass, sc_got, s_send, s_recv, (Y1,), (Y3,), ROWS
    )
    rows[0] = grad_low[...]
    weight = wo_all[...].reshape(4 * HEAD_DIM, D)
    moves = []

    def project(s):
        y = nt(rows[s], weight).astype(BF)
        place = pl.multiple_of(flip(t, 2 * s) * ROWS, ROWS)
        for r in range(4):
            proj[s, r] = y[:, r * HEAD_DIM : (r + 1) * HEAD_DIM]
            src, dst = proj.at[s, r], gc.at[pl.ds(place, ROWS)]
            if r:
                c = rcopy(src, dst, c_send.at[s, r], c_recv.at[s, r], (A_MASKS[r],))
            else:
                c = pltpu.make_async_copy(src, dst, c_send.at[s, r])
            c.start()
            moves.append((r, c))

    project(0)
    gather.forward()
    for c in late:
        c.wait()
    ring.begin()
    grid.begin()
    for s in (1, 3, 2):
        gather.arrived(s)
        project(s)
    ring.relay()
    grid.relay()
    all_rows = rows[...].reshape(4 * ROWS, D)
    sends = []
    for n, r in enumerate((1, 3, 0, 2)):
        lhs = jnp.concatenate([ctx_rows[s, r] for s in range(4)], axis=0)
        grad_o = tn(lhs, all_rows).astype(BF)
        for d in range(8):
            stage[n, d] = grad_o[:, d * 256 : (d + 1) * 256]
        if n < 2:
            c = rcopy(stage.at[n], sib_out.at[n], d_send.at[n], d_recv.at[n], (SIB,))
        else:
            c = pltpu.make_async_copy(stage.at[n], keep_out.at[n - 2], d_send.at[n])
        c.start()
        sends.append(c)
    for r, c in moves:
        c.wait_recv() if r else c.wait()
    hooks = {4: grid.turn, 7: grid.relay2}
    attend_back_kernel(q, k, v, gc, lengths, grads.at[0], grads.at[1], grads.at[2], dk_sum, dv_sum, hooks)
    summed[...] = grid.result()
    grid.finish()
    ring.arrive()
    output[...] = (middle[...] + ring.total(pl.ds(0, ROWS))).astype(BF)
    gather.finish()
    ring.finish()
    for r, c in moves:
        if r:
            c.wait_send()
    for n, c in enumerate(sends):
        c.wait()


def back(heads, lengths, grad_low, wo_all, ctx_rows, reduced, middle, keep):
    dma = pltpu.SemaphoreType.DMA
    vm, hbm, sm = [pl.BlockSpec(memory_space=m) for m in (VMEM, ANY, pltpu.SMEM)]
    return pl.pallas_call(
        back_kernel,
        in_specs=[sm, vm, vm] + [hbm] * 5,
        out_specs=[vm, vm, vm, hbm, hbm],
        out_shape=[
            jax.ShapeDtypeStruct((ROWS, D), BF),
            jax.ShapeDtypeStruct((3, 2048, HEAD_DIM), BF),
            jax.ShapeDtypeStruct((512, 256), F32),
            jax.ShapeDtypeStruct((2, 8, ROWS, 256), BF),
            jax.ShapeDtypeStruct((2, 8, ROWS, 256), BF),
        ],
        scratch_shapes=[
            VMEM((4, ROWS, D), BF),
            VMEM((4, 4, ROWS, HEAD_DIM), BF),
            VMEM((2048, HEAD_DIM), BF),
            VMEM((2048, HEAD_DIM), F32),
            VMEM((2048, HEAD_DIM), F32),
            VMEM((4, 8, ROWS, 256), BF),
            VMEM((3, ROWS, D), BF),
            VMEM((ROWS, D), BF),
            VMEM((2, ROWS, D), BF),
            dma((6,)), dma((6,)), dma((6,)), dma((6,)), dma((4, 4)), dma((4, 4)), dma((4,)), dma((4,)),
            VMEM((3, 2048, HEAD_DIM), BF),
            VMEM((4, 4, ROWS, HEAD_DIM), BF),
            VMEM((4, ROWS, D), BF),
            VMEM((ROWS, D), F32),
            dma((4,)),
            *GridSum.scratch(512, False),
        ],
        compiler_params=pltpu.CompilerParams(collective_id=3, has_side_effects=True, vmem_limit_bytes=61 * MIB),
        cost_estimate=pl.CostEstimate(flops=8 * 10**9, bytes_accessed=20 * MIB, transcendentals=0),
        name="back",
    )(lengths, grad_low, wo_all, heads, ctx_rows, reduced, middle, keep)


def streams_kernel(
    grads, rows_in, w_in, keep_in, hist_in, middle_in, normal_in, inv, gain_q, gain_k, gain_v,
    ds, mixed, newest, sums, summed, keep_out, sib_out,
    hist, hist_sem, rows, weights, g, turned, parts, stage, sc_out, sc_pass, sc_got,
    s_send, s_recv, c_send, c_recv, d_send, d_recv, local, grad_middle, n_in, late_sem, *grid_scratch,
):
    late = [
        pltpu.make_async_copy(middle_in, grad_middle, late_sem.at[0]),
        pltpu.make_async_copy(normal_in, n_in, late_sem.at[1]),
    ]
    for c in late:
        c.start()
    enter([(Y1,), (Y3,), (SIB,), (DIAG,), *X_RING, *Z_RING])
    t = lax.axis_index("tensor")
    part = pl.ds(512, 512)
    grid = GridSum([(keep_in.at[:, :, part], None)], grid_scratch)
    moves = {}
    for a in range(3):
        for s in (2, 1, 3, 0):
            for r in range(4):
                place = pl.multiple_of(flip(t, A_MASKS[r] + 2 * s) * ROWS, ROWS)
                src, dst = grads.at[a, pl.ds(place, ROWS)], g.at[a, s, r]
                if r:
                    c = rcopy(src, dst, c_send.at[a, s, r], c_recv.at[a, s, r], (A_MASKS[r],))
                else:
                    c = pltpu.make_async_copy(src, dst, c_send.at[a, s, r])
                c.start()
                moves[a, s, r] = c
    gains = (gain_q, gain_k, gain_v)
    tiles = ROWS // STEP
    lane = lax.broadcasted_iota(jnp.int32, (STEP, 256), 1)
    own = lax.rem(lane, STEP) == lax.broadcasted_iota(jnp.int32, (STEP, 256), 0)
    column = lax.broadcasted_iota(jnp.int32, (STEP, 128), 1)
    newest[...] = jnp.zeros(newest.shape, F32)

    def tile_load(tile):
        at = pl.ds(pl.multiple_of(tile * STEP, STEP), STEP)
        slot = lax.rem(tile, 2)
        return pltpu.make_async_copy(hist_in.at[:, at], hist.at[slot], hist_sem.at[slot])

    def rows_of_mixing(streams):
        tile_load(jnp.int32(0)).start()

        def step(tile, totals):
            at = pl.ds(pl.multiple_of(tile * STEP, STEP), STEP)

            @pl.when(tile < tiles - 1)
            def _():
                tile_load(tile + 1).start()

            totals, values = list(totals), []
            for i, k in enumerate(streams):
                if k == 3:
                    values.append(grad_middle[at])
                    continue
                grad, normal = rings[k].total(at), n_in[k, at].astype(F32)
                product = grad * normal
                totals[i] = totals[i] + product[:8] + product[8:]
                scaled = grad * gains[k][...]
                mean = jnp.sum(scaled * normal, axis=-1, keepdims=True) * (1.0 / D)
                value = (scaled - normal * mean) * inv[k, at, 0:1]
                ds[k, at] = value.astype(BF)
                values.append(value)
            split = [halves(value) for value in values]
            left = jnp.concatenate([h for h, _ in split] + [m for _, m in split], axis=0)
            tile_load(tile).wait()
            slot = lax.rem(tile, 2)
            product = nt(left, hist[slot, 0 : HISTORY - 1].reshape(256, D))
            last = hist[slot, HISTORY - 1].astype(F32)
            count = len(streams)
            for i, k in enumerate(streams):
                both = product[i * STEP : (i + 1) * STEP] + product[(count + i) * STEP : (count + i + 1) * STEP]
                mixed[k, at] = jnp.where(own, both, 0.0)
                newest[at] = jnp.where(column == k, jnp.sum(values[i] * last, axis=-1, keepdims=True), newest[at])
            return tuple(totals)

        totals = lax.fori_loop(0, tiles, step, (jnp.zeros((8, D), F32),) * len(streams))
        for total, k in zip(totals, streams):
            if k < 3:
                sums[k : k + 1] = jnp.sum(total, axis=0, keepdims=True)

    loads = []
    for a in range(3):
        c = pltpu.make_async_copy(w_in.at[a], weights.at[a], local.at[a])
        c.start()
        loads.append(c)
    for a in range(3):
        loads.append(pltpu.make_async_copy(rows_in.at[a], rows, local.at[3 + a]))
    loads[3].start()
    grid.load()
    rings = [
        Ring(
            lambda s, half, a=a: parts[a, pl.ds({0: 0, 1: 64, 3: 192}[s] + half.start, half.size)],
            sc_out.at[a], sc_pass.at[a], sc_got.at[a], s_send.at[a], s_recv.at[a], (Y1,), (Y3,), ROWS,
        )
        for a in range(3)
    ]

    def left_of(a, s):
        for r in range(4):
            c = moves[a, s, r]
            c.wait_recv() if r else c.wait()
        return jnp.concatenate([g[a, s, r] for r in range(4)], axis=1)

    def opposite(a):
        loads[a].wait()
        weight = jnp.concatenate([weights[a, r] for r in range(4)], axis=1)
        value, ring = nt(left_of(a, 2), weight), rings[a]
        ring.send(0, ring.lo, value[:64], 0)
        ring.send(0, ring.hi, value[64:], 1)

    def neighbours(a):
        weight = jnp.concatenate([weights[a, r] for r in range(4)], axis=1)
        ring = rings[a]
        value = nt(jnp.concatenate([left_of(a, 1), left_of(a, 3), left_of(a, 0)], axis=0), weight)
        ring.send(1, ring.lo, value[:64], 2)
        ring.send(2, ring.hi, value[192:256], 3)
        parts[a, 128:192] = value[64:128]
        parts[a, 192:256] = value[128:192]
        parts[a, 0:128] = value[256:384]

    def weight_gradient(a):
        loads[3 + a].wait()
        turned[...] = rows[...].reshape(512, D).T
        if a < 2:
            loads[4 + a].start()
        grad_w = nn(
            turned[...], jnp.concatenate([g[a, :, r].reshape(512, HEAD_DIM) for r in range(4)], axis=1)
        ).astype(BF)
        for n, r in enumerate((1, 3, 0, 2)):
            for d in range(8):
                block = grad_w[d * 256 : (d + 1) * 256, r * HEAD_DIM : (r + 1) * HEAD_DIM]
                if a < 2:
                    stage[n, d, 0:256, a * 128 : (a + 1) * 128] = block
                else:
                    stage[n, d, 256:384, 0:128] = block[:128]
                    stage[n, d, 256:384, 128:256] = block[128:]

    opposite(0)
    neighbours(0)
    opposite(1)
    grid.begin()
    rings[0].relay()
    neighbours(1)
    opposite(2)
    weight_gradient(0)
    weight_gradient(1)
    rings[1].relay()
    neighbours(2)
    grid.relay()
    weight_gradient(2)
    for c in late:
        c.wait()
    rings[0].arrive()
    rows_of_mixing((0, 3))
    grid.turn()
    rings[2].relay()
    sends = []
    for n in range(4):
        if n < 2:
            c = rcopy(stage.at[n], sib_out.at[n], d_send.at[n], d_recv.at[n], (SIB,))
        else:
            c = pltpu.make_async_copy(stage.at[n], keep_out.at[n - 2], d_send.at[n])
        c.start()
        sends.append(c)
    grid.relay2()
    rings[1].arrive()
    rows_of_mixing((1,))
    summed[...] = grid.result()
    grid.finish()
    rings[2].arrive()
    rows_of_mixing((2,))
    for ring in rings:
        ring.finish()
    for (a, s, r), c in moves.items():
        if r:
            c.wait_send()
    for c in sends:
        c.wait()


def streams_back(grads, rows, w_all, keep, history, grad_middle, n, inv, gains):
    dma = pltpu.SemaphoreType.DMA
    vm, hbm = pl.BlockSpec(memory_space=VMEM), pl.BlockSpec(memory_space=ANY)
    return pl.pallas_call(
        streams_kernel,
        in_specs=[vm] + [hbm] * 6 + [vm] * 4,
        out_specs=[vm] * 5 + [hbm] * 2,
        out_shape=[
            jax.ShapeDtypeStruct((3, ROWS, D), BF),
            jax.ShapeDtypeStruct((4, ROWS, 256), F32),
            jax.ShapeDtypeStruct((ROWS, 128), F32),
            jax.ShapeDtypeStruct((3, D), F32),
            jax.ShapeDtypeStruct((512, 256), F32),
            jax.ShapeDtypeStruct((2, 8, 384, 256), BF),
            jax.ShapeDtypeStruct((2, 8, 384, 256), BF),
        ],
        scratch_shapes=[
            VMEM((2, HISTORY, STEP, D), BF),
            dma((2,)),
            VMEM((4, ROWS, D), BF),
            VMEM((3, 4, D, HEAD_DIM), BF),
            VMEM((3, 4, 4, ROWS, HEAD_DIM), BF),
            VMEM((D, 512), BF),
            VMEM((3, 256, D), F32),
            VMEM((4, 8, 384, 256), BF),
            VMEM((3, 3, ROWS, D), BF),
            VMEM((3, ROWS, D), BF),
            VMEM((3, 2, ROWS, D), BF),
            dma((3, 6)), dma((3, 6)), dma((3, 4, 4)), dma((3, 4, 4)), dma((4,)), dma((4,)), dma((6,)),
            VMEM((ROWS, D), F32),
            VMEM((3, ROWS, D), BF),
            dma((2,)),
            *GridSum.scratch(512, False),
        ],
        compiler_params=pltpu.CompilerParams(collective_id=4, has_side_effects=True, vmem_limit_bytes=61 * MIB),
        cost_estimate=pl.CostEstimate(flops=8 * 10**9, bytes_accessed=20 * MIB, transcendentals=0),
        name="streams_back",
    )(grads, rows, w_all, keep, history, grad_middle, n, inv, *[x[None] for x in gains])


SMALL_ROWS, SMALL_COLS = 80, D + 128
NEAR = [(m, 0) for m in range(1, 8)]
FAR = [(XN if m // 4 in (1, 3) else 0, (4 if m // 4 in (2, 3) else 0) + m % 4) for m in range(1, 16)]
TILES = 11


def finish_kernel(
    hist_in, mixed, newest, sums, pre, mix_gain, mix_first, mix_second, gain_mlp,
    keep_q, sib_q, keep_o, sib_o,
    extra, summed, small_out,
    hist, pack, acc, acc1, near_out, near_got, far_out, far_got,
    res, hist_sem, r_send, r_recv, a_send, a_recv, *grid_scratch,
):
    load = pltpu.make_async_copy(hist_in.at[HISTORY - 1], hist, hist_sem)
    load.start()
    enter(NEAR + FAR)
    grid = GridSum([(keep_q, sib_q), (keep_o, sib_o)], grid_scratch)
    grid.load()
    t, dp = lax.axis_index("tensor"), lax.axis_index("dp")
    near = lax.rem(t, 8)
    far = 4 * (2 * lax.div(dp, 4) + lax.div(t, 8)) + lax.rem(dp, 4)
    grid.begin()
    load.wait()

    place = lax.broadcasted_iota(jnp.int32, (256, MIX), 1)
    entry = lax.div(lax.broadcasted_iota(jnp.int32, (256, MIX), 0), STEP)
    column = lax.broadcasted_iota(jnp.int32, (ROWS, MIX), 1)
    grad_mixing = jnp.zeros((ROWS, MIX), F32)
    for k in range(STREAMS):
        gathered = exact(mixed[k], (place == entry + k * HISTORY).astype(F32), ((1,), (0,)))
        grad_mixing = grad_mixing + gathered
        grad_mixing = jnp.where(column == k * HISTORY + HISTORY - 1, newest[:, k : k + 1], grad_mixing)
    hidden, slope = gelu_parts(pre[...])
    last = hist[...].astype(F32)
    inverse = lax.rsqrt(jnp.mean(last * last, axis=-1, keepdims=True) + NORM_EPS)
    normal = last * inverse
    grad_pre = exact(grad_mixing, mix_second[...], ((1,), (1,))) * slope
    grid.relay()
    pack[...] = jnp.zeros(pack.shape, F32)
    pack[0:MIX, 0:D] = exact(grad_pre, normal * mix_gain[...], ((0,), (0,)))
    pack[0:MIX, D : D + MIX] = exact(hidden, grad_mixing, ((0,), (0,)))
    grad_latest = exact(grad_pre, mix_first[...], ((1,), (0,)))
    pack[68:69, 0:D] = jnp.sum(grad_latest * normal, axis=0, keepdims=True)
    pack[69:72, 0:D] = sums[...]
    pack[72:73, 0:D] = gain_mlp[...]
    pack[68:69, D : D + MIX] = jnp.sum(grad_mixing, axis=0, keepdims=True)
    scaled = grad_latest * mix_gain[...]
    extra[...] = inverse * (scaled - normal * jnp.mean(scaled * normal, axis=-1, keepdims=True))
    acc[7, TILES - 3 : TILES] = jnp.zeros((3, 16, 128), F32)
    acc1[TILES:16] = jnp.zeros((16 - TILES, 16, 128), F32)
    columns = SMALL_COLS // 128
    for i in range(SMALL_ROWS // 16):
        for j in range(columns):
            b = i * columns + j
            acc[b // TILES, b % TILES] = pack[i * 16 : (i + 1) * 16, j * 128 : (j + 1) * 128]

    def exchange(targets, sources, places, level):
        copies = []
        for i, target in enumerate(targets):
            c = rcopy(sources(i), places(i), level[0].at[i], level[1].at[i], target)
            c.start()
            copies.append(c)
        return copies

    near_out[...] = acc[...].astype(BF)
    copies = exchange(NEAR, lambda i: near_out.at[flip(near, i + 1)], lambda i: near_got.at[i], (r_send.at[0], r_recv.at[0]))
    for c in copies:
        c.wait()
    total = acc[near]
    for i in range(7):
        total = total + near_got[i].astype(F32)
    acc1[0:TILES] = total
    far_out[...] = acc1[...].astype(BF)
    copies = exchange(FAR, lambda i: far_out.at[flip(far, i + 1)], lambda i: far_got.at[i], (r_send.at[1], r_recv.at[1]))
    for c in copies:
        c.wait()
    total = acc1[far]
    for i in range(15):
        total = total + far_got[i].astype(F32)
    res[near, far] = total.astype(BF)
    mine = res.at[near, far]
    copies = exchange(FAR, lambda i: mine, lambda i: mine, (a_send.at[1], a_recv.at[1]))
    grid.turn()
    for c in copies:
        c.wait()
    mine_all = res.at[near, pl.ds(0, TILES)]
    copies = exchange(NEAR, lambda i: mine_all, lambda i: mine_all, (a_send.at[0], a_recv.at[0]))
    grid.relay2()
    for c in copies:
        c.wait()
    for i in range(SMALL_ROWS // 16):
        for j in range(columns):
            b = i * columns + j
            small_out[i * 16 : (i + 1) * 16, j * 128 : (j + 1) * 128] = res[b // TILES, b % TILES].astype(F32)
    summed[...] = grid.result()
    grid.finish()


def finish(history, mixed, newest, sums, pre, mix_gain, mix_first, mix_second, gain_mlp, *packs):
    dma = pltpu.SemaphoreType.DMA
    vm, hbm = pl.BlockSpec(memory_space=VMEM), pl.BlockSpec(memory_space=ANY)
    tile = (16, 128)
    return pl.pallas_call(
        finish_kernel,
        in_specs=[hbm] + [vm] * 8 + [hbm] * 4,
        out_specs=[vm] * 3,
        out_shape=[
            jax.ShapeDtypeStruct((ROWS, D), F32),
            jax.ShapeDtypeStruct((512, 256), F32),
            jax.ShapeDtypeStruct((SMALL_ROWS, SMALL_COLS), F32),
        ],
        scratch_shapes=[
            VMEM((ROWS, D), BF),
            VMEM((SMALL_ROWS, SMALL_COLS), F32),
            VMEM((8, TILES, *tile), F32),
            VMEM((16, *tile), F32),
            VMEM((8, TILES, *tile), BF),
            VMEM((7, TILES, *tile), BF),
            VMEM((16, *tile), BF),
            VMEM((15, *tile), BF),
            VMEM((8, 16, *tile), BF),
            dma(()), dma((2, 15)), dma((2, 15)), dma((2, 15)), dma((2, 15)),
            *GridSum.scratch(512),
        ],
        compiler_params=pltpu.CompilerParams(collective_id=5, has_side_effects=True, vmem_limit_bytes=61 * MIB),
        cost_estimate=pl.CostEstimate(flops=10**9, bytes_accessed=30 * MIB, transcendentals=0),
        name="finish",
    )(history, mixed, newest, sums, pre, mix_gain[None], mix_first.T, mix_second, gain_mlp, *packs)


def last_kernel(
    ds, grad_low, extra, mix, small, sum_a, sum_e, sum_r, low,
    grad_hist, g_first, g_second, g_bias, g_mix, g_query, g_key, g_value, g_mlp, gw_q, gw_k, gw_v, gw_o, gw_e, gw_r, output,
):
    rows = ds.shape[1]

    @pl.when(pl.program_id(0) == 0)
    def _():
        g_first[...] = small[0:MIX, :D]
        g_second[...] = small[0:MIX, D : D + MIX]
        g_bias[...] = small[68:69, D : D + MIX]
        for i, ref in enumerate((g_mix, g_query, g_key, g_value, g_mlp)):
            ref[...] = small[68 + i : 69 + i, :D]
        gw_q[...] = sum_a[:256, :128]
        gw_k[...] = sum_a[:256, 128:]
        gw_v[:128] = sum_a[256:384, :128]
        gw_v[128:] = sum_a[256:384, 128:]
        gw_o[...] = sum_a[384:]
        gw_e[:, :256] = sum_e[:256]
        gw_e[:, 256:] = sum_e[256:]
        gw_r[...] = sum_r[...]
        output[...] = low[...]

    here = mix[...]
    lane = lax.broadcasted_iota(jnp.int32, (rows, 128), 1)
    own = lax.rem(lane, rows) == lax.broadcasted_iota(jnp.int32, (rows, 128), 0)
    stream = lax.rem(lax.div(lane, rows), STREAMS)
    left = []
    for j in range(HISTORY):
        piece = jnp.zeros((rows, 128), F32)
        for k in range(STREAMS):
            i = k * HISTORY + j
            piece = jnp.where(stream == k, here[:, i : i + 1], piece)
        high, low = halves(jnp.where(own, piece, 0.0))
        left.append(jnp.where(lane < 64, high.astype(F32), low.astype(F32)).astype(BF))
    left = jnp.concatenate(left, axis=0)
    for c in range(D // 512):
        cols = slice(c * 512, (c + 1) * 512)
        right = jnp.concatenate([ds[k, :, cols] if k < 3 else grad_low[:, cols] for k in range(STREAMS)], axis=0)
        product = nn(left, jnp.concatenate([right, right], axis=0))
        grad_hist[0 : HISTORY - 1, :, cols] = product[:256].astype(BF).reshape(HISTORY - 1, rows, 512)
        grad_hist[HISTORY - 1, :, cols] = (product[256:] + extra[:, cols]).astype(BF)


def last(ds, grad_low, extra, mix, small, sum_a, sum_e, sum_r, output):
    rows = 16

    def whole(*shape):
        return pl.BlockSpec(shape, lambda i: (0,) * len(shape))

    shapes = [(MIX, D), (MIX, MIX), (1, MIX)] + [(1, D)] * 5
    shapes += [(256, 128)] * 3 + [(128, 256), (256, 512), (512, 256)]
    return pl.pallas_call(
        last_kernel,
        grid=(ROWS // rows,),
        in_specs=[
            pl.BlockSpec((3, rows, D), lambda i: (0, i, 0)),
            pl.BlockSpec((rows, D), lambda i: (i, 0)),
            pl.BlockSpec((rows, D), lambda i: (i, 0)),
            pl.BlockSpec((rows, MIX), lambda i: (i, 0)),
            whole(SMALL_ROWS, SMALL_COLS),
            whole(512, 256),
            whole(512, 256),
            whole(512, 256),
            whole(ROWS, D),
        ],
        out_specs=[pl.BlockSpec((HISTORY, rows, D), lambda i: (0, i, 0))] + [whole(*x) for x in shapes] + [whole(ROWS, D)],
        out_shape=[jax.ShapeDtypeStruct((HISTORY, ROWS, D), BF)]
        + [jax.ShapeDtypeStruct(x, F32) for x in shapes]
        + [jax.ShapeDtypeStruct((ROWS, D), BF)],
        compiler_params=pltpu.CompilerParams(vmem_limit_bytes=61 * MIB),
        name="last",
    )(ds, grad_low, extra, mix, small, sum_a, sum_e, sum_r, output)


def on_device(
    history, cotangent, lengths, mix_gain, mix_first, mix_second, mix_bias,
    gain_query, gain_key, gain_value, gain_mlp, w_query, w_key, w_value, w_output, w_expand, w_reduce,
):
    gains = (gain_query, gain_key, gain_value)
    heads, rows, w_all, wo_all, we_two, cot_all, n, inv, resid, mix, pre = qkv(
        history, cotangent, mix_gain, mix_first, mix_second, mix_bias, gains, w_query, w_key, w_value, w_output, w_expand
    )
    heads = heads.reshape(3, 2048, HEAD_DIM)
    ctx_rows, middle, reduced, keep_mlp, g_gain_mlp, grad_middle, grad_low = mlp(
        heads, lengths, wo_all, resid, gain_mlp, cotangent, cot_all, w_expand, we_two, w_reduce
    )
    output, grads, sum_e, keep_o, sib_o = back(heads, lengths, grad_low, wo_all, ctx_rows, reduced, middle, keep_mlp)
    ds, mixed, newest, sums, sum_r, keep_q, sib_q = streams_back(
        grads, rows, w_all, keep_mlp, history, grad_middle, n, inv, gains
    )
    extra, sum_a, small = finish(
        history, mixed, newest, sums, pre, mix_gain, mix_first, mix_second, g_gain_mlp, keep_q, sib_q, keep_o, sib_o
    )
    outs = last(ds, grad_low, extra, mix, small, sum_a, sum_e, sum_r, output)
    grad_history, g_first, g_second, g_bias, g_mix, g_query, g_key, g_value, g_mlp = outs[:9]
    return (
        outs[15], grad_history, g_mix[0], g_first.T, g_second, g_bias[0], g_query[0], g_key[0], g_value[0], g_mlp[0],
        *outs[9:15],
    )


def solution(mesh):
    rows, cols, both = P("tensor", None), P(None, "tensor"), ("dp", "tensor")
    return jax.shard_map(
        on_device,
        mesh=mesh,
        in_specs=(P(None, both, None), P(both, None)) + (P(),) * 9 + (cols, cols, cols, rows, cols, rows),
        out_specs=(P(both, None), P(None, both, None)) + (P(),) * 8
        + (P("dp", "tensor"),) * 3 + (P("tensor", "dp"), P("dp", "tensor"), P("tensor", "dp")),
        check_vma=False,
    )
```
